32 devices in a mesh: groups: 2 (over y), inst: 4 (over z), tp: 4 (over x, core).
Axes of the slice: x: 2, y: 2, z: 4, core: 2. Of those that a mesh axis runs over, the one named last changes fastest.
Arguments:
- queries: bfloat16 [32, 128, 8192], P(('groups', 'inst'), None, 'tp'), parts along dimension 0, may hold values from -16 to 16
- kv_new: bfloat16 [32, 8, 128, 256], P(('groups', 'inst'), None, 'tp'), parts along dimension 0, may hold values from -16 to 16
- prompt_spans: int32 [8], P('groups'), parts along dimension 0, may hold values from 1 to 8, 16 in all
- prompt_tail: int32 [8], P('groups'), parts along dimension 0, may hold values from 1 to 128
- span_plan: int32 [32], P('groups'), parts along dimension 0, may hold values from 0 to 15, each once
- decode_owner: int32 [8], P('groups'), parts along dimension 0, may hold values from 0 to 3, as said below
Outputs:
- attended: bfloat16 [32, 128, 8192], P(('groups', 'inst'), None, 'tp'), parts along dimension 0
- owner_cache: bfloat16 [64, 8, 128, 256], P(('groups', 'inst'), None, 'tp'), parts along dimension 0
The draws below stay inside these ranges and needn't reach their ends.
There are 2 independent parts, one for each index of `groups`. The reference program is written for one: setup_inputs(seed, part) draws one part's arguments, and reference() takes and returns one part's arrays. A program takes and returns all parts, laid end to end along the dimension named above; each array names one. Nothing has to cross between parts.
Inputs may be any that keep to these rules, and one draw needn't show every extreme that they name: `prompt_spans`: they sum to 16. `decode_owner`: distinct instances.
All inputs are finite; a program needn't handle non-finite values.
Results may differ from the reference program's by a relative error of at most 0.0036.
Values may be sent and summed in bfloat16 or wider, within the bound.
No kernel may reach another device: no remote copies, remote signals or barrier semaphores. Data moves between devices by JAX's collectives and lax.ppermute only.
A program may use at most 64 MiB of HBM per device.

```python
import math
import jax
import jax.numpy as jnp
import numpy as np
from jax import lax

HEADS = 64
KVH = 8
HD = 128
SPAN = 128
NP = 4
NCH = 16
MAXCH = 8
N_INST = 4


def draw_queries(key, part):
    key = jax.random.fold_in(key, 11)
    first_key = jax.random.fold_in(key, 0)
    noise_part = jax.random.normal(first_key, (NCH, SPAN, HEADS, HD), jnp.float32)
    noise_part = jnp.clip(noise_part, -16.0, 16.0)
    return noise_part.reshape(NCH, SPAN, HEADS * HD).astype(jnp.bfloat16)


def draw_kv_new(key, part):
    key = jax.random.fold_in(key, 12)
    key_noise = jax.random.normal(jax.random.fold_in(key, 1), (NCH, KVH, SPAN, HD), jnp.float32)
    value_noise = jax.random.normal(jax.random.fold_in(key, 2), (NCH, KVH, SPAN, HD), jnp.float32)
    joined = jnp.concatenate([key_noise, value_noise], axis=-1)
    return jnp.clip(joined, -16.0, 16.0).astype(jnp.bfloat16)


def draw_decode_owner(key, part):
    key = jax.random.fold_in(key, 13)
    first_key, second_key = jax.random.split(key)
    middle = jax.random.permutation(first_key, jnp.arange(1, N_INST - 1, dtype=jnp.int32))
    chosen = jnp.concatenate([jnp.array([0, N_INST - 1], dtype=jnp.int32), middle[:NP - 2]])
    return jax.random.permutation(second_key, chosen).astype(jnp.int32)


def touch_ends(values, own_key, low, largest):
    place = [jax.random.randint(jax.random.fold_in(own_key, axis), (), 0, length) for axis, length in enumerate(values.shape)]
    longest = values.shape.index(max(values.shape))
    neighbour = place[:longest] + [(place[longest] + 1) % values.shape[longest]] + place[longest + 1:]
    return values.at[tuple(place)].set(low).at[tuple(neighbour)].set(largest)


def split_up(amount, total, most, slope):
    portions = [(1 << 20) // math.isqrt(standing ** slope) + 1 for standing in range(2, amount + 1)]
    rest, counts = total - most - (amount - 1), [1] * (amount - 1)
    while rest > 0:
        movable = [i for i in range(amount - 1) if counts[i] < most]
        mass, remaining = sum([portions[i] for i in movable]), rest
        for i in movable:
            addition = min(most - counts[i], max(1, remaining * portions[i] // mass), rest)
            counts[i] = counts[i] + addition
            rest = rest - addition
    return np.array([most] + counts)


def uneven_parts(rng, number_of, total, most, slope):
    if number_of == 2:
        one = jax.random.randint(rng, (), max(1, total - most), min(most, total - 1) + 1)
        return jnp.stack([one, total - one])
    sizes = jnp.asarray(split_up(number_of, total, most, slope), jnp.int32)
    pairs = (number_of - 1) // 2
    source_of, taker = sizes[1:1 + 2 * pairs:2], sizes[2:2 + 2 * pairs:2]
    margin = jnp.minimum(source_of - 1, most - taker)
    moved = jax.random.randint(jax.random.fold_in(rng, 1), (pairs,), 0, 1 << 20) % (margin + 1)
    sizes = sizes.at[1:1 + 2 * pairs:2].set(source_of - moved).at[2:2 + 2 * pairs:2].set(taker + moved)
    return sizes[jax.random.permutation(jax.random.fold_in(rng, 2), number_of)]


def setup_inputs(seed: int = 0, part: int = 0) -> dict:
    key_of = jax.random.split(jax.random.key(seed), 7)
    part_splits = jax.random.split(jax.random.fold_in(key_of[6], part), 7)
    queries = draw_queries(jax.random.fold_in(jax.random.fold_in(key_of[6], part), 71), part)
    kv_new = draw_kv_new(jax.random.fold_in(jax.random.fold_in(key_of[6], part), 71), part)
    prompt_spans = uneven_parts(part_splits[2], NP, NCH, MAXCH, 2).astype(jnp.int32)
    prompt_tail = touch_ends(jax.random.randint(part_splits[3], (NP,), 1, SPAN + 1), jax.random.fold_in(part_splits[3], 1), 1, SPAN).astype(jnp.int32)
    span_plan = jax.random.permutation(part_splits[4], NCH).astype(jnp.int32)
    decode_owner = draw_decode_owner(jax.random.fold_in(jax.random.fold_in(key_of[6], part), 71), part)
    return {"queries": queries, "kv_new": kv_new, "prompt_spans": prompt_spans, "prompt_tail": prompt_tail, "span_plan": span_plan, "decode_owner": decode_owner}


def span_meta(prompt_spans, prompt_tail, span_plan, span_total, span_len):
    span_ids = jnp.arange(span_total, dtype=jnp.int32)
    prompt_ends = jnp.cumsum(prompt_spans).astype(jnp.int32)
    prompt_count = prompt_spans.shape[0]
    prompt_of = lax.optimization_barrier(jnp.sum((span_ids[:, None] >= prompt_ends[None, :]).astype(jnp.int32), axis=1)).astype(jnp.int32)
    belongs = prompt_of[:, None] == jnp.arange(prompt_count, dtype=jnp.int32)[None, :]
    prompt_first = (prompt_ends - prompt_spans).astype(jnp.int32)
    index_of = (span_ids - lax.optimization_barrier(jnp.sum(jnp.where(belongs, prompt_first[None, :], 0), axis=1))).astype(jnp.int32)
    lengths = ((prompt_spans - 1) * span_len + prompt_tail).astype(jnp.int32)
    length_of = lax.optimization_barrier(jnp.sum(jnp.where(belongs, lengths[None, :], 0), axis=1)).astype(jnp.int32)
    plan_hits = span_plan[:, None] == span_ids[None, :]

    def lookup(values):
        return lax.optimization_barrier(jnp.sum(jnp.where(plan_hits, values[None, :], 0), axis=1)).astype(jnp.int32)
    return (lookup(prompt_of), lookup(index_of), lookup(length_of))

def reference(queries, kv_new, prompt_spans, prompt_tail, span_plan, decode_owner):
    slot_prompt, slot_index, slot_length = span_meta(prompt_spans, prompt_tail, span_plan, NCH, SPAN)
    offsets = jnp.arange(SPAN, dtype=jnp.int32)
    positions = (slot_index[:, None] * SPAN + offsets[None, :]).astype(jnp.int32)
    live_rows = positions < slot_length[:, None]
    prompts = jnp.broadcast_to(slot_prompt[:, None], (NCH, SPAN))
    key_rows = jnp.transpose(kv_new[:, :, :, :HD].astype(jnp.float32), (1, 0, 2, 3)).reshape(KVH, NCH * SPAN, HD)
    value_rows = jnp.transpose(kv_new[:, :, :, HD:].astype(jnp.float32), (1, 0, 2, 3)).reshape(KVH, NCH * SPAN, HD)
    flat_pos = positions.reshape(-1)
    flat_prompt = prompts.reshape(-1)
    flat_live = live_rows.reshape(-1)
    score_scale = 1.0 / math.sqrt(HD)
    group_size = HEADS // KVH

    def one_span(entries):
        query_block, query_pos, query_prompt, query_live = entries
        query_rows = query_block.astype(jnp.float32).reshape(SPAN, KVH, group_size, HD)
        scores = jnp.einsum('ckgd,knd->ckgn', query_rows, key_rows) * score_scale
        allowed = (query_prompt[:, None] == flat_prompt[None, :]) & (flat_pos[None, :] <= query_pos[:, None])
        allowed = allowed & flat_live[None, :] & query_live[:, None]
        allowed = allowed[:, None, None, :]
        masked = jnp.where(allowed, scores, -1e+30)
        row_peak = lax.optimization_barrier(jnp.max(masked, axis=-1, keepdims=True))
        weights = jnp.where(allowed, jnp.exp(masked - row_peak), 0.0)
        totals = lax.optimization_barrier(jnp.sum(weights, axis=-1))
        rounded = lax.optimization_barrier(weights.astype(jnp.bfloat16)).astype(jnp.float32)
        mixture = jnp.einsum('ckgn,knd->ckgd', rounded, value_rows)
        divisor = jnp.where(query_live[:, None, None], totals, 1.0)
        result = jnp.where(query_live[:, None, None, None], mixture / divisor[..., None], 0.0)
        return result.reshape(SPAN, HEADS * HD).astype(jnp.bfloat16)
    attended = lax.map(one_span, (queries, positions, prompts, live_rows))
    owner_hits = slot_prompt[:, None] == jnp.arange(NP, dtype=jnp.int32)[None, :]
    owners = lax.optimization_barrier(jnp.sum(jnp.where(owner_hits, decode_owner[None, :], 0), axis=1)).astype(jnp.int32)
    destination = (owners * MAXCH + slot_index).astype(jnp.int32)
    owner_cache = jnp.zeros((N_INST * MAXCH, KVH, SPAN, 2 * HD), jnp.bfloat16).at[destination].set(kv_new)
    return (attended, owner_cache)
```

```python
import functools
import math

import jax
import jax.numpy as jnp
from jax import lax
from jax.experimental import pallas as pl
from jax.experimental.pallas import tpu as pltpu
from jax.sharding import PartitionSpec as P

HEADS = 64
KVH = 8
LOG2E = 1.4426950408889634


def read_plan(spans_ref, plan_ref, place_ref, slot):
    span = plan_ref[slot]
    prompt = jnp.int32(0)
    first = jnp.int32(0)
    end = jnp.int32(0)
    for p in range(spans_ref.shape[0]):
        end = end + spans_ref[p]
        later = span >= end
        prompt = jnp.where(later, p + 1, prompt)
        first = jnp.where(later, end, first)
    return prompt, first, span


def attend_kernel(
    spans_ref, tail_ref, plan_ref, owner_ref, inst_ref,
    q_ref, kv_ref, pages_ref, out_ref, cache_ref,
    place_ref, acc_ref, max_ref, zero_ref, sems,
    *, kv_local, per_head, head_dim, span_len, slot_count, span_total, longest,
):
    step = pl.program_id(0)
    inst = inst_ref[0]
    prompt_count = spans_ref.shape[0]
    scale = LOG2E / math.sqrt(head_dim)

    def cache_copies(act):
        mine = jnp.int32(0)
        first = jnp.int32(0)
        count = jnp.int32(0)
        start = jnp.int32(0)
        for p in range(prompt_count):
            hit = owner_ref[p] == inst
            first = jnp.where(hit, start, first)
            count = jnp.where(hit, spans_ref[p], count)
            start = start + spans_ref[p]

        def row(r, unused):
            @pl.when(r < count)
            def _():
                page = place_ref[jnp.minimum(first + r, span_total - 1)]
                act(pltpu.make_async_copy(pages_ref.at[page], cache_ref.at[r], sems.at[r]))

            @pl.when(r >= count)
            def _():
                act(pltpu.make_async_copy(zero_ref, cache_ref.at[r], sems.at[r]))

            return unused

        lax.fori_loop(0, longest, row, 0)

    @pl.when(step == 0)
    def _():
        def put(g, unused):
            place_ref[plan_ref[g]] = g
            return unused

        lax.fori_loop(0, span_total, put, 0)
        zero_ref[...] = jnp.zeros_like(zero_ref)
        cache_copies(lambda copy: copy.start())

    prompt, first, span = read_plan(spans_ref, plan_ref, place_ref, inst * slot_count + step)
    index = span - first
    length = jnp.int32(0)
    for p in range(prompt_count):
        length = jnp.where(
            prompt == p, (spans_ref[p] - 1) * span_len + tail_ref[p], length
        )
    live_rows = length - index * span_len
    ones = jnp.ones((span_len, head_dim), jnp.bfloat16)
    row_ids = lax.broadcasted_iota(jnp.int32, (span_len, span_len), 0)
    col_ids = lax.broadcasted_iota(jnp.int32, (span_len, span_len), 1)
    causal = row_ids >= col_ids
    live = row_ids[:, :head_dim] < live_rows

    def load(pages, g):
        blocks = [kv_ref[page, g] for page in pages]
        keys = [b[:, :head_dim] for b in blocks]
        values = [jnp.concatenate([b[:, head_dim:], ones], axis=1) for b in blocks]
        if len(pages) == 1:
            return keys[0], values[0]
        return jnp.concatenate(keys, axis=0), jnp.concatenate(values, axis=0)

    def scores_of(g, h, keys):
        head = g * per_head + h
        q = q_ref[0, :, head * head_dim:(head + 1) * head_dim]
        return lax.dot_general(
            q, keys, (((1,), (1,)), ((), ())), preferred_element_type=jnp.float32
        ) * scale

    def begin(pages):
        for g in range(kv_local):
            keys, values = load(pages, g)
            for h in range(per_head):
                head = g * per_head + h
                s = scores_of(g, h, keys)
                tail = jnp.where(causal, s[:, -span_len:], -1e30)
                s = tail if len(pages) == 1 else jnp.concatenate([s[:, :span_len], tail], axis=1)
                top = jnp.max(s, axis=1, keepdims=True)
                w = jnp.exp2(s - top).astype(jnp.bfloat16)
                acc_ref[head] = jnp.dot(w, values, preferred_element_type=jnp.float32)
                max_ref[head] = jnp.broadcast_to(top, (span_len, head_dim))

    def more(pages):
        for g in range(kv_local):
            keys, values = load(pages, g)
            for h in range(per_head):
                head = g * per_head + h
                s = scores_of(g, h, keys)
                old = max_ref[head]
                top = jnp.maximum(old, jnp.max(s, axis=1, keepdims=True))
                rescale = jnp.exp2(old - top)
                wide = jnp.concatenate([top] * len(pages), axis=1)
                w = jnp.exp2(s - wide).astype(jnp.bfloat16)
                acc_ref[head] = acc_ref[head] * jnp.concatenate(
                    [rescale, rescale], axis=1
                ) + jnp.dot(w, values, preferred_element_type=jnp.float32)
                max_ref[head] = top

    own = inst * slot_count + step
    odd = lax.rem(index, 2)

    @pl.when(odd == 0)
    def _():
        begin([own])

    @pl.when(odd == 1)
    def _():
        begin([place_ref[first], own])

    def pair(j, unused):
        at = first + odd + 2 * j
        more([place_ref[at], place_ref[at + 1]])
        return unused

    lax.fori_loop(0, index // 2, pair, 0)

    for head in range(kv_local * per_head):
        total = acc_ref[head]
        mixed = total[:, :head_dim] / total[:, head_dim:]
        out_ref[0, :, head * head_dim:(head + 1) * head_dim] = jnp.where(
            live, mixed, 0.0
        ).astype(jnp.bfloat16)

    @pl.when(step == slot_count - 1)
    def _():
        cache_copies(lambda copy: copy.wait())


def body(queries, kv_new, prompt_spans, prompt_tail, span_plan, decode_owner):
    tp_size = lax.axis_size("tp")
    inst_size = lax.axis_size("inst")
    inst_index = lax.axis_index("inst")
    slot_count, span_len, row_width = queries.shape
    kv_heads, slice_len, width = kv_new.shape[1:]
    head_dim = width // 2
    local_heads = row_width // head_dim
    kv_local = max(1, kv_heads // tp_size)
    per_head = local_heads // kv_local
    span_total = slot_count * inst_size
    longest = span_total // 2
    pages = lax.all_gather(kv_new, "inst", axis=0, tiled=True)
    if tp_size > kv_heads:
        sent = jnp.repeat(pages, tp_size // kv_heads, axis=1)
    else:
        sent = pages
    own_heads = lax.all_to_all(sent, "tp", split_axis=1, concat_axis=2, tiled=True)
    kernel = functools.partial(
        attend_kernel,
        kv_local=kv_local,
        per_head=per_head,
        head_dim=head_dim,
        span_len=span_len,
        slot_count=slot_count,
        span_total=span_total,
        longest=longest,
    )
    work = slot_count * span_total // 4 * local_heads * span_len * span_len
    attended, owner_cache = pl.pallas_call(
        kernel,
        grid_spec=pltpu.PrefetchScalarGridSpec(
            num_scalar_prefetch=5,
            grid=(slot_count,),
            in_specs=[
                pl.BlockSpec((1, span_len, row_width), lambda i, *_: (i, 0, 0)),
                pl.BlockSpec(own_heads.shape, lambda i, *_: (0, 0, 0, 0)),
                pl.BlockSpec(memory_space=pl.ANY),
            ],
            out_specs=[
                pl.BlockSpec((1, span_len, row_width), lambda i, *_: (i, 0, 0)),
                pl.BlockSpec(memory_space=pl.ANY),
            ],
            scratch_shapes=[
                pltpu.SMEM((span_total,), jnp.int32),
                pltpu.VMEM((local_heads, span_len, 2 * head_dim), jnp.float32),
                pltpu.VMEM((local_heads, span_len, head_dim), jnp.float32),
                pltpu.VMEM((kv_heads, slice_len, width), jnp.bfloat16),
                pltpu.SemaphoreType.DMA((longest,)),
            ],
        ),
        out_shape=[
            jax.ShapeDtypeStruct(queries.shape, jnp.bfloat16),
            jax.ShapeDtypeStruct((longest, kv_heads, slice_len, width), jnp.bfloat16),
        ],
        cost_estimate=pl.CostEstimate(
            flops=4 * work * head_dim, bytes_accessed=8 << 20, transcendentals=work
        ),
        compiler_params=pltpu.CompilerParams(vmem_limit_bytes=48 << 20),
    )(
        prompt_spans, prompt_tail, span_plan, decode_owner,
        jnp.reshape(inst_index.astype(jnp.int32), (1,)),
        queries, own_heads, pages,
    )
    return (attended, owner_cache)


def solution(mesh):
    placed = (
        P(("groups", "inst"), None, "tp"),
        P(("groups", "inst"), None, "tp", None),
        P("groups"),
        P("groups"),
        P("groups"),
        P("groups"),
    )
    return jax.shard_map(
        body,
        mesh=mesh,
        in_specs=placed,
        out_specs=(P(("groups", "inst"), None, "tp"), P(("groups", "inst"), None, "tp", None)),
        check_vma=False,
    )
```

```python
import functools
import math

import jax
import jax.numpy as jnp
from jax import lax
from jax.experimental import pallas as pl
from jax.experimental.pallas import tpu as pltpu
from jax.sharding import PartitionSpec as P

HEADS = 64
KVH = 8
LOG2E = 1.4426950408889634


def source_of(unit, inst, inst_size):
    if unit == 0:
        return inst
    step, late = unit_steps(inst_size)[unit - 1]
    if not late:
        return jnp.where(inst <= inst_size - 1 - step, inst + step, inst - step)
    far = inst_size - step
    middle = (inst >= step) & (inst <= inst_size - 1 - step)
    return jnp.where(middle, inst - step, jnp.where(inst <= step - 1, inst + far, inst - far))


def unit_steps(inst_size):
    near = [(s, False) for s in range(1, inst_size // 2 + 1)]
    late = [(s, True) for s in range((inst_size - 1) // 2, 0, -1)]
    return near + late


def attend_kernel(
    spans_ref, tail_ref, plan_ref, owner_ref, where_ref, *refs,
    inst_size, tp_size, kv_local, per_head, head_dim, span_len, slot_count, longest,
):
    q_ref = refs[0]
    unit_refs = refs[1:1 + inst_size]
    part_refs = refs[1 + inst_size:1 + inst_size + inst_size * (tp_size - 1)]
    (out_ref, cache_ref, place_ref, kv_ref, s_ref, p_ref, acc_ref, max_ref, zero_ref,
     page_sems, part_sems) = refs[1 + inst_size + inst_size * (tp_size - 1):]
    step = pl.program_id(0)
    inst = where_ref[0]
    tp = where_ref[1]
    prompt_count = spans_ref.shape[0]
    span_total = slot_count * inst_size
    slice_len = span_len // tp_size
    rows = per_head * span_len
    scale = LOG2E / math.sqrt(head_dim)
    sources = [source_of(u, inst, inst_size) for u in range(inst_size)]
    first_head = tp * (kv_local * per_head) // (HEADS // KVH)

    def part_copies(act):
        for u in range(inst_size):
            slots = pl.ds(sources[u] * slot_count, slot_count)
            for j in range(tp_size):
                if j == 0:
                    src = unit_refs[u].at[:, pl.ds(first_head, kv_local)]
                else:
                    src = part_refs[u * (tp_size - 1) + j - 1]
                at = pl.multiple_of((tp ^ j) * slice_len, slice_len)
                act(pltpu.make_async_copy(
                    src, kv_ref.at[slots, :, pl.ds(at, slice_len)], part_sems.at[u, j]
                ))

    def cache_copies(act):
        first = jnp.int32(0)
        count = jnp.int32(0)
        start = jnp.int32(0)
        for p in range(prompt_count):
            hit = owner_ref[p] == inst
            first = jnp.where(hit, start, first)
            count = jnp.where(hit, spans_ref[p], count)
            start = start + spans_ref[p]

        def row(r, unused):
            page = place_ref[jnp.minimum(first + r, span_total - 1)]
            source = page // slot_count
            slot = page - source * slot_count
            for u in range(inst_size):
                @pl.when((r < count) & (source == sources[u]))
                def _():
                    act(pltpu.make_async_copy(
                        unit_refs[u].at[slot], cache_ref.at[r], page_sems.at[r]
                    ))

            @pl.when(r >= count)
            def _():
                act(pltpu.make_async_copy(zero_ref, cache_ref.at[r], page_sems.at[r]))

            return unused

        lax.fori_loop(0, longest, row, 0)

    @pl.when(step == 0)
    def _():
        part_copies(lambda copy: copy.start())

        def put(g, unused):
            place_ref[plan_ref[g]] = g
            return unused

        lax.fori_loop(0, span_total, put, 0)
        zero_ref[...] = jnp.zeros_like(zero_ref)
        cache_copies(lambda copy: copy.start())
        part_copies(lambda copy: copy.wait())

    own = inst * slot_count + step
    span = plan_ref[own]
    first = jnp.int32(0)
    end = jnp.int32(0)
    length = jnp.int32(0)
    for p in range(prompt_count):
        start = end
        end = end + spans_ref[p]
        inside = (span >= start) & (span < end)
        first = jnp.where(inside, start, first)
        length = jnp.where(inside, (spans_ref[p] - 1) * span_len + tail_ref[p], length)
    index = span - first
    live_rows = length - index * span_len
    ones = jnp.ones((span_len, head_dim), jnp.bfloat16)
    row_ids = lax.broadcasted_iota(jnp.int32, (span_len, span_len), 0)
    col_ids = lax.broadcasted_iota(jnp.int32, (span_len, span_len), 1)
    causal = row_ids >= col_ids

    def key_block(pages, g):
        return jnp.concatenate([kv_ref[page, g, :, :head_dim] for page in pages], axis=0)

    def value_block(pages, g):
        return jnp.concatenate(
            [
                jnp.concatenate([kv_ref[page, g, :, head_dim:], ones], axis=1)
                for page in pages
            ],
            axis=0,
        )

    def attend(pages, begin):
        wide = len(pages) * span_len
        for g in range(kv_local):
            q = jnp.concatenate(
                [
                    q_ref[0, :, (g * per_head + h) * head_dim:(g * per_head + h + 1) * head_dim]
                    for h in range(per_head)
                ],
                axis=0,
            )
            s_ref[g, :, :wide] = lax.dot_general(
                q, key_block(pages, g), (((1,), (1,)), ((), ())),
                preferred_element_type=jnp.float32,
            )
        for g in range(kv_local):
            rescales = []
            for h in range(per_head):
                at = slice(h * span_len, (h + 1) * span_len)
                s = s_ref[g, at, :wide] * scale
                if begin:
                    own_part = jnp.where(causal, s[:, wide - span_len:], -1e30)
                    if len(pages) > 1:
                        s = jnp.concatenate([s[:, :wide - span_len], own_part], axis=1)
                    else:
                        s = own_part
                top = jnp.max(s, axis=1, keepdims=True)
                if begin:
                    top = jnp.broadcast_to(top, (span_len, head_dim))
                else:
                    old = max_ref[g, at]
                    top = jnp.maximum(old, top)
                    rescales.append(jnp.exp2(old - top))
                max_ref[g, at] = top
                p_ref[g, at, :wide] = jnp.exp2(
                    s - jnp.concatenate([top] * len(pages), axis=1)
                ).astype(jnp.bfloat16)
            mixed = jnp.dot(
                p_ref[g, :, :wide], value_block(pages, g), preferred_element_type=jnp.float32
            )
            if begin:
                acc_ref[g] = mixed
            else:
                for h in range(per_head):
                    at = slice(h * span_len, (h + 1) * span_len)
                    acc_ref[g, at] = acc_ref[g, at] * jnp.concatenate(
                        [rescales[h], rescales[h]], axis=1
                    ) + mixed[at]

    odd = lax.rem(index, 2)

    @pl.when(odd == 0)
    def _():
        attend([own], True)

    @pl.when(odd == 1)
    def _():
        attend([place_ref[first], own], True)

    def pair(j, unused):
        at = first + odd + 2 * j
        attend([place_ref[at], place_ref[at + 1]], False)
        return unused

    lax.fori_loop(0, index // 2, pair, 0)

    live = lax.broadcasted_iota(jnp.int32, (span_len, head_dim), 0) < live_rows
    for g in range(kv_local):
        for h in range(per_head):
            head = g * per_head + h
            total = acc_ref[g, h * span_len:(h + 1) * span_len]
            out_ref[0, :, head * head_dim:(head + 1) * head_dim] = jnp.where(
                live, total[:, :head_dim] / total[:, head_dim:], 0.0
            ).astype(jnp.bfloat16)

    @pl.when(step == slot_count - 1)
    def _():
        cache_copies(lambda copy: copy.wait())


def gather_units(kv_new, inst_index, inst_size):
    up, down = [kv_new], [kv_new]
    for s in range(1, inst_size):
        up.append(lax.ppermute(up[-1], "inst", [(i, i + 1) for i in range(s - 1, inst_size - 1)]))
        down.append(lax.ppermute(down[-1], "inst", [(i + 1, i) for i in range(inst_size - s)]))
    units = [kv_new]
    for step, late in unit_steps(inst_size):
        far = inst_size - step
        if not late:
            unit = jnp.where(inst_index <= inst_size - 1 - step, down[step], up[step])
        else:
            middle = (inst_index >= step) & (inst_index <= inst_size - 1 - step)
            unit = jnp.where(
                middle, up[step], jnp.where(inst_index <= step - 1, down[far], up[far])
            )
        units.append(unit)
    return units


def body(queries, kv_new, prompt_spans, prompt_tail, span_plan, decode_owner):
    tp_size = lax.axis_size("tp")
    inst_size = lax.axis_size("inst")
    tp_index = lax.axis_index("tp")
    inst_index = lax.axis_index("inst")
    slot_count, span_len, row_width = queries.shape
    kv_heads, slice_len, width = kv_new.shape[1:]
    head_dim = width // 2
    local_heads = row_width // head_dim
    kv_local = max(1, kv_heads // tp_size)
    per_head = local_heads // kv_local
    span_total = slot_count * inst_size
    longest = span_total // 2
    units = gather_units(kv_new, inst_index, inst_size)
    parts = []
    for unit in units:
        for j in range(1, tp_size):
            head = (tp_index ^ j) * local_heads // (HEADS // KVH)
            sent = lax.dynamic_slice_in_dim(unit, head, kv_local, 1)
            parts.append(lax.ppermute(sent, "tp", [(t, t ^ j) for t in range(tp_size)]))
    kernel = functools.partial(
        attend_kernel,
        inst_size=inst_size,
        tp_size=tp_size,
        kv_local=kv_local,
        per_head=per_head,
        head_dim=head_dim,
        span_len=span_len,
        slot_count=slot_count,
        longest=longest,
    )
    work = slot_count * span_total // 4 * local_heads * span_len * span_len
    anywhere = pl.BlockSpec(memory_space=pl.ANY)
    by_slot = pl.BlockSpec((1, span_len, row_width), lambda i, *_: (i, 0, 0))
    rows = per_head * span_len
    return pl.pallas_call(
        kernel,
        grid_spec=pltpu.PrefetchScalarGridSpec(
            num_scalar_prefetch=5,
            grid=(slot_count,),
            in_specs=[by_slot] + [anywhere] * (len(units) + len(parts)),
            out_specs=[by_slot, anywhere],
            scratch_shapes=[
                pltpu.SMEM((span_total,), jnp.int32),
                pltpu.VMEM((span_total, kv_local, span_len, width), jnp.bfloat16),
                pltpu.VMEM((kv_local, rows, 2 * span_len), jnp.float32),
                pltpu.VMEM((kv_local, rows, 2 * span_len), jnp.bfloat16),
                pltpu.VMEM((kv_local, rows, 2 * head_dim), jnp.float32),
                pltpu.VMEM((kv_local, rows, head_dim), jnp.float32),
                pltpu.VMEM((kv_heads, slice_len, width), jnp.bfloat16),
                pltpu.SemaphoreType.DMA((longest,)),
                pltpu.SemaphoreType.DMA((inst_size, tp_size)),
            ],
        ),
        out_shape=[
            jax.ShapeDtypeStruct(queries.shape, jnp.bfloat16),
            jax.ShapeDtypeStruct((longest, kv_heads, slice_len, width), jnp.bfloat16),
        ],
        cost_estimate=pl.CostEstimate(
            flops=4 * work * head_dim, bytes_accessed=8 << 20, transcendentals=work
        ),
        compiler_params=pltpu.CompilerParams(vmem_limit_bytes=40 << 20),
    )(
        prompt_spans, prompt_tail, span_plan, decode_owner,
        jnp.stack([inst_index, tp_index]).astype(jnp.int32),
        queries, *units, *parts,
    )


def solution(mesh):
    placed = (
        P(("groups", "inst"), None, "tp"),
        P(("groups", "inst"), None, "tp", None),
        P("groups"),
        P("groups"),
        P("groups"),
        P("groups"),
    )
    return jax.shard_map(
        body,
        mesh=mesh,
        in_specs=placed,
        out_specs=(P(("groups", "inst"), None, "tp"), P(("groups", "inst"), None, "tp", None)),
        check_vma=False,
    )
```

```python
import functools
import math

import jax
import jax.numpy as jnp
from jax import lax
from jax.experimental import pallas as pl
from jax.experimental.pallas import tpu as pltpu
from jax.sharding import PartitionSpec as P

HEADS = 64
KVH = 8
LOG2E = 1.4426950408889634


def attend_kernel(
    spans_ref, tail_ref, plan_ref, owner_ref, place_at_ref, *refs,
    hops, parts, inst_size, tp_size, kv_local, per_head, head_dim, span_len, slot_count, longest,
):
    q_ref = refs[0]
    hop_refs = refs[1:1 + len(hops)]
    part_refs = refs[1 + len(hops):1 + len(hops) + len(parts)]
    (out_ref, cache_ref, place_ref, kv_ref, s_ref, p_ref, acc_ref, max_ref, zero_ref,
     page_sems, part_sems) = refs[1 + len(hops) + len(parts):]
    step = pl.program_id(0)
    inst = place_at_ref[0]
    tp = place_at_ref[1]
    prompt_count = spans_ref.shape[0]
    span_total = slot_count * inst_size
    slice_len = span_len // tp_size
    rows = per_head * span_len
    scale = LOG2E / math.sqrt(head_dim)

    def part_copies(act):
        for n, (pieces, j) in enumerate(parts):
            at = pl.ds(pl.multiple_of((tp ^ j) * slice_len, slice_len), slice_len)
            begin = 0
            for m, (hop, first_slot, size) in enumerate(pieces):
                slots = pl.ds(place_at_ref[2 + hop] * slot_count + first_slot, size)
                act(pltpu.make_async_copy(
                    part_refs[n].at[begin:begin + size], kv_ref.at[slots, :, at],
                    part_sems.at[n, m],
                ))
                begin += size

    def cache_copies(act):
        first = jnp.int32(0)
        count = jnp.int32(0)
        start = jnp.int32(0)
        for p in range(prompt_count):
            hit = owner_ref[p] == inst
            first = jnp.where(hit, start, first)
            count = jnp.where(hit, spans_ref[p], count)
            start = start + spans_ref[p]

        def row(r, unused):
            page = place_ref[jnp.minimum(first + r, span_total - 1)]
            for n, (hop, first_slot, size) in enumerate(hops):
                source = place_at_ref[2 + hop]
                slot = page - source * slot_count - first_slot
                here = (source >= 0) & (slot >= 0) & (slot < size)

                @pl.when((r < count) & here)
                def _():
                    act(pltpu.make_async_copy(
                        hop_refs[n].at[slot], cache_ref.at[r], page_sems.at[r]
                    ))

            @pl.when(r >= count)
            def _():
                act(pltpu.make_async_copy(zero_ref, cache_ref.at[r], page_sems.at[r]))

            return unused

        lax.fori_loop(0, longest, row, 0)

    @pl.when(step == 0)
    def _():
        part_copies(lambda copy: copy.start())

        def put(g, unused):
            place_ref[plan_ref[g]] = g
            return unused

        lax.fori_loop(0, span_total, put, 0)
        zero_ref[...] = jnp.zeros_like(zero_ref)
        cache_copies(lambda copy: copy.start())
        part_copies(lambda copy: copy.wait())

    own = inst * slot_count + step
    span = plan_ref[own]
    first = jnp.int32(0)
    end = jnp.int32(0)
    length = jnp.int32(0)
    for p in range(prompt_count):
        start = end
        end = end + spans_ref[p]
        inside = (span >= start) & (span < end)
        first = jnp.where(inside, start, first)
        length = jnp.where(inside, (spans_ref[p] - 1) * span_len + tail_ref[p], length)
    index = span - first
    live_rows = length - index * span_len
    ones = jnp.ones((span_len, head_dim), jnp.bfloat16)
    row_ids = lax.broadcasted_iota(jnp.int32, (span_len, span_len), 0)
    col_ids = lax.broadcasted_iota(jnp.int32, (span_len, span_len), 1)
    causal = row_ids >= col_ids

    def key_block(pages, g):
        return jnp.concatenate([kv_ref[page, g, :, :head_dim] for page in pages], axis=0)

    def value_block(pages, g):
        return jnp.concatenate(
            [
                jnp.concatenate([kv_ref[page, g, :, head_dim:], ones], axis=1)
                for page in pages
            ],
            axis=0,
        )

    def attend(pages, begin):
        wide = len(pages) * span_len
        for g in range(kv_local):
            q = jnp.concatenate(
                [
                    q_ref[0, :, (g * per_head + h) * head_dim:(g * per_head + h + 1) * head_dim]
                    for h in range(per_head)
                ],
                axis=0,
            )
            s_ref[g, :, :wide] = lax.dot_general(
                q, key_block(pages, g), (((1,), (1,)), ((), ())),
                preferred_element_type=jnp.float32,
            )
        for g in range(kv_local):
            rescales = []
            for h in range(per_head):
                at = slice(h * span_len, (h + 1) * span_len)
                s = s_ref[g, at, :wide] * scale
                if begin:
                    own_part = jnp.where(causal, s[:, wide - span_len:], -1e30)
                    if len(pages) > 1:
                        s = jnp.concatenate([s[:, :wide - span_len], own_part], axis=1)
                    else:
                        s = own_part
                top = jnp.max(s, axis=1, keepdims=True)
                if begin:
                    top = jnp.broadcast_to(top, (span_len, head_dim))
                else:
                    old = max_ref[g, at]
                    top = jnp.maximum(old, top)
                    rescales.append(jnp.exp2(old - top))
                max_ref[g, at] = top
                p_ref[g, at, :wide] = jnp.exp2(
                    s - jnp.concatenate([top] * len(pages), axis=1)
                ).astype(jnp.bfloat16)
            mixed = jnp.dot(
                p_ref[g, :, :wide], value_block(pages, g), preferred_element_type=jnp.float32
            )
            if begin:
                acc_ref[g] = mixed
            else:
                for h in range(per_head):
                    at = slice(h * span_len, (h + 1) * span_len)
                    acc_ref[g, at] = acc_ref[g, at] * jnp.concatenate(
                        [rescales[h], rescales[h]], axis=1
                    ) + mixed[at]

    odd = lax.rem(index, 2)

    @pl.when(odd == 0)
    def _():
        attend([own], True)

    @pl.when(odd == 1)
    def _():
        attend([place_ref[first], own], True)

    def pair(j, unused):
        at = first + odd + 2 * j
        attend([place_ref[at], place_ref[at + 1]], False)
        return unused

    lax.fori_loop(0, index // 2, pair, 0)

    live = lax.broadcasted_iota(jnp.int32, (span_len, head_dim), 0) < live_rows
    for g in range(kv_local):
        for h in range(per_head):
            head = g * per_head + h
            total = acc_ref[g, h * span_len:(h + 1) * span_len]
            out_ref[0, :, head * head_dim:(head + 1) * head_dim] = jnp.where(
                live, total[:, :head_dim] / total[:, head_dim:], 0.0
            ).astype(jnp.bfloat16)

    @pl.when(step == slot_count - 1)
    def _():
        cache_copies(lambda copy: copy.wait())


def after(values, earlier):
    return lax.optimization_barrier((list(values), list(earlier)))[0]


def move_pages(kv_new, kv_local):
    inst_size = lax.axis_size("inst")
    tp_size = lax.axis_size("tp")
    inst = lax.axis_index("inst")
    tp = lax.axis_index("tp")
    slot_count, kv_heads = kv_new.shape[:2]
    sources = [list(range(inst_size))]
    hops = [((0, 0, slot_count), kv_new)]
    parts = []

    def along(x, pairs):
        return lax.ppermute(x, "inst", pairs)

    def exchange(*pieces):
        names = [name for name, _ in pieces]
        found = []
        for j in range(tp_size):
            head = ((tp ^ j) * kv_heads) // tp_size
            sent = [lax.dynamic_slice_in_dim(x, head, kv_local, 1) for _, x in pieces]
            sent = jnp.concatenate(sent, axis=0) if len(sent) > 1 else sent[0]
            if j:
                sent = lax.ppermute(sent, "tp", [(t, t ^ j) for t in range(tp_size)])
            found.append(((names, j), sent))
        parts.extend(found)
        return [x for _, x in found]

    if inst_size != 4 or slot_count % 2:
        exchange(hops[0])
        for s in range(1, inst_size):
            sources.append([(i - s) % inst_size for i in range(inst_size)])
            pairs = [(i, (i + s) % inst_size) for i in range(inst_size)]
            hops.append(((s, 0, slot_count), along(kv_new, pairs)))
            exchange(hops[-1])
        return hops, parts, sources

    half = slot_count // 2
    sources += [[-1, 0, 1, 2], [1, 2, 3, -1], [-1, -1, 0, 1], [2, 3, -1, -1], [3, -1, -1, 0]]
    far, first, last = 6, 7, 8
    sources += [[2, 3, 0, 1], [1, 0, 3, 2], [3, 2, 1, 0]]
    mine = [kv_new[:half], kv_new[half:]]
    got = []
    for n in range(2):
        up2 = along(mine[n], [(0, 2), (1, 3)])
        down2 = along(mine[n], [(2, 0), (3, 1)])
        up1 = along(mine[n], [(0, 1), (1, 2), (2, 3)])
        down1 = along(mine[n], [(1, 0), (2, 1), (3, 2)])
        got.append((up1, down1, up2, down2))
        for hop, x in enumerate(got[-1], 1):
            hops.append(((hop, n * half, half), x))
    waiting = exchange(hops[0])
    lasts = []
    for n in range(2):
        up1, down1, up2, down2 = got[n]
        at = n * half
        two = after([jnp.where(inst < 2, down2, up2)], waiting)[0]
        handed = along(two, [(2, 3), (1, 0)])
        hops.append(((5, at, half), handed))
        one = jnp.where((inst == 0) | (inst == 2), down1, up1)
        waiting = exchange(((far, at, half), two), ((first, at, half), one))
        lasts.append((up1, down1, handed))
        if n == 0:
            before = waiting
    for n in range(2):
        up1, down1, handed = after(lasts[n], before)
        end = jnp.where(inst == 1, down1, jnp.where(inst == 2, up1, handed))
        before = exchange(((last, n * half, half), end)) + waiting
    return hops, parts, sources


def body(queries, kv_new, prompt_spans, prompt_tail, span_plan, decode_owner):
    tp_size = lax.axis_size("tp")
    inst_size = lax.axis_size("inst")
    tp_index = lax.axis_index("tp")
    inst_index = lax.axis_index("inst")
    slot_count, span_len, row_width = queries.shape
    kv_heads, slice_len, width = kv_new.shape[1:]
    head_dim = width // 2
    local_heads = row_width // head_dim
    kv_local = max(1, kv_heads // tp_size)
    per_head = local_heads // kv_local
    span_total = slot_count * inst_size
    longest = span_total // 2
    hops, parts, sources = move_pages(kv_new, kv_local)
    own_sources = lax.dynamic_index_in_dim(jnp.asarray(sources, jnp.int32), inst_index, 1, False)
    kernel = functools.partial(
        attend_kernel,
        hops=[name for name, _ in hops],
        parts=[name for name, _ in parts],
        inst_size=inst_size,
        tp_size=tp_size,
        kv_local=kv_local,
        per_head=per_head,
        head_dim=head_dim,
        span_len=span_len,
        slot_count=slot_count,
        longest=longest,
    )
    work = slot_count * span_total // 4 * local_heads * span_len * span_len
    anywhere = pl.BlockSpec(memory_space=pl.ANY)
    by_slot = pl.BlockSpec((1, span_len, row_width), lambda i, *_: (i, 0, 0))
    rows = per_head * span_len
    return pl.pallas_call(
        kernel,
        grid_spec=pltpu.PrefetchScalarGridSpec(
            num_scalar_prefetch=5,
            grid=(slot_count,),
            in_specs=[by_slot] + [anywhere] * (len(hops) + len(parts)),
            out_specs=[by_slot, anywhere],
            scratch_shapes=[
                pltpu.SMEM((span_total,), jnp.int32),
                pltpu.VMEM((span_total, kv_local, span_len, width), jnp.bfloat16),
                pltpu.VMEM((kv_local, rows, 2 * span_len), jnp.float32),
                pltpu.VMEM((kv_local, rows, 2 * span_len), jnp.bfloat16),
                pltpu.VMEM((kv_local, rows, 2 * head_dim), jnp.float32),
                pltpu.VMEM((kv_local, rows, head_dim), jnp.float32),
                pltpu.VMEM((kv_heads, slice_len, width), jnp.bfloat16),
                pltpu.SemaphoreType.DMA((longest,)),
                pltpu.SemaphoreType.DMA((len(parts), max(len(x[0][0]) for x in parts))),
            ],
        ),
        out_shape=[
            jax.ShapeDtypeStruct(queries.shape, jnp.bfloat16),
            jax.ShapeDtypeStruct((longest, kv_heads, slice_len, width), jnp.bfloat16),
        ],
        cost_estimate=pl.CostEstimate(
            flops=4 * work * head_dim, bytes_accessed=8 << 20, transcendentals=work
        ),
        compiler_params=pltpu.CompilerParams(vmem_limit_bytes=40 << 20),
    )(
        prompt_spans, prompt_tail, span_plan, decode_owner,
        jnp.concatenate([jnp.stack([inst_index, tp_index]).astype(jnp.int32), own_sources]),
        queries, *[x for _, x in hops], *[x for _, x in parts],
    )


def solution(mesh):
    placed = (
        P(("groups", "inst"), None, "tp"),
        P(("groups", "inst"), None, "tp", None),
        P("groups"),
        P("groups"),
        P("groups"),
        P("groups"),
    )
    return jax.shard_map(
        body,
        mesh=mesh,
        in_specs=placed,
        out_specs=(P(("groups", "inst"), None, "tp"), P(("groups", "inst"), None, "tp", None)),
        check_vma=False,
    )
```

```python
import functools
import math

import jax
import jax.numpy as jnp
from jax import lax
from jax.experimental import pallas as pl
from jax.experimental.pallas import tpu as pltpu
from jax.sharding import PartitionSpec as P

HEADS = 64
KVH = 8
LOG2E = 1.4426950408889634


def attend_kernel(
    spans_ref, tail_ref, plan_ref, owner_ref, place_at_ref, *refs,
    hops, parts, inst_size, tp_size, kv_local, per_head, head_dim, span_len, slot_count, longest,
):
    q_ref = refs[0]
    hop_refs = refs[1:1 + len(hops)]
    part_refs = refs[1 + len(hops):1 + len(hops) + len(parts)]
    (out_ref, cache_ref, place_ref, kv_ref, s_ref, p_ref, acc_ref, max_ref, zero_ref,
     page_sems, part_sems) = refs[1 + len(hops) + len(parts):]
    step = pl.program_id(0)
    inst = place_at_ref[0]
    tp = place_at_ref[1]
    prompt_count = spans_ref.shape[0]
    span_total = slot_count * inst_size
    slice_len = span_len // tp_size
    rows = per_head * span_len
    scale = LOG2E / math.sqrt(head_dim)

    def part_copies(act):
        for n, (pieces, j) in enumerate(parts):
            at = pl.ds(pl.multiple_of((tp ^ j) * slice_len, slice_len), slice_len)
            begin = 0
            for m, (hop, first_slot, size) in enumerate(pieces):
                slots = pl.ds(place_at_ref[2 + hop] * slot_count + first_slot, size)
                act(pltpu.make_async_copy(
                    part_refs[n].at[begin:begin + size], kv_ref.at[slots, :, at],
                    part_sems.at[n, m],
                ))
                begin += size

    def cache_copies(act):
        first = jnp.int32(0)
        count = jnp.int32(0)
        start = jnp.int32(0)
        for p in range(prompt_count):
            hit = owner_ref[p] == inst
            first = jnp.where(hit, start, first)
            count = jnp.where(hit, spans_ref[p], count)
            start = start + spans_ref[p]

        def row(r, unused):
            page = place_ref[jnp.minimum(first + r, span_total - 1)]
            for n, (hop, first_slot, size) in enumerate(hops):
                source = place_at_ref[2 + hop]
                slot = page - source * slot_count - first_slot
                here = (source >= 0) & (slot >= 0) & (slot < size)

                @pl.when((r < count) & here)
                def _():
                    act(pltpu.make_async_copy(
                        hop_refs[n].at[slot], cache_ref.at[r], page_sems.at[r]
                    ))

            @pl.when(r >= count)
            def _():
                act(pltpu.make_async_copy(zero_ref, cache_ref.at[r], page_sems.at[r]))

            return unused

        lax.fori_loop(0, longest, row, 0)

    @pl.when(step == 0)
    def _():
        part_copies(lambda copy: copy.start())

        def put(g, unused):
            place_ref[plan_ref[g]] = g
            return unused

        lax.fori_loop(0, span_total, put, 0)
        zero_ref[...] = jnp.zeros_like(zero_ref)
        cache_copies(lambda copy: copy.start())
        part_copies(lambda copy: copy.wait())

    own = inst * slot_count + step
    span = plan_ref[own]
    first = jnp.int32(0)
    end = jnp.int32(0)
    length = jnp.int32(0)
    for p in range(prompt_count):
        start = end
        end = end + spans_ref[p]
        inside = (span >= start) & (span < end)
        first = jnp.where(inside, start, first)
        length = jnp.where(inside, (spans_ref[p] - 1) * span_len + tail_ref[p], length)
    index = span - first
    live_rows = length - index * span_len
    ones = jnp.ones((span_len, head_dim), jnp.bfloat16)
    row_ids = lax.broadcasted_iota(jnp.int32, (span_len, span_len), 0)
    col_ids = lax.broadcasted_iota(jnp.int32, (span_len, span_len), 1)
    causal = row_ids >= col_ids

    def key_block(pages, g):
        return jnp.concatenate([kv_ref[page, g, :, :head_dim] for page in pages], axis=0)

    def value_block(pages, g):
        return jnp.concatenate(
            [
                jnp.concatenate([kv_ref[page, g, :, head_dim:], ones], axis=1)
                for page in pages
            ],
            axis=0,
        )

    def attend(pages, begin):
        wide = len(pages) * span_len
        for g in range(kv_local):
            q = jnp.concatenate(
                [
                    q_ref[0, :, (g * per_head + h) * head_dim:(g * per_head + h + 1) * head_dim]
                    for h in range(per_head)
                ],
                axis=0,
            )
            s_ref[g, :, :wide] = lax.dot_general(
                q, key_block(pages, g), (((1,), (1,)), ((), ())),
                preferred_element_type=jnp.float32,
            )
        for g in range(kv_local):
            rescales = []
            for h in range(per_head):
                at = slice(h * span_len, (h + 1) * span_len)
                s = s_ref[g, at, :wide] * scale
                if begin:
                    own_part = jnp.where(causal, s[:, wide - span_len:], -1e30)
                    if len(pages) > 1:
                        s = jnp.concatenate([s[:, :wide - span_len], own_part], axis=1)
                    else:
                        s = own_part
                top = jnp.max(s, axis=1, keepdims=True)
                if begin:
                    top = jnp.broadcast_to(top, (span_len, head_dim))
                else:
                    old = max_ref[g, at]
                    top = jnp.maximum(old, top)
                    rescales.append(jnp.exp2(old - top))
                max_ref[g, at] = top
                p_ref[g, at, :wide] = jnp.exp2(
                    s - jnp.concatenate([top] * len(pages), axis=1)
                ).astype(jnp.bfloat16)
            mixed = jnp.dot(
                p_ref[g, :, :wide], value_block(pages, g), preferred_element_type=jnp.float32
            )
            if begin:
                acc_ref[g] = mixed
            else:
                for h in range(per_head):
                    at = slice(h * span_len, (h + 1) * span_len)
                    acc_ref[g, at] = acc_ref[g, at] * jnp.concatenate(
                        [rescales[h], rescales[h]], axis=1
                    ) + mixed[at]

    odd = lax.rem(index, 2)

    @pl.when(odd == 0)
    def _():
        attend([own], True)

    @pl.when(odd == 1)
    def _():
        attend([place_ref[first], own], True)

    def pair(j, unused):
        at = first + odd + 2 * j
        attend([place_ref[at], place_ref[at + 1]], False)
        return unused

    lax.fori_loop(0, index // 2, pair, 0)

    live = lax.broadcasted_iota(jnp.int32, (span_len, head_dim), 0) < live_rows
    for g in range(kv_local):
        for h in range(per_head):
            head = g * per_head + h
            total = acc_ref[g, h * span_len:(h + 1) * span_len]
            out_ref[0, :, head * head_dim:(head + 1) * head_dim] = jnp.where(
                live, total[:, :head_dim] / total[:, head_dim:], 0.0
            ).astype(jnp.bfloat16)

    @pl.when(step == slot_count - 1)
    def _():
        cache_copies(lambda copy: copy.wait())


def after(values, earlier):
    return lax.optimization_barrier((list(values), list(earlier)))[0]


def move_pages(kv_new, kv_local):
    inst_size = lax.axis_size("inst")
    tp_size = lax.axis_size("tp")
    inst = lax.axis_index("inst")
    tp = lax.axis_index("tp")
    slot_count, kv_heads = kv_new.shape[:2]
    sources = [list(range(inst_size))]
    hops = [((0, 0, slot_count), kv_new)]
    parts = []

    def along(x, pairs):
        return lax.ppermute(x, "inst", pairs)

    def exchange(*pieces):
        names = [name for name, _ in pieces]
        found = []
        for j in range(tp_size):
            head = ((tp ^ j) * kv_heads) // tp_size
            sent = [lax.dynamic_slice_in_dim(x, head, kv_local, 1) for _, x in pieces]
            sent = jnp.concatenate(sent, axis=0) if len(sent) > 1 else sent[0]
            if j:
                sent = lax.ppermute(sent, "tp", [(t, t ^ j) for t in range(tp_size)])
            found.append(((names, j), sent))
        parts.extend(found)
        return [x for _, x in found]

    if inst_size != 4:
        exchange(hops[0])
        for s in range(1, inst_size):
            sources.append([(i - s) % inst_size for i in range(inst_size)])
            pairs = [(i, (i + s) % inst_size) for i in range(inst_size)]
            hops.append(((s, 0, slot_count), along(kv_new, pairs)))
            exchange(hops[-1])
        return hops, parts, sources

    middle = (inst == 1) | (inst == 2)
    sources += [[1, 0, 3, 2], [-1, 2, 1, -1], [-1, 3, 0, -1], [2, -1, -1, 1], [3, -1, -1, 0]]
    second, third = 6, 7
    sources += [[2, 2, 1, 1], [3, 3, 0, 0]]
    whole = slot_count
    outer = along(kv_new, [(0, 1), (1, 0), (2, 3), (3, 2)])
    inner = along(kv_new, [(1, 2), (2, 1)])
    waiting = exchange(hops[0])
    outer_on, inner_on = after([outer, inner], waiting)
    crossed = along(outer_on, [(1, 2), (2, 1)])
    inner_ends = along(inner_on, [(1, 0), (2, 3)])
    waiting = exchange(((1, 0, whole), outer_on))
    crossed_on = after([crossed], waiting)[0]
    crossed_ends = along(crossed_on, [(1, 0), (2, 3)])
    two = jnp.where(middle, inner, inner_ends)
    waiting = exchange(((second, 0, whole), two))
    three = after([jnp.where(middle, crossed, crossed_ends)], waiting)[0]
    exchange(((third, 0, whole), three))
    for hop, x in enumerate((outer, inner, crossed, inner_ends, crossed_ends), 1):
        hops.append(((hop, 0, whole), x))
    return hops, parts, sources


def body(queries, kv_new, prompt_spans, prompt_tail, span_plan, decode_owner):
    tp_size = lax.axis_size("tp")
    inst_size = lax.axis_size("inst")
    tp_index = lax.axis_index("tp")
    inst_index = lax.axis_index("inst")
    slot_count, span_len, row_width = queries.shape
    kv_heads, slice_len, width = kv_new.shape[1:]
    head_dim = width // 2
    local_heads = row_width // head_dim
    kv_local = max(1, kv_heads // tp_size)
    per_head = local_heads // kv_local
    span_total = slot_count * inst_size
    longest = span_total // 2
    hops, parts, sources = move_pages(kv_new, kv_local)
    own_sources = lax.dynamic_index_in_dim(jnp.asarray(sources, jnp.int32), inst_index, 1, False)
    kernel = functools.partial(
        attend_kernel,
        hops=[name for name, _ in hops],
        parts=[name for name, _ in parts],
        inst_size=inst_size,
        tp_size=tp_size,
        kv_local=kv_local,
        per_head=per_head,
        head_dim=head_dim,
        span_len=span_len,
        slot_count=slot_count,
        longest=longest,
    )
    work = slot_count * span_total // 4 * local_heads * span_len * span_len
    anywhere = pl.BlockSpec(memory_space=pl.ANY)
    by_slot = pl.BlockSpec((1, span_len, row_width), lambda i, *_: (i, 0, 0))
    rows = per_head * span_len
    return pl.pallas_call(
        kernel,
        grid_spec=pltpu.PrefetchScalarGridSpec(
            num_scalar_prefetch=5,
            grid=(slot_count,),
            in_specs=[by_slot] + [anywhere] * (len(hops) + len(parts)),
            out_specs=[by_slot, anywhere],
            scratch_shapes=[
                pltpu.SMEM((span_total,), jnp.int32),
                pltpu.VMEM((span_total, kv_local, span_len, width), jnp.bfloat16),
                pltpu.VMEM((kv_local, rows, 2 * span_len), jnp.float32),
                pltpu.VMEM((kv_local, rows, 2 * span_len), jnp.bfloat16),
                pltpu.VMEM((kv_local, rows, 2 * head_dim), jnp.float32),
                pltpu.VMEM((kv_local, rows, head_dim), jnp.float32),
                pltpu.VMEM((kv_heads, slice_len, width), jnp.bfloat16),
                pltpu.SemaphoreType.DMA((longest,)),
                pltpu.SemaphoreType.DMA((len(parts), max(len(x[0][0]) for x in parts))),
            ],
        ),
        out_shape=[
            jax.ShapeDtypeStruct(queries.shape, jnp.bfloat16),
            jax.ShapeDtypeStruct((longest, kv_heads, slice_len, width), jnp.bfloat16),
        ],
        cost_estimate=pl.CostEstimate(
            flops=4 * work * head_dim, bytes_accessed=8 << 20, transcendentals=work
        ),
        compiler_params=pltpu.CompilerParams(vmem_limit_bytes=40 << 20),
    )(
        prompt_spans, prompt_tail, span_plan, decode_owner,
        jnp.concatenate([jnp.stack([inst_index, tp_index]).astype(jnp.int32), own_sources]),
        queries, *[x for _, x in hops], *[x for _, x in parts],
    )


def solution(mesh):
    placed = (
        P(("groups", "inst"), None, "tp"),
        P(("groups", "inst"), None, "tp", None),
        P("groups"),
        P("groups"),
        P("groups"),
        P("groups"),
    )
    return jax.shard_map(
        body,
        mesh=mesh,
        in_specs=placed,
        out_specs=(P(("groups", "inst"), None, "tp"), P(("groups", "inst"), None, "tp", None)),
        check_vma=False,
    )
```

```python
import functools
import math

import jax
import jax.numpy as jnp
from jax import lax
from jax.experimental import pallas as pl
from jax.experimental.pallas import tpu as pltpu
from jax.sharding import PartitionSpec as P

HEADS = 64
KVH = 8
LOG2E = 1.4426950408889634


def attend_kernel(
    spans_ref, tail_ref, plan_ref, owner_ref, place_at_ref, *refs,
    covers, hops, parts, first_call, last_call,
    inst_size, tp_size, kv_local, per_head, head_dim, span_len, slot_count, longest,
):
    refs = list(refs)

    def take(count):
        taken = refs[:count]
        del refs[:count]
        return taken

    (q_ref,) = take(1)
    mixed_ref, total_ref = (None, None) if first_call else take(2)
    hop_refs = take(len(hops))
    part_refs = take(len(parts))
    if last_call:
        out_ref, cache_ref = take(2)
    else:
        out_ref, next_total_ref = take(2)
    place_ref, list_ref, kv_ref, s_ref, p_ref, acc_ref, max_ref, part_sems = take(8)
    if last_call:
        zero_ref, page_sems = take(2)
    step = pl.program_id(0)
    inst = place_at_ref[0]
    tp = place_at_ref[1]
    prompt_count = spans_ref.shape[0]
    span_total = slot_count * inst_size
    slice_len = span_len // tp_size
    scale = LOG2E / math.sqrt(head_dim)

    def part_copies(act):
        for n, (pieces, j) in enumerate(parts):
            at = pl.ds(pl.multiple_of((tp ^ j) * slice_len, slice_len), slice_len)
            begin = 0
            for m, (hop, first_slot, size) in enumerate(pieces):
                slots = pl.ds(place_at_ref[2 + hop] * slot_count + first_slot, size)
                act(pltpu.make_async_copy(
                    part_refs[n].at[begin:begin + size], kv_ref.at[slots, :, at],
                    part_sems.at[n, m],
                ))
                begin += size

    def cache_copies(act):
        first = jnp.int32(0)
        count = jnp.int32(0)
        start = jnp.int32(0)
        for p in range(prompt_count):
            hit = owner_ref[p] == inst
            first = jnp.where(hit, start, first)
            count = jnp.where(hit, spans_ref[p], count)
            start = start + spans_ref[p]

        def row(r, unused):
            page = place_ref[jnp.minimum(first + r, span_total - 1)]
            for n, (hop, first_slot, size) in enumerate(hops):
                source = place_at_ref[2 + hop]
                slot = page - source * slot_count - first_slot
                here = (source >= 0) & (slot >= 0) & (slot < size)

                @pl.when((r < count) & here)
                def _():
                    act(pltpu.make_async_copy(
                        hop_refs[n].at[slot], cache_ref.at[r], page_sems.at[r]
                    ))

            @pl.when(r >= count)
            def _():
                act(pltpu.make_async_copy(zero_ref, cache_ref.at[r], page_sems.at[r]))

            return unused

        lax.fori_loop(0, longest, row, 0)

    @pl.when(step == 0)
    def _():
        part_copies(lambda copy: copy.start())

        def put(g, unused):
            place_ref[plan_ref[g]] = g
            return unused

        lax.fori_loop(0, span_total, put, 0)
        if last_call:
            zero_ref[...] = jnp.zeros_like(zero_ref)
            cache_copies(lambda copy: copy.start())
        part_copies(lambda copy: copy.wait())

    own = inst * slot_count + step
    span = plan_ref[own]
    first = jnp.int32(0)
    end = jnp.int32(0)
    length = jnp.int32(0)
    for p in range(prompt_count):
        start = end
        end = end + spans_ref[p]
        inside = (span >= start) & (span < end)
        first = jnp.where(inside, start, first)
        length = jnp.where(inside, (spans_ref[p] - 1) * span_len + tail_ref[p], length)
    live_rows = length - (span - first) * span_len

    def look(k, count):
        page = place_ref[k]
        source = page // slot_count
        covered = jnp.bool_(False)
        for hop in covers:
            covered = covered | (place_at_ref[2 + hop] == source)
        list_ref[count] = page
        return count + covered.astype(jnp.int32)

    count = lax.fori_loop(first, span, look, jnp.int32(0))

    ones = jnp.ones((span_len, head_dim), jnp.bfloat16)
    row_ids = lax.broadcasted_iota(jnp.int32, (span_len, span_len), 0)
    col_ids = lax.broadcasted_iota(jnp.int32, (span_len, span_len), 1)
    causal = row_ids >= col_ids

    def rows_of(h):
        return slice(h * span_len, (h + 1) * span_len)

    def key_block(pages, g):
        return jnp.concatenate([kv_ref[page, g, :, :head_dim] for page in pages], axis=0)

    def value_block(pages, g):
        return jnp.concatenate(
            [
                jnp.concatenate([kv_ref[page, g, :, head_dim:], ones], axis=1)
                for page in pages
            ],
            axis=0,
        )

    def attend(pages, since):
        wide = len(pages) * span_len
        for g in range(kv_local):
            q = jnp.concatenate(
                [
                    q_ref[0, :, (g * per_head + h) * head_dim:(g * per_head + h + 1) * head_dim]
                    for h in range(per_head)
                ],
                axis=0,
            )
            s_ref[g, :, :wide] = lax.dot_general(
                q, key_block(pages, g), (((1,), (1,)), ((), ())),
                preferred_element_type=jnp.float32,
            )
        for g in range(kv_local):
            rescales = []
            for h in range(per_head):
                at = rows_of(h)
                s = s_ref[g, at, :wide] * scale
                if since == "start":
                    own_part = jnp.where(causal, s[:, wide - span_len:], -1e30)
                    if len(pages) > 1:
                        s = jnp.concatenate([s[:, :wide - span_len], own_part], axis=1)
                    else:
                        s = own_part
                top = jnp.max(s, axis=1, keepdims=True)
                if since == "start":
                    top = jnp.broadcast_to(top, (span_len, head_dim))
                else:
                    old = total_ref[0, g, at] if since == "given" else max_ref[g, at]
                    top = jnp.maximum(old, top)
                    rescales.append(jnp.exp2(old - top))
                max_ref[g, at] = top
                p_ref[g, at, :wide] = jnp.exp2(
                    s - jnp.concatenate([top] * len(pages), axis=1)
                ).astype(jnp.bfloat16)
            mixed = jnp.dot(
                p_ref[g, :, :wide], value_block(pages, g), preferred_element_type=jnp.float32
            )
            if since == "start":
                acc_ref[g] = mixed
                continue
            for h in range(per_head):
                at = rows_of(h)
                if since == "given":
                    old = jnp.concatenate([mixed_ref[0, g, at] * rescales[h], rescales[h]], axis=1)
                else:
                    old = acc_ref[g, at] * jnp.concatenate([rescales[h], rescales[h]], axis=1)
                acc_ref[g, at] = old + mixed[at]

    def pairs(begin):
        def pair(j, unused):
            at = begin + 2 * j
            attend([list_ref[at], list_ref[at + 1]], "here")
            return unused

        lax.fori_loop(0, (count - begin) // 2, pair, 0)

    live = lax.broadcasted_iota(jnp.int32, (span_len, head_dim), 0) < live_rows

    def put_out(g, h, mixed):
        head = g * per_head + h
        out_ref[0, :, head * head_dim:(head + 1) * head_dim] = jnp.where(
            live, mixed, 0.0
        ).astype(jnp.bfloat16)

    def finish():
        for g in range(kv_local):
            for h in range(per_head):
                at = rows_of(h)
                total = acc_ref[g, at, head_dim:]
                mixed = acc_ref[g, at, :head_dim] / total
                if last_call:
                    put_out(g, h, mixed)
                else:
                    out_ref[0, g, at] = mixed
                    next_total_ref[0, g, at] = max_ref[g, at] + jnp.log(total) * LOG2E

    if first_call:
        odd = lax.rem(count, 2)

        @pl.when(odd == 0)
        def _():
            attend([own], "start")

        @pl.when(odd == 1)
        def _():
            attend([list_ref[0], own], "start")

        pairs(odd)
        finish()
    else:
        used = 2 - lax.rem(count, 2)

        @pl.when(count == 0)
        def _():
            for g in range(kv_local):
                for h in range(per_head):
                    put_out(g, h, mixed_ref[0, g, rows_of(h)])

        @pl.when(count > 0)
        def _():
            @pl.when(used == 1)
            def _():
                attend([list_ref[0]], "given")

            @pl.when(used == 2)
            def _():
                attend([list_ref[0], list_ref[1]], "given")

            pairs(used)
            finish()

    if last_call:
        @pl.when(step == slot_count - 1)
        def _():
            cache_copies(lambda copy: copy.wait())


def after(values, earlier):
    return lax.optimization_barrier((list(values), list(earlier)))[0]


def move_pages(kv_new, kv_local, attend):
    inst_size = lax.axis_size("inst")
    tp_size = lax.axis_size("tp")
    inst = lax.axis_index("inst")
    tp = lax.axis_index("tp")
    slot_count, kv_heads = kv_new.shape[:2]
    sources = [list(range(inst_size))]
    hops = [((0, 0, slot_count), kv_new)]
    parts = []

    def along(x, pairs):
        return lax.ppermute(x, "inst", pairs)

    def exchange(*pieces):
        names = [name for name, _ in pieces]
        found = []
        for j in range(tp_size):
            head = ((tp ^ j) * kv_heads) // tp_size
            sent = [lax.dynamic_slice_in_dim(x, head, kv_local, 1) for _, x in pieces]
            sent = jnp.concatenate(sent, axis=0) if len(sent) > 1 else sent[0]
            if j:
                sent = lax.ppermute(sent, "tp", [(t, t ^ j) for t in range(tp_size)])
            found.append(((names, j), sent))
        parts.extend(found)
        return [x for _, x in found]

    if inst_size != 4:
        exchange(hops[0])
        for s in range(1, inst_size):
            sources.append([(i - s) % inst_size for i in range(inst_size)])
            pairs = [(i, (i + s) % inst_size) for i in range(inst_size)]
            hops.append(((s, 0, slot_count), along(kv_new, pairs)))
            exchange(hops[-1])
        return [], (list(range(inst_size)), parts, sources), hops

    middle = (inst == 1) | (inst == 2)
    sources += [[1, 0, 3, 2], [-1, 2, 1, -1], [-1, 3, 0, -1], [2, -1, -1, 1], [3, -1, -1, 0]]
    second, third = 6, 7
    sources += [[2, 2, 1, 1], [3, 3, 0, 0]]
    whole = slot_count
    half = slot_count // 2
    outer = along(kv_new, [(0, 1), (1, 0), (2, 3), (3, 2)])
    inner = along(kv_new, [(1, 2), (2, 1)])
    waiting = exchange(hops[0])
    outer_on, inner_on = after([outer, inner], waiting)
    crossed = along(outer_on, [(1, 2), (2, 1)])
    inner_ends = along(inner_on, [(1, 0), (2, 3)])
    waiting = exchange(((1, 0, whole), outer_on))
    early = len(parts)
    state = attend([0, 1], parts, sources)
    crossed_on = after([crossed], waiting)[0]
    crossed_half = lax.optimization_barrier([crossed_on[:half], crossed_on[half:]])
    crossed_ends = [along(x, [(1, 0), (2, 3)]) for x in crossed_half]
    two = jnp.where(middle, inner, inner_ends)
    waiting = exchange(((second, 0, whole), two))
    waiting = waiting + list(state)
    for n in range(2):
        three = jnp.where(middle, crossed_half[n], crossed_ends[n])
        three = after([three], waiting)[0]
        exchange(((third, n * half, half), three))
        hops.append(((5, n * half, half), crossed_ends[n]))
    for hop, x in enumerate((outer, inner, crossed, inner_ends), 1):
        hops.append(((hop, 0, whole), x))
    return state, ([second, third], parts[early:], sources), hops


def body(queries, kv_new, prompt_spans, prompt_tail, span_plan, decode_owner):
    tp_size = lax.axis_size("tp")
    inst_size = lax.axis_size("inst")
    tp_index = lax.axis_index("tp")
    inst_index = lax.axis_index("inst")
    slot_count, span_len, row_width = queries.shape
    kv_heads, slice_len, width = kv_new.shape[1:]
    head_dim = width // 2
    local_heads = row_width // head_dim
    kv_local = max(1, kv_heads // tp_size)
    per_head = local_heads // kv_local
    span_total = slot_count * inst_size
    longest = span_total // 2
    anywhere = pl.BlockSpec(memory_space=pl.ANY)
    by_slot = pl.BlockSpec((1, span_len, row_width), lambda i, *_: (i, 0, 0))
    rows = per_head * span_len
    state_shape = (slot_count, kv_local, rows, head_dim)
    state_spec = pl.BlockSpec((1,) + state_shape[1:], lambda i, *_: (i, 0, 0, 0))
    work = slot_count * 4 * local_heads * span_len * span_len

    def attend(covers, parts, sources, state=(), hops=None):
        first_call, last_call = not state, hops is not None
        hops = hops or []
        own_sources = lax.dynamic_index_in_dim(
            jnp.asarray(sources, jnp.int32), inst_index, 1, False
        )
        numbers = (
            prompt_spans, prompt_tail, span_plan, decode_owner,
            jnp.concatenate([jnp.stack([inst_index, tp_index]).astype(jnp.int32), own_sources]),
        )
        kernel = functools.partial(
            attend_kernel,
            covers=covers,
            hops=[name for name, _ in hops],
            parts=[name for name, _ in parts],
            first_call=first_call,
            last_call=last_call,
            inst_size=inst_size,
            tp_size=tp_size,
            kv_local=kv_local,
            per_head=per_head,
            head_dim=head_dim,
            span_len=span_len,
            slot_count=slot_count,
            longest=longest,
        )
        scratch = [
            pltpu.SMEM((span_total,), jnp.int32),
            pltpu.SMEM((span_total,), jnp.int32),
            pltpu.VMEM((span_total, kv_local, span_len, width), jnp.bfloat16),
            pltpu.VMEM((kv_local, rows, 2 * span_len), jnp.float32),
            pltpu.VMEM((kv_local, rows, 2 * span_len), jnp.bfloat16),
            pltpu.VMEM((kv_local, rows, 2 * head_dim), jnp.float32),
            pltpu.VMEM((kv_local, rows, head_dim), jnp.float32),
            pltpu.SemaphoreType.DMA((len(parts), max(len(x[0][0]) for x in parts))),
        ]
        if last_call:
            scratch += [
                pltpu.VMEM((kv_heads, slice_len, width), jnp.bfloat16),
                pltpu.SemaphoreType.DMA((longest,)),
            ]
            out_specs = [by_slot, anywhere]
            out_shape = [
                jax.ShapeDtypeStruct(queries.shape, jnp.bfloat16),
                jax.ShapeDtypeStruct((longest, kv_heads, slice_len, width), jnp.bfloat16),
            ]
        else:
            out_specs = [state_spec] * 2
            out_shape = [jax.ShapeDtypeStruct(state_shape, jnp.float32)] * 2
        return pl.pallas_call(
            kernel,
            grid_spec=pltpu.PrefetchScalarGridSpec(
                num_scalar_prefetch=len(numbers),
                grid=(slot_count,),
                in_specs=[by_slot] + [state_spec] * len(state)
                + [anywhere] * (len(hops) + len(parts)),
                out_specs=out_specs,
                scratch_shapes=scratch,
            ),
            out_shape=out_shape,
            cost_estimate=pl.CostEstimate(
                flops=4 * work * head_dim, bytes_accessed=8 << 20, transcendentals=work
            ),
            compiler_params=pltpu.CompilerParams(vmem_limit_bytes=40 << 20),
        )(
            *numbers, queries, *state, *[x for _, x in hops], *[x for _, x in parts],
        )

    state, left, hops = move_pages(kv_new, kv_local, attend)
    return tuple(attend(*left, state, hops))


def solution(mesh):
    placed = (
        P(("groups", "inst"), None, "tp"),
        P(("groups", "inst"), None, "tp", None),
        P("groups"),
        P("groups"),
        P("groups"),
        P("groups"),
    )
    return jax.shard_map(
        body,
        mesh=mesh,
        in_specs=placed,
        out_specs=(P(("groups", "inst"), None, "tp"), P(("groups", "inst"), None, "tp", None)),
        check_vma=False,
    )
```

```python
import functools
import math

import jax
import jax.numpy as jnp
from jax import lax
from jax.experimental import pallas as pl
from jax.experimental.pallas import tpu as pltpu
from jax.sharding import PartitionSpec as P

HEADS = 64
KVH = 8
LOG2E = 1.4426950408889634
STEP = 4


class Part:
    def __init__(self, ref, start):
        self.ref, self.start = ref, start

    def __getitem__(self, at):
        return self.ref[self.start + at]


def attend_kernel(
    numbers_ref, *refs,
    covers, hops, parts, first_call, last_call,
    inst_size, tp_size, kv_local, per_head, head_dim, span_len, slot_count, longest, prompt_count,
):
    refs = list(refs)

    def take(count):
        taken = refs[:count]
        del refs[:count]
        return taken

    (q_ref,) = take(1)
    mixed_ref, total_ref = (None, None) if first_call else take(2)
    hop_refs = take(len(hops))
    part_refs = take(len(parts))
    if last_call:
        out_ref, cache_ref = take(2)
    else:
        out_ref, next_total_ref, mark_ref = take(3)
        mark_ref[...] = jnp.zeros_like(mark_ref)
    place_ref, list_ref, kv_ref, s_ref, p_ref, acc_ref, max_ref, part_sems = take(8)
    if last_call:
        zero_ref, page_sems = take(2)
    step = pl.program_id(0)
    span_total = slot_count * inst_size
    spans_ref = Part(numbers_ref, 0)
    tail_ref = Part(numbers_ref, prompt_count)
    owner_ref = Part(numbers_ref, 2 * prompt_count)
    plan_ref = Part(numbers_ref, 3 * prompt_count)
    place_at_ref = Part(numbers_ref, 3 * prompt_count + span_total)
    inst = place_at_ref[0]
    tp = place_at_ref[1]
    slice_len = span_len // tp_size
    scale = LOG2E / math.sqrt(head_dim)

    def part_copies(act):
        for n, (pieces, j) in enumerate(parts):
            at = pl.ds(pl.multiple_of((tp ^ j) * slice_len, slice_len), slice_len)
            begin = 0
            for m, (hop, first_slot, size) in enumerate(pieces):
                slots = pl.ds(place_at_ref[2 + hop] * slot_count + first_slot, size)
                act(pltpu.make_async_copy(
                    part_refs[n].at[begin:begin + size], kv_ref.at[slots, :, at],
                    part_sems.at[n, m],
                ))
                begin += size

    def cache_copies(act):
        first = jnp.int32(0)
        count = jnp.int32(0)
        start = jnp.int32(0)
        for p in range(prompt_count):
            hit = owner_ref[p] == inst
            first = jnp.where(hit, start, first)
            count = jnp.where(hit, spans_ref[p], count)
            start = start + spans_ref[p]

        def row(r, unused):
            page = place_ref[jnp.minimum(first + r, span_total - 1)]
            for n, (hop, first_slot, size) in enumerate(hops):
                source = place_at_ref[2 + hop]
                slot = page - source * slot_count - first_slot
                here = (source >= 0) & (slot >= 0) & (slot < size)

                @pl.when((r < count) & here)
                def _():
                    act(pltpu.make_async_copy(
                        hop_refs[n].at[slot], cache_ref.at[r], page_sems.at[r]
                    ))

            @pl.when(r >= count)
            def _():
                act(pltpu.make_async_copy(zero_ref, cache_ref.at[r], page_sems.at[r]))

            return unused

        lax.fori_loop(0, longest, row, 0)

    @pl.when(step == 0)
    def _():
        part_copies(lambda copy: copy.start())

        def put(g, unused):
            place_ref[plan_ref[g]] = g
            return unused

        lax.fori_loop(0, span_total, put, 0)
        if last_call:
            zero_ref[...] = jnp.zeros_like(zero_ref)
            cache_copies(lambda copy: copy.start())
        part_copies(lambda copy: copy.wait())

    own = inst * slot_count + step
    span = plan_ref[own]
    first = jnp.int32(0)
    end = jnp.int32(0)
    length = jnp.int32(0)
    for p in range(prompt_count):
        start = end
        end = end + spans_ref[p]
        inside = (span >= start) & (span < end)
        first = jnp.where(inside, start, first)
        length = jnp.where(inside, (spans_ref[p] - 1) * span_len + tail_ref[p], length)
    live_rows = length - (span - first) * span_len

    def look(k, count):
        page = place_ref[k]
        source = page // slot_count
        covered = jnp.bool_(False)
        for hop in covers:
            covered = covered | (place_at_ref[2 + hop] == source)
        list_ref[count] = page
        return count + covered.astype(jnp.int32)

    count = lax.fori_loop(first, span, look, jnp.int32(0))

    ones = jnp.ones((span_len, head_dim), jnp.bfloat16)
    row_ids = lax.broadcasted_iota(jnp.int32, (span_len, span_len), 0)
    col_ids = lax.broadcasted_iota(jnp.int32, (span_len, span_len), 1)
    causal = row_ids >= col_ids

    def rows_of(h):
        return slice(h * span_len, (h + 1) * span_len)

    def key_block(pages, g):
        return jnp.concatenate([kv_ref[page, g, :, :head_dim] for page in pages], axis=0)

    def value_block(pages, g):
        return jnp.concatenate(
            [
                jnp.concatenate([kv_ref[page, g, :, head_dim:], ones], axis=1)
                for page in pages
            ],
            axis=0,
        )

    def attend(pages, since):
        wide = len(pages) * span_len
        for g in range(kv_local):
            q = jnp.concatenate(
                [
                    q_ref[0, :, (g * per_head + h) * head_dim:(g * per_head + h + 1) * head_dim]
                    for h in range(per_head)
                ],
                axis=0,
            )
            s_ref[g, :, :wide] = lax.dot_general(
                q, key_block(pages, g), (((1,), (1,)), ((), ())),
                preferred_element_type=jnp.float32,
            )
        for g in range(kv_local):
            rescales = []
            for h in range(per_head):
                at = rows_of(h)
                s = s_ref[g, at, :wide] * scale
                if since == "start":
                    own_part = jnp.where(causal, s[:, wide - span_len:], -1e30)
                    if len(pages) > 1:
                        s = jnp.concatenate([s[:, :wide - span_len], own_part], axis=1)
                    else:
                        s = own_part
                top = jnp.max(s, axis=1, keepdims=True)
                if since == "start":
                    top = jnp.broadcast_to(top, (span_len, head_dim))
                else:
                    old = total_ref[0, g, at] if since == "given" else max_ref[g, at]
                    top = jnp.maximum(old, top)
                    rescales.append(jnp.exp2(old - top))
                max_ref[g, at] = top
                p_ref[g, at, :wide] = jnp.exp2(
                    s - jnp.concatenate([top] * len(pages), axis=1)
                ).astype(jnp.bfloat16)
            mixed = jnp.dot(
                p_ref[g, :, :wide], value_block(pages, g), preferred_element_type=jnp.float32
            )
            if since == "start":
                acc_ref[g] = mixed
                continue
            for h in range(per_head):
                at = rows_of(h)
                if since == "given":
                    old = jnp.concatenate([mixed_ref[0, g, at] * rescales[h], rescales[h]], axis=1)
                else:
                    old = acc_ref[g, at] * jnp.concatenate([rescales[h], rescales[h]], axis=1)
                acc_ref[g, at] = old + mixed[at]

    def rest(begin):
        def block(j, unused):
            at = begin + STEP * j
            attend([list_ref[at + n] for n in range(STEP)], "here")
            return unused

        lax.fori_loop(0, (count - begin) // STEP, block, 0)

    live = lax.broadcasted_iota(jnp.int32, (span_len, head_dim), 0) < live_rows

    def put_out(g, h, mixed):
        head = g * per_head + h
        out_ref[0, :, head * head_dim:(head + 1) * head_dim] = jnp.where(
            live, mixed, 0.0
        ).astype(jnp.bfloat16)

    def finish():
        for g in range(kv_local):
            for h in range(per_head):
                at = rows_of(h)
                total = acc_ref[g, at, head_dim:]
                mixed = acc_ref[g, at, :head_dim] / total
                if last_call:
                    put_out(g, h, mixed)
                else:
                    out_ref[0, g, at] = mixed
                    next_total_ref[0, g, at] = max_ref[g, at] + jnp.log(total) * LOG2E

    if first_call:
        over = lax.rem(count, STEP)
        for n in range(STEP):
            @pl.when(over == n)
            def _():
                attend([list_ref[m] for m in range(n)] + [own], "start")

        rest(over)
        finish()
    else:
        over = lax.rem(count + STEP - 1, STEP) + 1

        @pl.when(count == 0)
        def _():
            for g in range(kv_local):
                for h in range(per_head):
                    put_out(g, h, mixed_ref[0, g, rows_of(h)])

        @pl.when(count > 0)
        def _():
            for n in range(1, STEP + 1):
                @pl.when(over == n)
                def _():
                    attend([list_ref[m] for m in range(n)], "given")

            rest(over)
            finish()

    if last_call:
        @pl.when(step == slot_count - 1)
        def _():
            cache_copies(lambda copy: copy.wait())


def after(values, earlier):
    return lax.optimization_barrier((list(values), list(earlier)))[0]


def move_pages(kv_new, kv_local, attend):
    inst_size = lax.axis_size("inst")
    tp_size = lax.axis_size("tp")
    inst = lax.axis_index("inst")
    tp = lax.axis_index("tp")
    slot_count, kv_heads = kv_new.shape[:2]
    sources = [list(range(inst_size))]
    hops = [((0, 0, slot_count), kv_new)]
    parts = []

    def along(x, pairs):
        return lax.ppermute(x, "inst", pairs)

    def exchange(*pieces):
        names = [name for name, _ in pieces]
        found = []
        for j in range(tp_size):
            head = ((tp ^ j) * kv_heads) // tp_size
            sent = [lax.dynamic_slice_in_dim(x, head, kv_local, 1) for _, x in pieces]
            sent = jnp.concatenate(sent, axis=0) if len(sent) > 1 else sent[0]
            if j:
                sent = lax.ppermute(sent, "tp", [(t, t ^ j) for t in range(tp_size)])
            found.append(((names, j), sent))
        parts.extend(found)
        return [x for _, x in found]

    if inst_size != 4:
        exchange(hops[0])
        for s in range(1, inst_size):
            sources.append([(i - s) % inst_size for i in range(inst_size)])
            pairs = [(i, (i + s) % inst_size) for i in range(inst_size)]
            hops.append(((s, 0, slot_count), along(kv_new, pairs)))
            exchange(hops[-1])
        return [], (list(range(inst_size)), parts, sources), hops

    middle = (inst == 1) | (inst == 2)
    sources += [[1, 0, 3, 2], [-1, 2, 1, -1], [-1, 3, 0, -1], [2, -1, -1, 1], [3, -1, -1, 0]]
    second, third = 6, 7
    sources += [[2, 2, 1, 1], [3, 3, 0, 0]]
    whole = slot_count
    half = slot_count // 2
    outer = along(kv_new, [(0, 1), (1, 0), (2, 3), (3, 2)])
    inner = along(kv_new, [(1, 2), (2, 1)])
    waiting = exchange(hops[0])
    outer_on, inner_on = after([outer, inner], waiting)
    crossed = along(outer_on, [(1, 2), (2, 1)])
    inner_ends = along(inner_on, [(1, 0), (2, 3)])
    waiting = exchange(((1, 0, whole), outer_on))
    names, arrays = zip(*parts)
    *state, mark = attend([0, 1], list(zip(names, after(arrays, [crossed, inner_ends]))), sources)
    early = len(parts)
    crossed_on = after([crossed], waiting)[0]
    crossed_half = lax.optimization_barrier([crossed_on[:half], crossed_on[half:]])
    crossed_ends = [along(x, [(1, 0), (2, 3)]) for x in crossed_half]
    two = jnp.where(middle, inner, inner_ends)
    waiting = exchange(((second, 0, whole), two))
    waiting = waiting + [mark]
    for n in range(2):
        three = jnp.where(middle, crossed_half[n], crossed_ends[n])
        three = after([three], waiting)[0]
        waiting = exchange(((third, n * half, half), three))
        hops.append(((5, n * half, half), crossed_ends[n]))
    for hop, x in enumerate((outer, inner, crossed, inner_ends), 1):
        hops.append(((hop, 0, whole), x))
    return state, ([second, third], parts[early:], sources), hops


def body(queries, kv_new, prompt_spans, prompt_tail, span_plan, decode_owner):
    tp_size = lax.axis_size("tp")
    inst_size = lax.axis_size("inst")
    tp_index = lax.axis_index("tp")
    inst_index = lax.axis_index("inst")
    slot_count, span_len, row_width = queries.shape
    kv_heads, slice_len, width = kv_new.shape[1:]
    head_dim = width // 2
    local_heads = row_width // head_dim
    kv_local = max(1, kv_heads // tp_size)
    per_head = local_heads // kv_local
    span_total = slot_count * inst_size
    longest = span_total // 2
    anywhere = pl.BlockSpec(memory_space=pl.ANY)
    by_slot = pl.BlockSpec((1, span_len, row_width), lambda i, *_: (i, 0, 0))
    rows = per_head * span_len
    state_shape = (slot_count, kv_local, rows, head_dim)
    state_spec = pl.BlockSpec((1,) + state_shape[1:], lambda i, *_: (i, 0, 0, 0))
    work = slot_count * 4 * local_heads * span_len * span_len

    def attend(covers, parts, sources, state=(), hops=None):
        first_call, last_call = not state, hops is not None
        hops = hops or []
        own_sources = lax.dynamic_index_in_dim(
            jnp.asarray(sources, jnp.int32), inst_index, 1, False
        )
        numbers = jnp.concatenate([
            prompt_spans, prompt_tail, decode_owner, span_plan,
            jnp.stack([inst_index, tp_index]).astype(jnp.int32), own_sources,
        ])
        kernel = functools.partial(
            attend_kernel,
            covers=covers,
            hops=[name for name, _ in hops],
            parts=[name for name, _ in parts],
            first_call=first_call,
            last_call=last_call,
            inst_size=inst_size,
            tp_size=tp_size,
            kv_local=kv_local,
            per_head=per_head,
            head_dim=head_dim,
            span_len=span_len,
            slot_count=slot_count,
            longest=longest,
            prompt_count=prompt_spans.shape[0],
        )
        scratch = [
            pltpu.SMEM((span_total,), jnp.int32),
            pltpu.SMEM((span_total,), jnp.int32),
            pltpu.VMEM((span_total, kv_local, span_len, width), jnp.bfloat16),
            pltpu.VMEM((kv_local, rows, STEP * span_len), jnp.float32),
            pltpu.VMEM((kv_local, rows, STEP * span_len), jnp.bfloat16),
            pltpu.VMEM((kv_local, rows, 2 * head_dim), jnp.float32),
            pltpu.VMEM((kv_local, rows, head_dim), jnp.float32),
            pltpu.SemaphoreType.DMA((len(parts), max(len(x[0][0]) for x in parts))),
        ]
        if last_call:
            scratch += [
                pltpu.VMEM((kv_heads, slice_len, width), jnp.bfloat16),
                pltpu.SemaphoreType.DMA((longest,)),
            ]
            out_specs = [by_slot, anywhere]
            out_shape = [
                jax.ShapeDtypeStruct(queries.shape, jnp.bfloat16),
                jax.ShapeDtypeStruct((longest, kv_heads, slice_len, width), jnp.bfloat16),
            ]
        else:
            out_specs = [state_spec] * 2 + [pl.BlockSpec((8, 128), lambda i, *_: (0, 0))]
            out_shape = [jax.ShapeDtypeStruct(state_shape, jnp.float32)] * 2
            out_shape += [jax.ShapeDtypeStruct((8, 128), jnp.float32)]
        return pl.pallas_call(
            kernel,
            grid_spec=pltpu.PrefetchScalarGridSpec(
                num_scalar_prefetch=1,
                grid=(slot_count,),
                in_specs=[by_slot] + [state_spec] * len(state)
                + [anywhere] * (len(hops) + len(parts)),
                out_specs=out_specs,
                scratch_shapes=scratch,
            ),
            out_shape=out_shape,
            cost_estimate=pl.CostEstimate(
                flops=4 * work * head_dim, bytes_accessed=8 << 20, transcendentals=work
            ),
            compiler_params=pltpu.CompilerParams(vmem_limit_bytes=40 << 20),
        )(
            numbers, queries, *state, *[x for _, x in hops], *[x for _, x in parts],
        )

    state, left, hops = move_pages(kv_new, kv_local, attend)
    return tuple(attend(*left, state, hops))


def solution(mesh):
    placed = (
        P(("groups", "inst"), None, "tp"),
        P(("groups", "inst"), None, "tp", None),
        P("groups"),
        P("groups"),
        P("groups"),
        P("groups"),
    )
    return jax.shard_map(
        body,
        mesh=mesh,
        in_specs=placed,
        out_specs=(P(("groups", "inst"), None, "tp"), P(("groups", "inst"), None, "tp", None)),
        check_vma=False,
    )
```

```python
import functools
import math

import jax
import jax.numpy as jnp
from jax import lax
from jax.experimental import pallas as pl
from jax.experimental.pallas import tpu as pltpu
from jax.sharding import PartitionSpec as P

HEADS = 64
KVH = 8
LOG2E = 1.4426950408889634
STEP = 4
TOGETHER = 4


class Part:
    def __init__(self, ref, start):
        self.ref, self.start = ref, start

    def __getitem__(self, at):
        return self.ref[self.start + at]


def attend_kernel(
    numbers_ref, *refs,
    covers, hops, parts, later, first_call, last_call,
    inst_size, tp_size, kv_local, per_head, head_dim, span_len, slot_count, longest, prompt_count,
):
    refs = list(refs)

    def take(count):
        taken = refs[:count]
        del refs[:count]
        return taken

    (q_ref,) = take(1)
    mixed_ref, total_ref = (None, None) if first_call else take(2)
    hop_refs = take(len(hops))
    part_refs = take(len(parts))
    take(later)
    if last_call:
        out_ref, cache_ref = take(2)
    else:
        out_ref, next_total_ref, mark_ref = take(3)
        next_total_ref[...] = jnp.zeros_like(next_total_ref)
        mark_ref[...] = jnp.zeros_like(mark_ref)
    place_ref, list_ref, kv_ref, s_ref, p_ref, acc_ref, max_ref, part_sems = take(8)
    if last_call:
        zero_ref, page_sems = take(2)
    step = pl.program_id(0)
    span_total = slot_count * inst_size
    spans_ref = Part(numbers_ref, 0)
    tail_ref = Part(numbers_ref, prompt_count)
    owner_ref = Part(numbers_ref, 2 * prompt_count)
    plan_ref = Part(numbers_ref, 3 * prompt_count)
    place_at_ref = Part(numbers_ref, 3 * prompt_count + span_total)
    inst = place_at_ref[0]
    tp = place_at_ref[1]
    slice_len = span_len // tp_size
    scale = LOG2E / math.sqrt(head_dim)

    def part_copies(act):
        for n, (pieces, j) in enumerate(parts):
            at = pl.ds(pl.multiple_of((tp ^ j) * slice_len, slice_len), slice_len)
            begin = 0
            for m, (hop, first_slot, size) in enumerate(pieces):
                slots = pl.ds(place_at_ref[2 + hop] * slot_count + first_slot, size)
                act(pltpu.make_async_copy(
                    part_refs[n].at[begin:begin + size], kv_ref.at[slots, :, at],
                    part_sems.at[n, m],
                ))
                begin += size

    def cache_copies(act):
        first = jnp.int32(0)
        count = jnp.int32(0)
        start = jnp.int32(0)
        for p in range(prompt_count):
            hit = owner_ref[p] == inst
            first = jnp.where(hit, start, first)
            count = jnp.where(hit, spans_ref[p], count)
            start = start + spans_ref[p]

        def row(r, unused):
            page = place_ref[jnp.minimum(first + r, span_total - 1)]
            for n, (hop, first_slot, size) in enumerate(hops):
                source = place_at_ref[2 + hop]
                slot = page - source * slot_count - first_slot
                here = (source >= 0) & (slot >= 0) & (slot < size)

                @pl.when((r < count) & here)
                def _():
                    act(pltpu.make_async_copy(
                        hop_refs[n].at[slot], cache_ref.at[r], page_sems.at[r]
                    ))

            @pl.when(r >= count)
            def _():
                act(pltpu.make_async_copy(zero_ref, cache_ref.at[r], page_sems.at[r]))

            return unused

        lax.fori_loop(0, longest, row, 0)

    @pl.when(step == 0)
    def _():
        part_copies(lambda copy: copy.start())

        def put(g, unused):
            place_ref[plan_ref[g]] = g
            return unused

        lax.fori_loop(0, span_total, put, 0)
        if last_call:
            zero_ref[...] = jnp.zeros_like(zero_ref)
            cache_copies(lambda copy: copy.start())
        part_copies(lambda copy: copy.wait())

    own = inst * slot_count + step
    span = plan_ref[own]
    first = jnp.int32(0)
    end = jnp.int32(0)
    length = jnp.int32(0)
    for p in range(prompt_count):
        start = end
        end = end + spans_ref[p]
        inside = (span >= start) & (span < end)
        first = jnp.where(inside, start, first)
        length = jnp.where(inside, (spans_ref[p] - 1) * span_len + tail_ref[p], length)
    live_rows = length - (span - first) * span_len

    def look(k, count):
        page = place_ref[k]
        source = page // slot_count
        covered = jnp.bool_(False)
        for hop in covers:
            covered = covered | (place_at_ref[2 + hop] == source)
        list_ref[count] = page
        return count + covered.astype(jnp.int32)

    count = lax.fori_loop(first, span, look, jnp.int32(0))

    ones = jnp.ones((span_len, head_dim), jnp.bfloat16)
    row_ids = lax.broadcasted_iota(jnp.int32, (span_len, span_len), 0)
    col_ids = lax.broadcasted_iota(jnp.int32, (span_len, span_len), 1)
    causal = row_ids >= col_ids
    lane_ids = lax.broadcasted_iota(jnp.int32, (span_len, head_dim), 1)
    heads = kv_local * per_head
    together = math.gcd(per_head, TOGETHER)

    def lanes_of(head):
        return pl.ds(pl.multiple_of(head * head_dim, head_dim), head_dim)

    def rows_of(h):
        return slice(h * span_len, (h + 1) * span_len)

    def attend(pages, since):
        wide = len(pages) * span_len

        def some_heads(c, unused):
            head0 = c * together
            g = head0 // per_head
            keys = jnp.concatenate([kv_ref[page, g, :, :head_dim] for page in pages], axis=0)
            values = jnp.concatenate(
                [
                    jnp.concatenate([kv_ref[page, g, :, head_dim:], ones], axis=1)
                    for page in pages
                ],
                axis=0,
            )
            q = jnp.concatenate(
                [q_ref[0, :, lanes_of(head0 + h)] for h in range(together)], axis=0
            )
            s_ref[:, :wide] = lax.dot_general(
                q, keys, (((1,), (1,)), ((), ())), preferred_element_type=jnp.float32
            )
            rescales = []
            for h in range(together):
                head = head0 + h
                s = s_ref[rows_of(h), :wide] * scale
                if since == "start":
                    own_part = jnp.where(causal, s[:, wide - span_len:], -1e30)
                    if len(pages) > 1:
                        s = jnp.concatenate([s[:, :wide - span_len], own_part], axis=1)
                    else:
                        s = own_part
                top = jnp.max(s, axis=1, keepdims=True)
                if since == "start":
                    top = jnp.broadcast_to(top, (span_len, head_dim))
                else:
                    if since == "given":
                        old = jnp.broadcast_to(
                            jnp.sum(
                                jnp.where(lane_ids == head, total_ref[0], 0.0),
                                axis=1, keepdims=True,
                            ),
                            (span_len, head_dim),
                        )
                    else:
                        old = max_ref[head]
                    top = jnp.maximum(old, top)
                    rescales.append(jnp.exp2(old - top))
                max_ref[head] = top
                p_ref[rows_of(h), :wide] = jnp.exp2(
                    s - jnp.concatenate([top] * len(pages), axis=1)
                ).astype(jnp.bfloat16)
            mixed = jnp.dot(p_ref[:, :wide], values, preferred_element_type=jnp.float32)
            for h in range(together):
                head = head0 + h
                new = mixed[rows_of(h)]
                if since == "given":
                    given = mixed_ref[0, :, lanes_of(head)].astype(jnp.float32)
                    new = new + jnp.concatenate([given * rescales[h], rescales[h]], axis=1)
                elif since == "here":
                    new = new + acc_ref[head] * jnp.concatenate([rescales[h]] * 2, axis=1)
                acc_ref[head] = new
            return unused

        lax.fori_loop(0, heads // together, some_heads, 0)

    def rest(begin):
        def block(j, unused):
            at = begin + STEP * j
            attend([list_ref[at + n] for n in range(STEP)], "here")
            return unused

        lax.fori_loop(0, (count - begin) // STEP, block, 0)

    live = lax.broadcasted_iota(jnp.int32, (span_len, head_dim), 0) < live_rows

    def finish():
        def one_head(head, unused):
            total = acc_ref[head, :, head_dim:]
            mixed = acc_ref[head, :, :head_dim] / total
            if last_call:
                mixed = jnp.where(live, mixed, 0.0)
            else:
                next_total_ref[0] = jnp.where(
                    lane_ids == head, max_ref[head] + jnp.log(total) * LOG2E, next_total_ref[0]
                )
            out_ref[0, :, lanes_of(head)] = mixed.astype(jnp.bfloat16)
            return unused

        lax.fori_loop(0, heads, one_head, 0)

    if first_call:
        over = lax.rem(count, STEP)
        for n in range(STEP):
            @pl.when(over == n)
            def _():
                attend([list_ref[m] for m in range(n)] + [own], "start")

        rest(over)
        finish()
    else:
        over = lax.rem(count + STEP - 1, STEP) + 1

        @pl.when(count == 0)
        def _():
            def one_head(head, unused):
                given = mixed_ref[0, :, lanes_of(head)]
                out_ref[0, :, lanes_of(head)] = jnp.where(live, given, jnp.zeros_like(given))
                return unused

            lax.fori_loop(0, heads, one_head, 0)

        @pl.when(count > 0)
        def _():
            for n in range(1, STEP + 1):
                @pl.when(over == n)
                def _():
                    attend([list_ref[m] for m in range(n)], "given")

            rest(over)
            finish()

    if last_call:
        @pl.when(step == slot_count - 1)
        def _():
            cache_copies(lambda copy: copy.wait())


def after(values, earlier):
    return lax.optimization_barrier((list(values), list(earlier)))[0]


def move_pages(kv_new, kv_local, attend):
    inst_size = lax.axis_size("inst")
    tp_size = lax.axis_size("tp")
    inst = lax.axis_index("inst")
    tp = lax.axis_index("tp")
    slot_count, kv_heads = kv_new.shape[:2]
    sources = [list(range(inst_size))]
    hops = [((0, 0, slot_count), kv_new)]
    parts = []

    def along(x, pairs):
        return lax.ppermute(x, "inst", pairs)

    def exchange(*pieces, zero=0):
        names = [name for name, _ in pieces]
        found = []
        for j in range(tp_size):
            head = ((tp ^ j) * kv_heads) // tp_size + zero
            sent = [lax.dynamic_slice_in_dim(x, head, kv_local, 1) for _, x in pieces]
            sent = jnp.concatenate(sent, axis=0) if len(sent) > 1 else sent[0]
            if j:
                sent = lax.ppermute(sent, "tp", [(t, t ^ j) for t in range(tp_size)])
            found.append(((names, j), sent))
        parts.extend(found)
        return [x for _, x in found]

    if inst_size != 4:
        exchange(hops[0])
        for s in range(1, inst_size):
            sources.append([(i - s) % inst_size for i in range(inst_size)])
            pairs = [(i, (i + s) % inst_size) for i in range(inst_size)]
            hops.append(((s, 0, slot_count), along(kv_new, pairs)))
            exchange(hops[-1])
        return [], (list(range(inst_size)), parts, sources), hops

    middle = (inst == 1) | (inst == 2)
    sources += [[1, 0, 3, 2], [-1, 2, 1, -1], [-1, 3, 0, -1], [2, -1, -1, 1], [3, -1, -1, 0]]
    second, third = 6, 7
    sources += [[2, 2, 1, 1], [3, 3, 0, 0]]
    whole = slot_count
    half = slot_count // 2
    outer = along(kv_new, [(0, 1), (1, 0), (2, 3), (3, 2)])
    inner = along(kv_new, [(1, 2), (2, 1)])
    waiting = exchange(hops[0])
    outer_on, inner_on = after([outer, inner], waiting)
    crossed = along(outer_on, [(1, 2), (2, 1)])
    inner_ends = along(inner_on, [(1, 0), (2, 3)])
    waiting = exchange(((1, 0, whole), outer_on))
    crossed_on = after([crossed], waiting)[0]
    crossed_half = lax.optimization_barrier([crossed_on[:half], crossed_on[half:]])
    crossed_ends = [along(x, [(1, 0), (2, 3)]) for x in crossed_half]
    early = len(parts)
    two = jnp.where(middle, inner, inner_ends)
    waiting = exchange(((second, 0, whole), two))
    *state, mark = attend([0, 1], parts[:early], sources, later=[waiting[0], *crossed_half])
    for n in range(2):
        three = jnp.where(middle, crossed_half[n], crossed_ends[n])
        three = after([three], waiting)[0]
        waiting = exchange(((third, n * half, half), three), zero=mark[0, 0])
        hops.append(((5, n * half, half), crossed_ends[n]))
    for hop, x in enumerate((outer, inner, crossed, inner_ends), 1):
        hops.append(((hop, 0, whole), x))
    return state, ([second, third], parts[early:], sources), hops


def body(queries, kv_new, prompt_spans, prompt_tail, span_plan, decode_owner):
    tp_size = lax.axis_size("tp")
    inst_size = lax.axis_size("inst")
    tp_index = lax.axis_index("tp")
    inst_index = lax.axis_index("inst")
    slot_count, span_len, row_width = queries.shape
    kv_heads, slice_len, width = kv_new.shape[1:]
    head_dim = width // 2
    local_heads = row_width // head_dim
    kv_local = max(1, kv_heads // tp_size)
    per_head = local_heads // kv_local
    span_total = slot_count * inst_size
    longest = span_total // 2
    anywhere = pl.BlockSpec(memory_space=pl.ANY)
    by_slot = pl.BlockSpec((1, span_len, row_width), lambda i, *_: (i, 0, 0))
    rows = math.gcd(per_head, TOGETHER) * span_len
    total_spec = pl.BlockSpec((1, span_len, head_dim), lambda i, *_: (i, 0, 0))
    state_specs = [by_slot, total_spec]
    work = slot_count * 4 * local_heads * span_len * span_len

    def attend(covers, parts, sources, state=(), hops=None, later=()):
        first_call, last_call = not state, hops is not None
        hops = hops or []
        own_sources = lax.dynamic_index_in_dim(
            jnp.asarray(sources, jnp.int32), inst_index, 1, False
        )
        numbers = jnp.concatenate([
            prompt_spans, prompt_tail, decode_owner, span_plan,
            jnp.stack([inst_index, tp_index]).astype(jnp.int32), own_sources,
        ])
        kernel = functools.partial(
            attend_kernel,
            covers=covers,
            hops=[name for name, _ in hops],
            parts=[name for name, _ in parts],
            later=len(later),
            first_call=first_call,
            last_call=last_call,
            inst_size=inst_size,
            tp_size=tp_size,
            kv_local=kv_local,
            per_head=per_head,
            head_dim=head_dim,
            span_len=span_len,
            slot_count=slot_count,
            longest=longest,
            prompt_count=prompt_spans.shape[0],
        )
        scratch = [
            pltpu.SMEM((span_total,), jnp.int32),
            pltpu.SMEM((span_total,), jnp.int32),
            pltpu.VMEM((span_total, kv_local, span_len, width), jnp.bfloat16),
            pltpu.VMEM((rows, STEP * span_len), jnp.float32),
            pltpu.VMEM((rows, STEP * span_len), jnp.bfloat16),
            pltpu.VMEM((local_heads, span_len, 2 * head_dim), jnp.float32),
            pltpu.VMEM((local_heads, span_len, head_dim), jnp.float32),
            pltpu.SemaphoreType.DMA((len(parts), max(len(x[0][0]) for x in parts))),
        ]
        if last_call:
            scratch += [
                pltpu.VMEM((kv_heads, slice_len, width), jnp.bfloat16),
                pltpu.SemaphoreType.DMA((longest,)),
            ]
            out_specs = [by_slot, anywhere]
            out_shape = [
                jax.ShapeDtypeStruct(queries.shape, jnp.bfloat16),
                jax.ShapeDtypeStruct((longest, kv_heads, slice_len, width), jnp.bfloat16),
            ]
        else:
            out_specs = state_specs + [pl.BlockSpec((8, 128), lambda i, *_: (0, 0))]
            out_shape = [
                jax.ShapeDtypeStruct(queries.shape, jnp.bfloat16),
                jax.ShapeDtypeStruct((slot_count, span_len, head_dim), jnp.float32),
                jax.ShapeDtypeStruct((8, 128), jnp.int32),
            ]
        return pl.pallas_call(
            kernel,
            grid_spec=pltpu.PrefetchScalarGridSpec(
                num_scalar_prefetch=1,
                grid=(slot_count,),
                in_specs=[by_slot] + (state_specs if state else [])
                + [anywhere] * (len(hops) + len(parts) + len(later)),
                out_specs=out_specs,
                scratch_shapes=scratch,
            ),
            out_shape=out_shape,
            cost_estimate=pl.CostEstimate(
                flops=4 * work * head_dim, bytes_accessed=8 << 20, transcendentals=work
            ),
            compiler_params=pltpu.CompilerParams(vmem_limit_bytes=40 << 20),
        )(
            numbers, queries, *state, *[x for _, x in hops], *[x for _, x in parts],
            *later,
        )

    state, left, hops = move_pages(kv_new, kv_local, attend)
    return tuple(attend(*left, state, hops))


def solution(mesh):
    placed = (
        P(("groups", "inst"), None, "tp"),
        P(("groups", "inst"), None, "tp", None),
        P("groups"),
        P("groups"),
        P("groups"),
        P("groups"),
    )
    return jax.shard_map(
        body,
        mesh=mesh,
        in_specs=placed,
        out_specs=(P(("groups", "inst"), None, "tp"), P(("groups", "inst"), None, "tp", None)),
        check_vma=False,
    )
```

```python
import functools
import math

import jax
import jax.numpy as jnp
from jax import lax
from jax.experimental import pallas as pl
from jax.experimental.pallas import tpu as pltpu
from jax.sharding import PartitionSpec as P

HEADS = 64
KVH = 8
LOG2E = 1.4426950408889634
STEP = 4
VMEM_BYTES = 24 << 20


class Part:
    def __init__(self, ref, start):
        self.ref, self.start = ref, start

    def __getitem__(self, at):
        return self.ref[self.start + at]


def attend_kernel(
    numbers_ref, *refs,
    covers, hops, parts, later, first_call, last_call,
    inst_size, tp_size, kv_local, per_head, head_dim, span_len, slot_count, longest, prompt_count,
):
    refs = list(refs)

    def take(count):
        taken = refs[:count]
        del refs[:count]
        return taken

    (q_ref,) = take(1)
    mixed_ref, total_ref = (None, None) if first_call else take(2)
    hop_refs = take(len(hops))
    part_refs = take(len(parts))
    take(later)
    if last_call:
        out_ref, cache_ref = take(2)
    else:
        out_ref, next_total_ref = take(2)
    place_ref, list_ref, kv_ref, s_ref, p_ref, acc_ref, max_ref, part_sems = take(8)
    if last_call:
        zero_ref, page_sems = take(2)
    step = pl.program_id(0)
    span_total = slot_count * inst_size
    spans_ref = Part(numbers_ref, 0)
    tail_ref = Part(numbers_ref, prompt_count)
    owner_ref = Part(numbers_ref, 2 * prompt_count)
    plan_ref = Part(numbers_ref, 3 * prompt_count)
    place_at_ref = Part(numbers_ref, 3 * prompt_count + span_total)
    inst = place_at_ref[0]
    tp = place_at_ref[1]
    slice_len = span_len // tp_size
    most = min(longest, len(covers) * slot_count)
    scale = LOG2E / math.sqrt(head_dim)

    def part_copies(act):
        for n, (pieces, j) in enumerate(parts):
            at = pl.ds(pl.multiple_of((tp ^ j) * slice_len, slice_len), slice_len)
            begin = 0
            for m, (hop, first_slot, size) in enumerate(pieces):
                slots = pl.ds(place_at_ref[2 + hop] * slot_count + first_slot, size)
                act(pltpu.make_async_copy(
                    part_refs[n].at[begin:begin + size], kv_ref.at[slots, :, at],
                    part_sems.at[n, m],
                ))
                begin += size

    def cache_copies(act):
        first = jnp.int32(0)
        count = jnp.int32(0)
        start = jnp.int32(0)
        for p in range(prompt_count):
            hit = owner_ref[p] == inst
            first = jnp.where(hit, start, first)
            count = jnp.where(hit, spans_ref[p], count)
            start = start + spans_ref[p]

        def row(r, unused):
            page = place_ref[jnp.minimum(first + r, span_total - 1)]
            for n, (hop, first_slot, size) in enumerate(hops):
                source = place_at_ref[2 + hop]
                slot = page - source * slot_count - first_slot
                here = (source >= 0) & (slot >= 0) & (slot < size)

                @pl.when((r < count) & here)
                def _():
                    act(pltpu.make_async_copy(
                        hop_refs[n].at[slot], cache_ref.at[r], page_sems.at[r]
                    ))

            @pl.when(r >= count)
            def _():
                act(pltpu.make_async_copy(zero_ref, cache_ref.at[r], page_sems.at[r]))

            return unused

        lax.fori_loop(0, longest, row, 0)

    @pl.when(step == 0)
    def _():
        part_copies(lambda copy: copy.start())

        def put(g, unused):
            place_ref[plan_ref[g]] = g
            return unused

        lax.fori_loop(0, span_total, put, 0)
        if last_call:
            zero_ref[...] = jnp.zeros_like(zero_ref)
            cache_copies(lambda copy: copy.start())
        part_copies(lambda copy: copy.wait())

    own = inst * slot_count + step
    span = plan_ref[own]
    first = jnp.int32(0)
    end = jnp.int32(0)
    length = jnp.int32(0)
    for p in range(prompt_count):
        start = end
        end = end + spans_ref[p]
        inside = (span >= start) & (span < end)
        first = jnp.where(inside, start, first)
        length = jnp.where(inside, (spans_ref[p] - 1) * span_len + tail_ref[p], length)
    live_rows = length - (span - first) * span_len

    def look(k, count):
        page = place_ref[k]
        source = page // slot_count
        covered = jnp.bool_(False)
        for hop in covers:
            covered = covered | (place_at_ref[2 + hop] == source)
        list_ref[count] = page
        return count + covered.astype(jnp.int32)

    count = lax.fori_loop(first, span, look, jnp.int32(0))

    ones = jnp.ones((span_len, head_dim), jnp.bfloat16)
    row_ids = lax.broadcasted_iota(jnp.int32, (span_len, span_len), 0)
    col_ids = lax.broadcasted_iota(jnp.int32, (span_len, span_len), 1)
    causal = row_ids >= col_ids
    lane_ids = lax.broadcasted_iota(jnp.int32, (span_len, head_dim), 1)
    def lanes_of(head):
        return slice(head * head_dim, (head + 1) * head_dim)

    def rows_of(h):
        return slice(h * span_len, (h + 1) * span_len)

    def attend(pages, since):
        wide = len(pages) * span_len
        for g in range(kv_local):
            keys = jnp.concatenate([kv_ref[page, g, :, :head_dim] for page in pages], axis=0)
            q = jnp.concatenate(
                [q_ref[0, :, lanes_of(g * per_head + h)] for h in range(per_head)], axis=0
            )
            s_ref[g, :, :wide] = lax.dot_general(
                q, keys, (((1,), (1,)), ((), ())), preferred_element_type=jnp.float32
            )
        for g in range(kv_local):
            rescales = []
            for h in range(per_head):
                head = g * per_head + h
                s = s_ref[g, rows_of(h), :wide] * scale
                if since == "start":
                    own_part = jnp.where(causal, s[:, wide - span_len:], -1e30)
                    if len(pages) > 1:
                        s = jnp.concatenate([s[:, :wide - span_len], own_part], axis=1)
                    else:
                        s = own_part
                top = jnp.max(s, axis=1, keepdims=True)
                if since == "start":
                    top = jnp.broadcast_to(top, (span_len, head_dim))
                else:
                    if since == "given":
                        old = jnp.broadcast_to(
                            total_ref[0, :, head:head + 1], (span_len, head_dim)
                        )
                    else:
                        old = max_ref[head]
                    top = jnp.maximum(old, top)
                    rescales.append(jnp.exp2(old - top))
                max_ref[head] = top
                p_ref[g, rows_of(h), :wide] = jnp.exp2(
                    s - jnp.concatenate([top] * len(pages), axis=1)
                ).astype(jnp.bfloat16)
            values = jnp.concatenate(
                [
                    jnp.concatenate([kv_ref[page, g, :, head_dim:], ones], axis=1)
                    for page in pages
                ],
                axis=0,
            )
            mixed = jnp.dot(p_ref[g, :, :wide], values, preferred_element_type=jnp.float32)
            for h in range(per_head):
                head = g * per_head + h
                new = mixed[rows_of(h)]
                if since == "given":
                    given = mixed_ref[0, :, lanes_of(head)].astype(jnp.float32)
                    new = new + jnp.concatenate([given * rescales[h], rescales[h]], axis=1)
                elif since == "here":
                    new = new + acc_ref[head] * jnp.concatenate([rescales[h]] * 2, axis=1)
                acc_ref[head] = new

    def rest(begin):
        if most <= STEP:
            return

        def block(j, unused):
            at = begin + STEP * j
            attend([list_ref[at + n] for n in range(STEP)], "here")
            return unused

        lax.fori_loop(0, (count - begin) // STEP, block, 0)

    live = lax.broadcasted_iota(jnp.int32, (span_len, head_dim), 0) < live_rows

    def finish():
        tops = jnp.zeros((span_len, head_dim), jnp.float32)
        totals = jnp.ones((span_len, head_dim), jnp.float32)
        for head in range(kv_local * per_head):
            total = acc_ref[head, :, head_dim:]
            mixed = acc_ref[head, :, :head_dim] / total
            if last_call:
                mixed = jnp.where(live, mixed, 0.0)
            else:
                tops = jnp.where(lane_ids == head, max_ref[head], tops)
                totals = jnp.where(lane_ids == head, total, totals)
            out_ref[0, :, lanes_of(head)] = mixed.astype(jnp.bfloat16)
        if not last_call:
            next_total_ref[0] = tops + jnp.log(totals) * LOG2E

    if first_call:
        over = lax.rem(count, STEP)
        for n in range(STEP):
            @pl.when(over == n)
            def _():
                attend([list_ref[m] for m in range(n)] + [own], "start")

        rest(over)
        finish()
    else:
        over = lax.rem(count + STEP - 1, STEP) + 1

        @pl.when(count == 0)
        def _():
            if last_call:
                for head in range(kv_local * per_head):
                    given = mixed_ref[0, :, lanes_of(head)]
                    out_ref[0, :, lanes_of(head)] = jnp.where(live, given, jnp.zeros_like(given))
            else:
                out_ref[...] = mixed_ref[...]
                next_total_ref[...] = total_ref[...]

        @pl.when(count > 0)
        def _():
            for n in range(1, STEP + 1):
                @pl.when(over == n)
                def _():
                    attend([list_ref[m] for m in range(n)], "given")

            rest(over)
            finish()

    if last_call:
        @pl.when(step == slot_count - 1)
        def _():
            cache_copies(lambda copy: copy.wait())


def after(values, earlier):
    return lax.optimization_barrier((list(values), list(earlier)))[0]


def move_pages(kv_new, kv_local, attend):
    inst_size = lax.axis_size("inst")
    tp_size = lax.axis_size("tp")
    inst = lax.axis_index("inst")
    tp = lax.axis_index("tp")
    slot_count, kv_heads = kv_new.shape[:2]
    sources = [list(range(inst_size))]
    hops = [((0, 0, slot_count), kv_new)]
    parts = []

    def along(x, pairs):
        return lax.ppermute(x, "inst", pairs)

    def exchange(*pieces):
        names = [name for name, _ in pieces]
        found = []
        for j in range(tp_size):
            head = ((tp ^ j) * kv_heads) // tp_size
            sent = [lax.dynamic_slice_in_dim(x, head, kv_local, 1) for _, x in pieces]
            sent = jnp.concatenate(sent, axis=0) if len(sent) > 1 else sent[0]
            if j:
                sent = lax.ppermute(sent, "tp", [(t, t ^ j) for t in range(tp_size)])
            found.append(((names, j), sent))
        parts.extend(found)
        return [x for _, x in found]

    if inst_size != 4:
        exchange(hops[0])
        for s in range(1, inst_size):
            sources.append([(i - s) % inst_size for i in range(inst_size)])
            pairs = [(i, (i + s) % inst_size) for i in range(inst_size)]
            hops.append(((s, 0, slot_count), along(kv_new, pairs)))
            exchange(hops[-1])
        return [], (list(range(inst_size)), parts, sources), hops

    middle = (inst == 1) | (inst == 2)
    sources += [[1, 0, 3, 2], [-1, 2, 1, -1], [-1, 3, 0, -1], [2, -1, -1, 1], [3, -1, -1, 0]]
    second, third = 6, 7
    sources += [[2, 2, 1, 1], [3, 3, 0, 0]]
    whole = slot_count
    half = slot_count // 2
    outer = along(kv_new, [(0, 1), (1, 0), (2, 3), (3, 2)])
    inner = along(kv_new, [(1, 2), (2, 1)])
    waiting = exchange(hops[0])
    outer_on, inner_on = after([outer, inner], waiting)
    crossed = along(outer_on, [(1, 2), (2, 1)])
    inner_ends = along(inner_on, [(1, 0), (2, 3)])
    own_parts = parts[:]
    first_parts = exchange(((1, 0, whole), outer_on))
    state = attend([0], own_parts, sources, later=first_parts[:1])
    state = attend([1], parts[tp_size:], sources, state=state)
    crossed_on = after([crossed], first_parts)[0]
    crossed_half = lax.optimization_barrier([crossed_on[:half], crossed_on[half:]])
    crossed_ends = [along(x, [(1, 0), (2, 3)]) for x in crossed_half]
    two = jnp.where(middle, inner, inner_ends)
    waiting = exchange(((second, 0, whole), two))
    second_parts = parts[2 * tp_size:]
    third_parts = len(parts)
    threes = [jnp.where(middle, crossed_half[n], crossed_ends[n]) for n in range(2)]
    waiting = exchange(((third, 0, half), after(threes[:1], waiting)[0]))
    state = attend([second], second_parts, sources, state=state, later=waiting[:1])
    exchange(((third, half, half), after(threes[1:], waiting)[0]))
    for n in range(2):
        hops.append(((5, n * half, half), crossed_ends[n]))
    for hop, x in enumerate((outer, inner, crossed, inner_ends), 1):
        hops.append(((hop, 0, whole), x))
    return state, ([third], parts[third_parts:], sources), hops


def body(queries, kv_new, prompt_spans, prompt_tail, span_plan, decode_owner):
    tp_size = lax.axis_size("tp")
    inst_size = lax.axis_size("inst")
    tp_index = lax.axis_index("tp")
    inst_index = lax.axis_index("inst")
    slot_count, span_len, row_width = queries.shape
    kv_heads, slice_len, width = kv_new.shape[1:]
    head_dim = width // 2
    local_heads = row_width // head_dim
    kv_local = max(1, kv_heads // tp_size)
    per_head = local_heads // kv_local
    span_total = slot_count * inst_size
    longest = span_total // 2
    anywhere = pl.BlockSpec(memory_space=pl.ANY)
    by_slot = pl.BlockSpec((1, span_len, row_width), lambda i, *_: (i, 0, 0))
    rows = per_head * span_len
    total_spec = pl.BlockSpec((1, span_len, head_dim), lambda i, *_: (i, 0, 0))
    state_specs = [by_slot, total_spec]
    work = slot_count * 4 * local_heads * span_len * span_len

    def attend(covers, parts, sources, state=(), hops=None, later=()):
        first_call, last_call = not state, hops is not None
        hops = hops or []
        own_sources = lax.dynamic_index_in_dim(
            jnp.asarray(sources, jnp.int32), inst_index, 1, False
        )
        numbers = jnp.concatenate([
            prompt_spans, prompt_tail, decode_owner, span_plan,
            jnp.stack([inst_index, tp_index]).astype(jnp.int32), own_sources,
        ])
        kernel = functools.partial(
            attend_kernel,
            covers=covers,
            hops=[name for name, _ in hops],
            parts=[name for name, _ in parts],
            later=len(later),
            first_call=first_call,
            last_call=last_call,
            inst_size=inst_size,
            tp_size=tp_size,
            kv_local=kv_local,
            per_head=per_head,
            head_dim=head_dim,
            span_len=span_len,
            slot_count=slot_count,
            longest=longest,
            prompt_count=prompt_spans.shape[0],
        )
        scratch = [
            pltpu.SMEM((span_total,), jnp.int32),
            pltpu.SMEM((span_total,), jnp.int32),
            pltpu.VMEM((span_total, kv_local, span_len, width), jnp.bfloat16),
            pltpu.VMEM((kv_local, rows, STEP * span_len), jnp.float32),
            pltpu.VMEM((kv_local, rows, STEP * span_len), jnp.bfloat16),
            pltpu.VMEM((local_heads, span_len, 2 * head_dim), jnp.float32),
            pltpu.VMEM((local_heads, span_len, head_dim), jnp.float32),
            pltpu.SemaphoreType.DMA((len(parts), max(len(x[0][0]) for x in parts))),
        ]
        if last_call:
            scratch += [
                pltpu.VMEM((kv_heads, slice_len, width), jnp.bfloat16),
                pltpu.SemaphoreType.DMA((longest,)),
            ]
            out_specs = [by_slot, anywhere]
            out_shape = [
                jax.ShapeDtypeStruct(queries.shape, jnp.bfloat16),
                jax.ShapeDtypeStruct((longest, kv_heads, slice_len, width), jnp.bfloat16),
            ]
        else:
            out_specs = state_specs
            out_shape = [
                jax.ShapeDtypeStruct(queries.shape, jnp.bfloat16),
                jax.ShapeDtypeStruct((slot_count, span_len, head_dim), jnp.float32),
            ]
        return pl.pallas_call(
            kernel,
            grid_spec=pltpu.PrefetchScalarGridSpec(
                num_scalar_prefetch=1,
                grid=(slot_count,),
                in_specs=[by_slot] + (state_specs if state else [])
                + [anywhere] * (len(hops) + len(parts) + len(later)),
                out_specs=out_specs,
                scratch_shapes=scratch,
            ),
            out_shape=out_shape,
            cost_estimate=pl.CostEstimate(
                flops=4 * work * head_dim, bytes_accessed=8 << 20, transcendentals=work
            ),
            compiler_params=pltpu.CompilerParams(vmem_limit_bytes=VMEM_BYTES),
        )(
            numbers, queries, *state, *[x for _, x in hops], *[x for _, x in parts],
            *later,
        )

    state, left, hops = move_pages(kv_new, kv_local, attend)
    return tuple(attend(*left, state, hops))


def solution(mesh):
    placed = (
        P(("groups", "inst"), None, "tp"),
        P(("groups", "inst"), None, "tp", None),
        P("groups"),
        P("groups"),
        P("groups"),
        P("groups"),
    )
    return jax.shard_map(
        body,
        mesh=mesh,
        in_specs=placed,
        out_specs=(P(("groups", "inst"), None, "tp"), P(("groups", "inst"), None, "tp", None)),
        check_vma=False,
    )
```

```python
import functools
import math

import jax
import jax.numpy as jnp
from jax import lax
from jax.experimental import pallas as pl
from jax.experimental.pallas import tpu as pltpu
from jax.sharding import PartitionSpec as P

HEADS = 64
KVH = 8
LOG2E = 1.4426950408889634
STEP = 8
VMEM_BYTES = 24 << 20


class Part:
    def __init__(self, ref, start):
        self.ref, self.start = ref, start

    def __getitem__(self, at):
        return self.ref[self.start + at]


def attend_kernel(
    numbers_ref, q_ref, *refs, hops, parts,
    inst_size, tp_size, kv_local, per_head, head_dim, span_len, slot_count, longest, prompt_count,
):
    hop_refs = refs[:len(hops)]
    part_refs = refs[len(hops):len(hops) + len(parts)]
    (out_ref, cache_ref, place_ref, kv_ref, s_ref, p_ref, acc_ref, max_ref, zero_ref,
     part_sems, page_sems) = refs[len(hops) + len(parts):]
    step = pl.program_id(0)
    span_total = slot_count * inst_size
    spans_ref = Part(numbers_ref, 0)
    tail_ref = Part(numbers_ref, prompt_count)
    owner_ref = Part(numbers_ref, 2 * prompt_count)
    plan_ref = Part(numbers_ref, 3 * prompt_count)
    place_at_ref = Part(numbers_ref, 3 * prompt_count + span_total)
    inst = place_at_ref[0]
    tp = place_at_ref[1]
    slice_len = span_len // tp_size
    scale = LOG2E / math.sqrt(head_dim)

    def part_copies(act):
        for n, (pieces, j) in enumerate(parts):
            at = pl.ds(pl.multiple_of((tp ^ j) * slice_len, slice_len), slice_len)
            begin = 0
            for m, (hop, first_slot, size) in enumerate(pieces):
                slots = pl.ds(place_at_ref[2 + hop] * slot_count + first_slot, size)
                act(pltpu.make_async_copy(
                    part_refs[n].at[begin:begin + size], kv_ref.at[slots, :, at],
                    part_sems.at[n, m],
                ))
                begin += size

    def cache_copies(act):
        first = jnp.int32(0)
        count = jnp.int32(0)
        start = jnp.int32(0)
        for p in range(prompt_count):
            hit = owner_ref[p] == inst
            first = jnp.where(hit, start, first)
            count = jnp.where(hit, spans_ref[p], count)
            start = start + spans_ref[p]

        def row(r, unused):
            page = place_ref[jnp.minimum(first + r, span_total - 1)]
            for n, (hop, first_slot, size) in enumerate(hops):
                source = place_at_ref[2 + hop]
                slot = page - source * slot_count - first_slot
                here = (source >= 0) & (slot >= 0) & (slot < size)

                @pl.when((r < count) & here)
                def _():
                    act(pltpu.make_async_copy(
                        hop_refs[n].at[slot], cache_ref.at[r], page_sems.at[r]
                    ))

            @pl.when(r >= count)
            def _():
                act(pltpu.make_async_copy(zero_ref, cache_ref.at[r], page_sems.at[r]))

            return unused

        lax.fori_loop(0, longest, row, 0)

    @pl.when(step == 0)
    def _():
        part_copies(lambda copy: copy.start())

        def put(g, unused):
            place_ref[plan_ref[g]] = g
            return unused

        lax.fori_loop(0, span_total, put, 0)
        zero_ref[...] = jnp.zeros_like(zero_ref)
        cache_copies(lambda copy: copy.start())
        part_copies(lambda copy: copy.wait())

    own = inst * slot_count + step
    span = plan_ref[own]
    first = jnp.int32(0)
    end = jnp.int32(0)
    length = jnp.int32(0)
    for p in range(prompt_count):
        start = end
        end = end + spans_ref[p]
        inside = (span >= start) & (span < end)
        first = jnp.where(inside, start, first)
        length = jnp.where(inside, (spans_ref[p] - 1) * span_len + tail_ref[p], length)
    count = span - first
    live_rows = length - count * span_len
    ones = jnp.ones((span_len, head_dim), jnp.bfloat16)
    row_ids = lax.broadcasted_iota(jnp.int32, (span_len, span_len), 0)
    col_ids = lax.broadcasted_iota(jnp.int32, (span_len, span_len), 1)
    causal = row_ids >= col_ids
    live = lax.broadcasted_iota(jnp.int32, (span_len, head_dim), 0) < live_rows
    one_step = longest <= STEP

    def lanes_of(head):
        return pl.ds(pl.multiple_of(head * head_dim, head_dim), head_dim)

    def rows_of(h):
        return slice(h * span_len, (h + 1) * span_len)

    def put_out(head, total):
        out_ref[0, :, lanes_of(head)] = jnp.where(
            live, total[:, :head_dim] / total[:, head_dim:], 0.0
        ).astype(jnp.bfloat16)

    def attend(pages, begin):
        wide = len(pages) * span_len

        def kv_head(g, unused):
            keys = jnp.concatenate([kv_ref[page, g, :, :head_dim] for page in pages], axis=0)
            q = jnp.concatenate(
                [q_ref[0, :, lanes_of(g * per_head + h)] for h in range(per_head)], axis=0
            )
            s_ref[:, :wide] = lax.dot_general(
                q, keys, (((1,), (1,)), ((), ())), preferred_element_type=jnp.float32
            )
            rescales = []
            for h in range(per_head):
                head = g * per_head + h
                s = s_ref[rows_of(h), :wide] * scale
                if begin:
                    own_part = jnp.where(causal, s[:, wide - span_len:], -1e30)
                    if len(pages) > 1:
                        s = jnp.concatenate([s[:, :wide - span_len], own_part], axis=1)
                    else:
                        s = own_part
                top = jnp.max(s, axis=1, keepdims=True)
                if begin:
                    top = jnp.broadcast_to(top, (span_len, head_dim))
                else:
                    old = max_ref[head]
                    top = jnp.maximum(old, top)
                    rescales.append(jnp.exp2(old - top))
                if not one_step:
                    max_ref[head] = top
                p_ref[rows_of(h), :wide] = jnp.exp2(
                    s - jnp.concatenate([top] * len(pages), axis=1)
                ).astype(jnp.bfloat16)
            values = jnp.concatenate(
                [
                    jnp.concatenate([kv_ref[page, g, :, head_dim:], ones], axis=1)
                    for page in pages
                ],
                axis=0,
            )
            mixed = jnp.dot(p_ref[:, :wide], values, preferred_element_type=jnp.float32)
            for h in range(per_head):
                head = g * per_head + h
                new = mixed[rows_of(h)]
                if one_step:
                    put_out(head, new)
                elif begin:
                    acc_ref[head] = new
                else:
                    acc_ref[head] = new + acc_ref[head] * jnp.concatenate(
                        [rescales[h]] * 2, axis=1
                    )
            return unused

        lax.fori_loop(0, kv_local, kv_head, 0)

    over = lax.rem(count, STEP)
    for n in range(STEP):
        @pl.when(over == n)
        def _():
            attend([place_ref[first + m] for m in range(n)] + [own], True)

    if not one_step:
        def block(j, unused):
            at = first + over + STEP * j
            attend([place_ref[at + n] for n in range(STEP)], False)
            return unused

        lax.fori_loop(0, count // STEP, block, 0)
        for head in range(kv_local * per_head):
            put_out(head, acc_ref[head])

    @pl.when(step == slot_count - 1)
    def _():
        cache_copies(lambda copy: copy.wait())


def after(values, earlier):
    return lax.optimization_barrier((list(values), list(earlier)))[0]


def move_pages(kv_new, kv_local):
    inst_size = lax.axis_size("inst")
    tp_size = lax.axis_size("tp")
    inst = lax.axis_index("inst")
    tp = lax.axis_index("tp")
    slot_count, kv_heads = kv_new.shape[:2]
    sources = [list(range(inst_size))]
    hops = [((0, 0, slot_count), kv_new)]
    parts = []

    def along(x, pairs):
        return lax.ppermute(x, "inst", pairs)

    def exchange(hop, x):
        found = []
        for j in range(tp_size):
            head = ((tp ^ j) * kv_heads) // tp_size
            sent = lax.dynamic_slice_in_dim(x, head, kv_local, 1)
            if j:
                sent = lax.ppermute(sent, "tp", [(t, t ^ j) for t in range(tp_size)])
            found.append((([(hop, 0, slot_count)], j), sent))
        parts.extend(found)
        return [x for _, x in found]

    if inst_size != 4:
        exchange(0, kv_new)
        for s in range(1, inst_size):
            sources.append([(i - s) % inst_size for i in range(inst_size)])
            pairs = [(i, (i + s) % inst_size) for i in range(inst_size)]
            hops.append(((s, 0, slot_count), along(kv_new, pairs)))
            exchange(s, hops[-1][1])
        return hops, parts, sources

    sources += [[2, 3, 0, 1], [1, 0, 3, 2], [3, -1, -1, 0], [-1, 2, 1, -1], [3, 2, 1, 0]]
    middle = (inst == 1) | (inst == 2)
    shifted = along(kv_new, [(0, 2), (1, 3), (2, 0), (3, 1)])
    outer = along(kv_new, [(0, 1), (1, 0), (2, 3), (3, 2)])
    waiting = exchange(0, kv_new)
    handed = along(after([shifted], waiting)[0], [(1, 0), (2, 3)])
    inner = along(jnp.where(middle, kv_new, shifted), [(1, 2), (2, 1)])
    waiting = exchange(2, outer)
    waiting = exchange(1, after([shifted], waiting)[0])
    exchange(5, after([jnp.where(middle, inner, handed)], waiting)[0])
    for hop, x in enumerate((shifted, outer, handed, inner), 1):
        hops.append(((hop, 0, slot_count), x))
    return hops, parts, sources


def body(queries, kv_new, prompt_spans, prompt_tail, span_plan, decode_owner):
    tp_size = lax.axis_size("tp")
    inst_size = lax.axis_size("inst")
    tp_index = lax.axis_index("tp")
    inst_index = lax.axis_index("inst")
    slot_count, span_len, row_width = queries.shape
    kv_heads, slice_len, width = kv_new.shape[1:]
    head_dim = width // 2
    local_heads = row_width // head_dim
    kv_local = max(1, kv_heads // tp_size)
    per_head = local_heads // kv_local
    rows = per_head * span_len
    span_total = slot_count * inst_size
    longest = span_total // 2
    hops, parts, sources = move_pages(kv_new, kv_local)
    own_sources = lax.dynamic_index_in_dim(jnp.asarray(sources, jnp.int32), inst_index, 1, False)
    numbers = jnp.concatenate([
        prompt_spans, prompt_tail, decode_owner, span_plan,
        jnp.stack([inst_index, tp_index]).astype(jnp.int32), own_sources,
    ])
    kernel = functools.partial(
        attend_kernel,
        hops=[name for name, _ in hops],
        parts=[name for name, _ in parts],
        inst_size=inst_size,
        tp_size=tp_size,
        kv_local=kv_local,
        per_head=per_head,
        head_dim=head_dim,
        span_len=span_len,
        slot_count=slot_count,
        longest=longest,
        prompt_count=prompt_spans.shape[0],
    )
    work = slot_count * span_total // 4 * local_heads * span_len * span_len
    anywhere = pl.BlockSpec(memory_space=pl.ANY)
    by_slot = pl.BlockSpec((1, span_len, row_width), lambda i, *_: (i, 0, 0))
    kept = (local_heads, span_len) if longest > STEP else (1, 8)
    return pl.pallas_call(
        kernel,
        grid_spec=pltpu.PrefetchScalarGridSpec(
            num_scalar_prefetch=1,
            grid=(slot_count,),
            in_specs=[by_slot] + [anywhere] * (len(hops) + len(parts)),
            out_specs=[by_slot, anywhere],
            scratch_shapes=[
                pltpu.SMEM((span_total,), jnp.int32),
                pltpu.VMEM((span_total, kv_local, span_len, width), jnp.bfloat16),
                pltpu.VMEM((rows, STEP * span_len), jnp.float32),
                pltpu.VMEM((rows, STEP * span_len), jnp.bfloat16),
                pltpu.VMEM(kept + (2 * head_dim,), jnp.float32),
                pltpu.VMEM(kept + (head_dim,), jnp.float32),
                pltpu.VMEM((kv_heads, slice_len, width), jnp.bfloat16),
                pltpu.SemaphoreType.DMA((len(parts), max(len(x[0][0]) for x in parts))),
                pltpu.SemaphoreType.DMA((longest,)),
            ],
        ),
        out_shape=[
            jax.ShapeDtypeStruct(queries.shape, jnp.bfloat16),
            jax.ShapeDtypeStruct((longest, kv_heads, slice_len, width), jnp.bfloat16),
        ],
        cost_estimate=pl.CostEstimate(
            flops=4 * work * head_dim, bytes_accessed=8 << 20, transcendentals=work
        ),
        compiler_params=pltpu.CompilerParams(vmem_limit_bytes=VMEM_BYTES),
    )(numbers, queries, *[x for _, x in hops], *[x for _, x in parts])


def solution(mesh):
    placed = (
        P(("groups", "inst"), None, "tp"),
        P(("groups", "inst"), None, "tp", None),
        P("groups"),
        P("groups"),
        P("groups"),
        P("groups"),
    )
    return jax.shard_map(
        body,
        mesh=mesh,
        in_specs=placed,
        out_specs=(P(("groups", "inst"), None, "tp"), P(("groups", "inst"), None, "tp", None)),
        check_vma=False,
    )
```

```python
import functools
import math

import jax
import jax.numpy as jnp
from jax import lax
from jax.experimental import pallas as pl
from jax.experimental.pallas import tpu as pltpu
from jax.sharding import PartitionSpec as P

HEADS = 64
KVH = 8
LOG2E = 1.4426950408889634
STEP = 8
VMEM_BYTES = 40 << 20


class Part:
    def __init__(self, ref, start):
        self.ref, self.start = ref, start

    def __getitem__(self, at):
        return self.ref[self.start + at]


def attend_kernel(
    numbers_ref, q_ref, *refs, hops, parts,
    inst_size, tp_size, kv_local, per_head, head_dim, span_len, slot_count, longest, prompt_count,
):
    hop_refs = refs[:len(hops)]
    part_refs = refs[len(hops):len(hops) + len(parts)]
    (out_ref, cache_ref, place_ref, kv_ref, s_ref, p_ref, acc_ref, max_ref, zero_ref,
     part_sems, page_sems) = refs[len(hops) + len(parts):]
    step = pl.program_id(0)
    span_total = slot_count * inst_size
    spans_ref = Part(numbers_ref, 0)
    tail_ref = Part(numbers_ref, prompt_count)
    owner_ref = Part(numbers_ref, 2 * prompt_count)
    plan_ref = Part(numbers_ref, 3 * prompt_count)
    place_at_ref = Part(numbers_ref, 3 * prompt_count + span_total)
    inst = place_at_ref[0]
    tp = place_at_ref[1]
    slice_len = span_len // tp_size
    scale = LOG2E / math.sqrt(head_dim)

    def part_copies(act):
        for n, (pieces, j) in enumerate(parts):
            at = pl.ds(pl.multiple_of((tp ^ j) * slice_len, slice_len), slice_len)
            begin = 0
            for m, (hop, first_slot, size) in enumerate(pieces):
                slots = pl.ds(place_at_ref[2 + hop] * slot_count + first_slot, size)
                act(pltpu.make_async_copy(
                    part_refs[n].at[begin:begin + size], kv_ref.at[slots, :, at],
                    part_sems.at[n, m],
                ))
                begin += size

    def cache_copies(act):
        first = jnp.int32(0)
        count = jnp.int32(0)
        start = jnp.int32(0)
        for p in range(prompt_count):
            hit = owner_ref[p] == inst
            first = jnp.where(hit, start, first)
            count = jnp.where(hit, spans_ref[p], count)
            start = start + spans_ref[p]

        def row(r, unused):
            page = place_ref[jnp.minimum(first + r, span_total - 1)]
            for n, (hop, first_slot, size) in enumerate(hops):
                source = place_at_ref[2 + hop]
                slot = page - source * slot_count - first_slot
                here = (source >= 0) & (slot >= 0) & (slot < size)

                @pl.when((r < count) & here)
                def _():
                    act(pltpu.make_async_copy(
                        hop_refs[n].at[slot], cache_ref.at[r], page_sems.at[r]
                    ))

            @pl.when(r >= count)
            def _():
                act(pltpu.make_async_copy(zero_ref, cache_ref.at[r], page_sems.at[r]))

            return unused

        lax.fori_loop(0, longest, row, 0)

    @pl.when(step == 0)
    def _():
        part_copies(lambda copy: copy.start())

        def put(g, unused):
            place_ref[plan_ref[g]] = g
            return unused

        lax.fori_loop(0, span_total, put, 0)
        zero_ref[...] = jnp.zeros_like(zero_ref)
        cache_copies(lambda copy: copy.start())
        part_copies(lambda copy: copy.wait())

    own = inst * slot_count + step
    span = plan_ref[own]
    first = jnp.int32(0)
    end = jnp.int32(0)
    length = jnp.int32(0)
    for p in range(prompt_count):
        start = end
        end = end + spans_ref[p]
        inside = (span >= start) & (span < end)
        first = jnp.where(inside, start, first)
        length = jnp.where(inside, (spans_ref[p] - 1) * span_len + tail_ref[p], length)
    count = span - first
    live_rows = length - count * span_len
    ones = jnp.ones((span_len, head_dim), jnp.bfloat16)
    row_ids = lax.broadcasted_iota(jnp.int32, (span_len, span_len), 0)
    col_ids = lax.broadcasted_iota(jnp.int32, (span_len, span_len), 1)
    causal = row_ids >= col_ids
    live = lax.broadcasted_iota(jnp.int32, (span_len, head_dim), 0) < live_rows
    one_step = longest <= STEP

    def lanes_of(head):
        return slice(head * head_dim, (head + 1) * head_dim)

    def rows_of(h):
        return slice(h * span_len, (h + 1) * span_len)

    def put_out(head, total):
        out_ref[0, :, lanes_of(head)] = jnp.where(
            live, total[:, :head_dim] / total[:, head_dim:], 0.0
        ).astype(jnp.bfloat16)

    def attend(pages, begin):
        wide = len(pages) * span_len

        def cols_of(n):
            return slice(n * span_len, (n + 1) * span_len)

        for g in range(kv_local):
            q = jnp.concatenate(
                [q_ref[0, :, lanes_of(g * per_head + h)] for h in range(per_head)], axis=0
            )
            for n in range(0, len(pages), 2):
                some = pages[n:n + 2]
                keys = jnp.concatenate([kv_ref[p, g, :, :head_dim] for p in some], axis=0)
                s = lax.dot_general(
                    q, keys, (((1,), (1,)), ((), ())), preferred_element_type=jnp.float32
                )
                for m in range(len(some)):
                    if begin and n + m == len(pages) - 1:
                        for h in range(per_head):
                            s_ref[g, rows_of(h), cols_of(n + m)] = jnp.where(
                                causal, s[rows_of(h), cols_of(m)], -1e30
                            )
                    else:
                        s_ref[g, :, cols_of(n + m)] = s[:, cols_of(m)]
        for g in range(kv_local):
            rescales = []
            for h in range(per_head):
                head = g * per_head + h
                top = s_ref[g, rows_of(h), cols_of(0)]
                for n in range(1, len(pages)):
                    top = jnp.maximum(top, s_ref[g, rows_of(h), cols_of(n)])
                top = jnp.broadcast_to(
                    jnp.max(top, axis=1, keepdims=True) * scale, (span_len, head_dim)
                )
                if not begin:
                    old = max_ref[head]
                    top = jnp.maximum(old, top)
                    rescales.append(jnp.exp2(old - top))
                if not one_step:
                    max_ref[head] = top
                for n in range(len(pages)):
                    p_ref[g, rows_of(h), cols_of(n)] = jnp.exp2(
                        s_ref[g, rows_of(h), cols_of(n)] * scale - top
                    ).astype(jnp.bfloat16)
            values = jnp.concatenate(
                [
                    jnp.concatenate([kv_ref[page, g, :, head_dim:], ones], axis=1)
                    for page in pages
                ],
                axis=0,
            )
            mixed = jnp.dot(p_ref[g, :, :wide], values, preferred_element_type=jnp.float32)
            for h in range(per_head):
                head = g * per_head + h
                new = mixed[rows_of(h)]
                if one_step:
                    put_out(head, new)
                elif begin:
                    acc_ref[head] = new
                else:
                    acc_ref[head] = new + acc_ref[head] * jnp.concatenate(
                        [rescales[h]] * 2, axis=1
                    )

    over = lax.rem(count, STEP)
    for n in range(STEP):
        @pl.when(over == n)
        def _():
            attend([place_ref[first + m] for m in range(n)] + [own], True)

    if not one_step:
        def block(j, unused):
            at = first + over + STEP * j
            attend([place_ref[at + n] for n in range(STEP)], False)
            return unused

        lax.fori_loop(0, count // STEP, block, 0)
        for head in range(kv_local * per_head):
            put_out(head, acc_ref[head])

    @pl.when(step == slot_count - 1)
    def _():
        cache_copies(lambda copy: copy.wait())


def after(values, earlier):
    return lax.optimization_barrier((list(values), list(earlier)))[0]


def move_pages(kv_new, kv_local):
    inst_size = lax.axis_size("inst")
    tp_size = lax.axis_size("tp")
    inst = lax.axis_index("inst")
    tp = lax.axis_index("tp")
    slot_count, kv_heads = kv_new.shape[:2]
    sources = [list(range(inst_size))]
    hops = [((0, 0, slot_count), kv_new)]
    parts = []

    def along(x, pairs):
        return lax.ppermute(x, "inst", pairs)

    def exchange(hop, x):
        found = []
        for j in range(tp_size):
            head = ((tp ^ j) * kv_heads) // tp_size
            sent = lax.dynamic_slice_in_dim(x, head, kv_local, 1)
            if j:
                sent = lax.ppermute(sent, "tp", [(t, t ^ j) for t in range(tp_size)])
            found.append((([(hop, 0, slot_count)], j), sent))
        parts.extend(found)
        return [x for _, x in found]

    if inst_size != 4:
        exchange(0, kv_new)
        for s in range(1, inst_size):
            sources.append([(i - s) % inst_size for i in range(inst_size)])
            pairs = [(i, (i + s) % inst_size) for i in range(inst_size)]
            hops.append(((s, 0, slot_count), along(kv_new, pairs)))
            exchange(s, hops[-1][1])
        return hops, parts, sources

    sources += [[1, 0, 3, 2], [-1, 2, 1, -1], [-1, 3, 0, -1], [2, -1, -1, 1], [3, -1, -1, 0]]
    sources += [[2, 2, 1, 1], [3, 3, 0, 0]]
    middle = (inst == 1) | (inst == 2)
    outer = along(kv_new, [(0, 1), (1, 0), (2, 3), (3, 2)])
    inner = along(kv_new, [(1, 2), (2, 1)])
    waiting = exchange(0, kv_new)
    outer_on, inner_on = after([outer, inner], waiting)
    crossed = along(outer_on, [(1, 2), (2, 1)])
    inner_ends = along(inner_on, [(1, 0), (2, 3)])
    waiting = exchange(1, outer_on)
    crossed_ends = along(after([crossed], waiting)[0], [(1, 0), (2, 3)])
    waiting = exchange(6, jnp.where(middle, inner, inner_ends))
    exchange(7, after([jnp.where(middle, crossed, crossed_ends)], waiting)[0])
    for hop, x in enumerate((outer, inner, crossed, inner_ends, crossed_ends), 1):
        hops.append(((hop, 0, slot_count), x))
    return hops, parts, sources


def body(queries, kv_new, prompt_spans, prompt_tail, span_plan, decode_owner):
    tp_size = lax.axis_size("tp")
    inst_size = lax.axis_size("inst")
    tp_index = lax.axis_index("tp")
    inst_index = lax.axis_index("inst")
    slot_count, span_len, row_width = queries.shape
    kv_heads, slice_len, width = kv_new.shape[1:]
    head_dim = width // 2
    local_heads = row_width // head_dim
    kv_local = max(1, kv_heads // tp_size)
    per_head = local_heads // kv_local
    rows = per_head * span_len
    span_total = slot_count * inst_size
    longest = span_total // 2
    hops, parts, sources = move_pages(kv_new, kv_local)
    own_sources = lax.dynamic_index_in_dim(jnp.asarray(sources, jnp.int32), inst_index, 1, False)
    numbers = jnp.concatenate([
        prompt_spans, prompt_tail, decode_owner, span_plan,
        jnp.stack([inst_index, tp_index]).astype(jnp.int32), own_sources,
    ])
    kernel = functools.partial(
        attend_kernel,
        hops=[name for name, _ in hops],
        parts=[name for name, _ in parts],
        inst_size=inst_size,
        tp_size=tp_size,
        kv_local=kv_local,
        per_head=per_head,
        head_dim=head_dim,
        span_len=span_len,
        slot_count=slot_count,
        longest=longest,
        prompt_count=prompt_spans.shape[0],
    )
    work = slot_count * span_total // 4 * local_heads * span_len * span_len
    outside = pl.BlockSpec(memory_space=pltpu.HBM)
    by_slot = pl.BlockSpec((1, span_len, row_width), lambda i, *_: (i, 0, 0))
    kept = (local_heads, span_len) if longest > STEP else (1, 8)
    return pl.pallas_call(
        kernel,
        grid_spec=pltpu.PrefetchScalarGridSpec(
            num_scalar_prefetch=1,
            grid=(slot_count,),
            in_specs=[by_slot] + [outside] * (len(hops) + len(parts)),
            out_specs=[by_slot, outside],
            scratch_shapes=[
                pltpu.SMEM((span_total,), jnp.int32),
                pltpu.VMEM((span_total, kv_local, span_len, width), jnp.bfloat16),
                pltpu.VMEM((kv_local, rows, STEP * span_len), jnp.float32),
                pltpu.VMEM((kv_local, rows, STEP * span_len), jnp.bfloat16),
                pltpu.VMEM(kept + (2 * head_dim,), jnp.float32),
                pltpu.VMEM(kept + (head_dim,), jnp.float32),
                pltpu.VMEM((kv_heads, slice_len, width), jnp.bfloat16),
                pltpu.SemaphoreType.DMA((len(parts), max(len(x[0][0]) for x in parts))),
                pltpu.SemaphoreType.DMA((longest,)),
            ],
        ),
        out_shape=[
            jax.ShapeDtypeStruct(queries.shape, jnp.bfloat16),
            jax.ShapeDtypeStruct((longest, kv_heads, slice_len, width), jnp.bfloat16),
        ],
        cost_estimate=pl.CostEstimate(
            flops=4 * work * head_dim, bytes_accessed=8 << 20, transcendentals=work
        ),
        compiler_params=pltpu.CompilerParams(vmem_limit_bytes=VMEM_BYTES),
    )(numbers, queries, *[x for _, x in hops], *[x for _, x in parts])


def solution(mesh):
    placed = (
        P(("groups", "inst"), None, "tp"),
        P(("groups", "inst"), None, "tp", None),
        P("groups"),
        P("groups"),
        P("groups"),
        P("groups"),
    )
    return jax.shard_map(
        body,
        mesh=mesh,
        in_specs=placed,
        out_specs=(P(("groups", "inst"), None, "tp"), P(("groups", "inst"), None, "tp", None)),
        check_vma=False,
    )
```

```python
import functools
import math

import jax
import jax.numpy as jnp
from jax import lax
from jax.experimental import pallas as pl
from jax.experimental.pallas import tpu as pltpu
from jax.sharding import PartitionSpec as P

HEADS = 64
KVH = 8
LOG2E = 1.4426950408889634
STEP = 8
VMEM_BYTES = 40 << 20


def place_kernel(
    spans_ref, owner_ref, plan_ref, place_at_ref, *refs, hops, slot_count, longest,
):
    hop_refs = refs[:len(hops)]
    cache_ref, place_ref, zero_ref, sems = refs[len(hops):]
    inst = place_at_ref[0]
    first, count, start = jnp.int32(0), jnp.int32(0), jnp.int32(0)
    for p in range(spans_ref.shape[0]):
        hit = owner_ref[p] == inst
        first = jnp.where(hit, start, first)
        count = jnp.where(hit, spans_ref[p], count)
        start = start + spans_ref[p]
    span_total = plan_ref.shape[0]

    def put(g, unused):
        place_ref[plan_ref[g]] = g
        return unused

    lax.fori_loop(0, span_total, put, 0)
    zero_ref[...] = jnp.zeros_like(zero_ref)

    def copies(act):
        def row(r, unused):
            page = place_ref[jnp.minimum(first + r, span_total - 1)]
            for n, hop in enumerate(hops):
                source = place_at_ref[2 + hop]
                slot = page - source * slot_count

                @pl.when((r < count) & (source >= 0) & (slot >= 0) & (slot < slot_count))
                def _():
                    act(pltpu.make_async_copy(hop_refs[n].at[slot], cache_ref.at[r], sems.at[r]))

            @pl.when(r >= count)
            def _():
                act(pltpu.make_async_copy(zero_ref, cache_ref.at[r], sems.at[r]))

            return unused

        lax.fori_loop(0, longest, row, 0)

    copies(lambda copy: copy.start())
    copies(lambda copy: copy.wait())


def attend_kernel(
    spans_ref, tail_ref, plan_ref, place_at_ref, q_ref, *refs, parts,
    inst_size, tp_size, kv_local, per_head, head_dim, span_len, slot_count, longest,
):
    part_refs = refs[:len(parts)]
    out_ref, place_ref, kv_ref, s_ref, p_ref, acc_ref, max_ref, part_sems = refs[len(parts):]
    step = pl.program_id(0)
    span_total = slot_count * inst_size
    prompt_count = spans_ref.shape[0]
    inst = place_at_ref[0]
    tp = place_at_ref[1]
    slice_len = span_len // tp_size
    scale = LOG2E / math.sqrt(head_dim)

    def part_copies(act):
        for n, (hop, j) in enumerate(parts):
            slots = pl.ds(place_at_ref[2 + hop] * slot_count, slot_count)
            at = pl.ds(pl.multiple_of((tp ^ j) * slice_len, slice_len), slice_len)
            act(pltpu.make_async_copy(part_refs[n], kv_ref.at[slots, :, at], part_sems.at[n]))

    @pl.when(step == 0)
    def _():
        part_copies(lambda copy: copy.start())

        def put(g, unused):
            place_ref[plan_ref[g]] = g
            return unused

        lax.fori_loop(0, span_total, put, 0)
        part_copies(lambda copy: copy.wait())

    own = inst * slot_count + step
    span = plan_ref[own]
    first = jnp.int32(0)
    end = jnp.int32(0)
    length = jnp.int32(0)
    for p in range(prompt_count):
        start = end
        end = end + spans_ref[p]
        inside = (span >= start) & (span < end)
        first = jnp.where(inside, start, first)
        length = jnp.where(inside, (spans_ref[p] - 1) * span_len + tail_ref[p], length)
    count = span - first
    live_rows = length - count * span_len
    ones = jnp.ones((span_len, head_dim), jnp.bfloat16)
    row_ids = lax.broadcasted_iota(jnp.int32, (span_len, span_len), 0)
    col_ids = lax.broadcasted_iota(jnp.int32, (span_len, span_len), 1)
    causal = row_ids >= col_ids
    live = lax.broadcasted_iota(jnp.int32, (span_len, head_dim), 0) < live_rows
    one_step = longest <= STEP

    def lanes_of(head):
        return slice(head * head_dim, (head + 1) * head_dim)

    def rows_of(h):
        return slice(h * span_len, (h + 1) * span_len)

    def put_out(head, total):
        out_ref[0, :, lanes_of(head)] = jnp.where(
            live, total[:, :head_dim] / total[:, head_dim:], 0.0
        ).astype(jnp.bfloat16)

    def attend(pages, begin):
        wide = len(pages) * span_len

        def cols_of(n):
            return slice(n * span_len, (n + 1) * span_len)

        for g in range(kv_local):
            q = jnp.concatenate(
                [q_ref[0, :, lanes_of(g * per_head + h)] for h in range(per_head)], axis=0
            )
            for n in range(0, len(pages), 2):
                some = pages[n:n + 2]
                keys = jnp.concatenate([kv_ref[p, g, :, :head_dim] for p in some], axis=0)
                s = lax.dot_general(
                    q, keys, (((1,), (1,)), ((), ())), preferred_element_type=jnp.float32
                )
                for m in range(len(some)):
                    if begin and n + m == len(pages) - 1:
                        for h in range(per_head):
                            s_ref[g, rows_of(h), cols_of(n + m)] = jnp.where(
                                causal, s[rows_of(h), cols_of(m)], -1e30
                            )
                    else:
                        s_ref[g, :, cols_of(n + m)] = s[:, cols_of(m)]
        for g in range(kv_local):
            rescales = []
            for h in range(per_head):
                head = g * per_head + h
                top = s_ref[g, rows_of(h), cols_of(0)]
                for n in range(1, len(pages)):
                    top = jnp.maximum(top, s_ref[g, rows_of(h), cols_of(n)])
                top = jnp.broadcast_to(
                    jnp.max(top, axis=1, keepdims=True) * scale, (span_len, head_dim)
                )
                if not begin:
                    old = max_ref[head]
                    top = jnp.maximum(old, top)
                    rescales.append(jnp.exp2(old - top))
                if not one_step:
                    max_ref[head] = top
                for n in range(len(pages)):
                    p_ref[g, rows_of(h), cols_of(n)] = jnp.exp2(
                        s_ref[g, rows_of(h), cols_of(n)] * scale - top
                    ).astype(jnp.bfloat16)
            values = jnp.concatenate(
                [
                    jnp.concatenate([kv_ref[page, g, :, head_dim:], ones], axis=1)
                    for page in pages
                ],
                axis=0,
            )
            mixed = jnp.dot(p_ref[g, :, :wide], values, preferred_element_type=jnp.float32)
            for h in range(per_head):
                head = g * per_head + h
                new = mixed[rows_of(h)]
                if one_step:
                    put_out(head, new)
                elif begin:
                    acc_ref[head] = new
                else:
                    acc_ref[head] = new + acc_ref[head] * jnp.concatenate(
                        [rescales[h]] * 2, axis=1
                    )

    over = lax.rem(count, STEP)
    for n in range(STEP):
        @pl.when(over == n)
        def _():
            attend([place_ref[first + m] for m in range(n)] + [own], True)

    if not one_step:
        def block(j, unused):
            at = first + over + STEP * j
            attend([place_ref[at + n] for n in range(STEP)], False)
            return unused

        lax.fori_loop(0, count // STEP, block, 0)
        for head in range(kv_local * per_head):
            put_out(head, acc_ref[head])


def after(values, earlier):
    return lax.optimization_barrier((list(values), list(earlier)))[0]


def move_pages(kv_new, kv_local):
    inst_size = lax.axis_size("inst")
    tp_size = lax.axis_size("tp")
    inst = lax.axis_index("inst")
    tp = lax.axis_index("tp")
    slot_count, kv_heads = kv_new.shape[:2]
    sources = [list(range(inst_size))]
    hops = [(0, kv_new)]
    parts = []

    def along(x, pairs):
        return lax.ppermute(x, "inst", pairs)

    def exchange(hop, x):
        found = []
        for j in range(tp_size):
            head = ((tp ^ j) * kv_heads) // tp_size
            sent = lax.dynamic_slice_in_dim(x, head, kv_local, 1)
            if j:
                sent = lax.ppermute(sent, "tp", [(t, t ^ j) for t in range(tp_size)])
            found.append(((hop, j), sent))
        parts.extend(found)
        return [x for _, x in found]

    if inst_size != 4:
        exchange(0, kv_new)
        for s in range(1, inst_size):
            sources.append([(i - s) % inst_size for i in range(inst_size)])
            pairs = [(i, (i + s) % inst_size) for i in range(inst_size)]
            hops.append((s, along(kv_new, pairs)))
            exchange(s, hops[-1][1])
        return hops, parts, sources

    sources += [[1, 0, 3, 2], [-1, 2, 1, -1], [-1, 3, 0, -1], [2, -1, -1, 1], [3, -1, -1, 0]]
    sources += [[2, 2, 1, 1], [3, 3, 0, 0]]
    middle = (inst == 1) | (inst == 2)
    outer = along(kv_new, [(0, 1), (1, 0), (2, 3), (3, 2)])
    inner = along(kv_new, [(1, 2), (2, 1)])
    waiting = exchange(0, kv_new)
    outer_on, inner_on = after([outer, inner], waiting)
    crossed = along(outer_on, [(1, 2), (2, 1)])
    inner_ends = along(inner_on, [(1, 0), (2, 3)])
    waiting = exchange(1, outer_on)
    crossed_ends = along(after([crossed], waiting)[0], [(1, 0), (2, 3)])
    waiting = exchange(6, jnp.where(middle, inner, inner_ends))
    exchange(7, after([jnp.where(middle, crossed, crossed_ends)], waiting)[0])
    hops += enumerate((outer, inner, crossed, inner_ends, crossed_ends), 1)
    return hops, parts, sources


def body(queries, kv_new, prompt_spans, prompt_tail, span_plan, decode_owner):
    tp_size = lax.axis_size("tp")
    inst_size = lax.axis_size("inst")
    tp_index = lax.axis_index("tp")
    inst_index = lax.axis_index("inst")
    slot_count, span_len, row_width = queries.shape
    kv_heads, slice_len, width = kv_new.shape[1:]
    head_dim = width // 2
    local_heads = row_width // head_dim
    kv_local = max(1, kv_heads // tp_size)
    per_head = local_heads // kv_local
    rows = per_head * span_len
    span_total = slot_count * inst_size
    longest = span_total // 2
    hops, parts, sources = move_pages(kv_new, kv_local)
    own_sources = lax.dynamic_index_in_dim(jnp.asarray(sources, jnp.int32), inst_index, 1, False)
    place_at = jnp.concatenate([jnp.stack([inst_index, tp_index]).astype(jnp.int32), own_sources])
    anywhere = pl.BlockSpec(memory_space=pl.ANY)
    page_shape = (kv_heads, slice_len, width)
    owner_cache = pl.pallas_call(
        functools.partial(
            place_kernel,
            hops=[name for name, _ in hops],
            slot_count=slot_count,
            longest=longest,
        ),
        grid_spec=pltpu.PrefetchScalarGridSpec(
            num_scalar_prefetch=4,
            grid=(1,),
            in_specs=[anywhere] * len(hops),
            out_specs=anywhere,
            scratch_shapes=[
                pltpu.SMEM((span_total,), jnp.int32),
                pltpu.VMEM(page_shape, jnp.bfloat16),
                pltpu.SemaphoreType.DMA((longest,)),
            ],
        ),
        out_shape=jax.ShapeDtypeStruct((longest,) + page_shape, jnp.bfloat16),
        cost_estimate=pl.CostEstimate(flops=0, bytes_accessed=8 << 20, transcendentals=0),
    )(prompt_spans, decode_owner, span_plan, place_at, *[x for _, x in hops])
    kernel = functools.partial(
        attend_kernel,
        parts=[name for name, _ in parts],
        inst_size=inst_size,
        tp_size=tp_size,
        kv_local=kv_local,
        per_head=per_head,
        head_dim=head_dim,
        span_len=span_len,
        slot_count=slot_count,
        longest=longest,
    )
    work = slot_count * span_total // 4 * local_heads * span_len * span_len
    by_slot = pl.BlockSpec((1, span_len, row_width), lambda i, *_: (i, 0, 0))
    kept = (local_heads, span_len) if longest > STEP else (1, 8)
    attended = pl.pallas_call(
        kernel,
        grid_spec=pltpu.PrefetchScalarGridSpec(
            num_scalar_prefetch=4,
            grid=(slot_count,),
            in_specs=[by_slot] + [anywhere] * len(parts),
            out_specs=by_slot,
            scratch_shapes=[
                pltpu.SMEM((span_total,), jnp.int32),
                pltpu.VMEM((span_total, kv_local, span_len, width), jnp.bfloat16),
                pltpu.VMEM((kv_local, rows, STEP * span_len), jnp.float32),
                pltpu.VMEM((kv_local, rows, STEP * span_len), jnp.bfloat16),
                pltpu.VMEM(kept + (2 * head_dim,), jnp.float32),
                pltpu.VMEM(kept + (head_dim,), jnp.float32),
                pltpu.SemaphoreType.DMA((len(parts),)),
            ],
        ),
        out_shape=jax.ShapeDtypeStruct(queries.shape, jnp.bfloat16),
        cost_estimate=pl.CostEstimate(
            flops=4 * work * head_dim, bytes_accessed=8 << 20, transcendentals=work
        ),
        compiler_params=pltpu.CompilerParams(vmem_limit_bytes=VMEM_BYTES),
    )(prompt_spans, prompt_tail, span_plan, place_at, queries, *[x for _, x in parts])
    return attended, owner_cache


def solution(mesh):
    placed = (
        P(("groups", "inst"), None, "tp"),
        P(("groups", "inst"), None, "tp", None),
        P("groups"),
        P("groups"),
        P("groups"),
        P("groups"),
    )
    return jax.shard_map(
        body,
        mesh=mesh,
        in_specs=placed,
        out_specs=(P(("groups", "inst"), None, "tp"), P(("groups", "inst"), None, "tp", None)),
        check_vma=False,
    )
```

```python
import functools
import math

import jax
import jax.numpy as jnp
from jax import lax
from jax.experimental import pallas as pl
from jax.experimental.pallas import tpu as pltpu
from jax.sharding import PartitionSpec as P

HEADS = 64
KVH = 8
LOG2E = 1.4426950408889634
STEP = 4
VMEM_BYTES = 24 << 20


class Part:
    def __init__(self, ref, start):
        self.ref, self.start = ref, start

    def __getitem__(self, at):
        return self.ref[self.start + at]


def place_kernel(numbers_ref, *refs, hops, slot_count, span_total, longest, prompt_count):
    hop_refs = refs[:len(hops)]
    cache_ref, place_ref, stage_ref, sems, out_sem = refs[len(hops):]
    spans_ref = Part(numbers_ref, 0)
    owner_ref = Part(numbers_ref, 2 * prompt_count)
    plan_ref = Part(numbers_ref, 3 * prompt_count)
    place_at_ref = Part(numbers_ref, 3 * prompt_count + span_total)
    inst = place_at_ref[0]
    first, count, start = jnp.int32(0), jnp.int32(0), jnp.int32(0)
    for p in range(prompt_count):
        hit = owner_ref[p] == inst
        first = jnp.where(hit, start, first)
        count = jnp.where(hit, spans_ref[p], count)
        start = start + spans_ref[p]

    def put(g, unused):
        place_ref[plan_ref[g]] = g
        return unused

    lax.fori_loop(0, span_total, put, 0)

    def copies(act, fill):
        def row(r, unused):
            page = place_ref[jnp.minimum(first + r, span_total - 1)]
            for n, hop in enumerate(hops):
                source = place_at_ref[2 + hop]
                slot = page - source * slot_count

                @pl.when((r < count) & (source >= 0) & (slot >= 0) & (slot < slot_count))
                def _():
                    act(pltpu.make_async_copy(hop_refs[n].at[slot], stage_ref.at[r], sems.at[r]))

            if fill:
                @pl.when(r >= count)
                def _():
                    stage_ref[r] = jnp.zeros(stage_ref.shape[1:], stage_ref.dtype)

            return unused

        lax.fori_loop(0, longest, row, 0)

    copies(lambda copy: copy.start(), True)
    copies(lambda copy: copy.wait(), False)
    out = pltpu.make_async_copy(stage_ref, cache_ref, out_sem)
    out.start()
    out.wait()


def attend_kernel(
    numbers_ref, *refs,
    covers, parts, later, first_call, last_call,
    inst_size, tp_size, kv_local, per_head, head_dim, span_len, slot_count, longest, prompt_count,
):
    refs = list(refs)

    def take(count):
        taken = refs[:count]
        del refs[:count]
        return taken

    (q_ref,) = take(1)
    mixed_ref, total_ref = (None, None) if first_call else take(2)
    part_refs = take(len(parts))
    take(later)
    (out_ref,) = take(1)
    if not last_call:
        (next_total_ref,) = take(1)
    place_ref, list_ref, kv_ref, s_ref, p_ref, acc_ref, max_ref, part_sems = take(8)
    step = pl.program_id(0)
    span_total = slot_count * inst_size
    spans_ref = Part(numbers_ref, 0)
    tail_ref = Part(numbers_ref, prompt_count)
    owner_ref = Part(numbers_ref, 2 * prompt_count)
    plan_ref = Part(numbers_ref, 3 * prompt_count)
    place_at_ref = Part(numbers_ref, 3 * prompt_count + span_total)
    inst = place_at_ref[0]
    tp = place_at_ref[1]
    slice_len = span_len // tp_size
    most = min(longest, len(covers) * slot_count)
    scale = LOG2E / math.sqrt(head_dim)

    def part_copies(act):
        for n, (hop, j) in enumerate(parts):
            slots = pl.ds(place_at_ref[2 + hop] * slot_count, slot_count)
            at = pl.ds(pl.multiple_of((tp ^ j) * slice_len, slice_len), slice_len)
            act(pltpu.make_async_copy(part_refs[n], kv_ref.at[slots, :, at], part_sems.at[n]))

    @pl.when(step == 0)
    def _():
        part_copies(lambda copy: copy.start())

        def put(g, unused):
            place_ref[plan_ref[g]] = g
            return unused

        lax.fori_loop(0, span_total, put, 0)
        part_copies(lambda copy: copy.wait())

    own = inst * slot_count + step
    span = plan_ref[own]
    first = jnp.int32(0)
    end = jnp.int32(0)
    length = jnp.int32(0)
    for p in range(prompt_count):
        start = end
        end = end + spans_ref[p]
        inside = (span >= start) & (span < end)
        first = jnp.where(inside, start, first)
        length = jnp.where(inside, (spans_ref[p] - 1) * span_len + tail_ref[p], length)
    live_rows = length - (span - first) * span_len

    def look(k, count):
        page = place_ref[k]
        source = page // slot_count
        covered = jnp.bool_(False)
        for hop in covers:
            covered = covered | (place_at_ref[2 + hop] == source)
        list_ref[count] = page
        return count + covered.astype(jnp.int32)

    count = lax.fori_loop(first, span, look, jnp.int32(0))

    ones = jnp.ones((span_len, head_dim), jnp.bfloat16)
    row_ids = lax.broadcasted_iota(jnp.int32, (span_len, span_len), 0)
    col_ids = lax.broadcasted_iota(jnp.int32, (span_len, span_len), 1)
    causal = row_ids >= col_ids
    lane_ids = lax.broadcasted_iota(jnp.int32, (span_len, head_dim), 1)
    def lanes_of(head):
        return slice(head * head_dim, (head + 1) * head_dim)

    def rows_of(h):
        return slice(h * span_len, (h + 1) * span_len)

    def attend(pages, since):
        wide = len(pages) * span_len
        for g in range(kv_local):
            keys = jnp.concatenate([kv_ref[page, g, :, :head_dim] for page in pages], axis=0)
            q = jnp.concatenate(
                [q_ref[0, :, lanes_of(g * per_head + h)] for h in range(per_head)], axis=0
            )
            s_ref[g, :, :wide] = lax.dot_general(
                q, keys, (((1,), (1,)), ((), ())), preferred_element_type=jnp.float32
            )
        for g in range(kv_local):
            rescales = []
            for h in range(per_head):
                head = g * per_head + h
                s = s_ref[g, rows_of(h), :wide] * scale
                if since == "start":
                    own_part = jnp.where(causal, s[:, wide - span_len:], -1e30)
                    if len(pages) > 1:
                        s = jnp.concatenate([s[:, :wide - span_len], own_part], axis=1)
                    else:
                        s = own_part
                top = jnp.max(s, axis=1, keepdims=True)
                if since == "start":
                    top = jnp.broadcast_to(top, (span_len, head_dim))
                else:
                    if since == "given":
                        old = jnp.broadcast_to(
                            total_ref[0, :, head:head + 1], (span_len, head_dim)
                        )
                    else:
                        old = max_ref[head]
                    top = jnp.maximum(old, top)
                    rescales.append(jnp.exp2(old - top))
                max_ref[head] = top
                p_ref[g, rows_of(h), :wide] = jnp.exp2(
                    s - jnp.concatenate([top] * len(pages), axis=1)
                ).astype(jnp.bfloat16)
            values = jnp.concatenate(
                [
                    jnp.concatenate([kv_ref[page, g, :, head_dim:], ones], axis=1)
                    for page in pages
                ],
                axis=0,
            )
            mixed = jnp.dot(p_ref[g, :, :wide], values, preferred_element_type=jnp.float32)
            for h in range(per_head):
                head = g * per_head + h
                new = mixed[rows_of(h)]
                if since == "given":
                    given = mixed_ref[0, :, lanes_of(head)].astype(jnp.float32)
                    new = new + jnp.concatenate([given * rescales[h], rescales[h]], axis=1)
                elif since == "here":
                    new = new + acc_ref[head] * jnp.concatenate([rescales[h]] * 2, axis=1)
                acc_ref[head] = new

    def rest(begin):
        if most <= STEP:
            return

        def block(j, unused):
            at = begin + STEP * j
            attend([list_ref[at + n] for n in range(STEP)], "here")
            return unused

        lax.fori_loop(0, (count - begin) // STEP, block, 0)

    live = lax.broadcasted_iota(jnp.int32, (span_len, head_dim), 0) < live_rows

    def finish():
        tops = jnp.zeros((span_len, head_dim), jnp.float32)
        totals = jnp.ones((span_len, head_dim), jnp.float32)
        for head in range(kv_local * per_head):
            total = acc_ref[head, :, head_dim:]
            inverse = pl.reciprocal(total, approx=True)
            mixed = acc_ref[head, :, :head_dim] * (inverse * (2.0 - total * inverse))
            if last_call:
                mixed = jnp.where(live, mixed, 0.0)
            else:
                tops = jnp.where(lane_ids == head, max_ref[head], tops)
                totals = jnp.where(lane_ids == head, total, totals)
            out_ref[0, :, lanes_of(head)] = mixed.astype(jnp.bfloat16)
        if not last_call:
            next_total_ref[0] = tops + jnp.log(totals) * LOG2E

    if first_call:
        over = lax.rem(count, STEP)
        for n in range(STEP):
            @pl.when(over == n)
            def _():
                attend([list_ref[m] for m in range(n)] + [own], "start")

        rest(over)
        finish()
    else:
        over = lax.rem(count + STEP - 1, STEP) + 1

        @pl.when(count == 0)
        def _():
            if last_call:
                for head in range(kv_local * per_head):
                    given = mixed_ref[0, :, lanes_of(head)]
                    out_ref[0, :, lanes_of(head)] = jnp.where(live, given, jnp.zeros_like(given))
            else:
                out_ref[...] = mixed_ref[...]
                next_total_ref[...] = total_ref[...]

        @pl.when(count > 0)
        def _():
            for n in range(1, STEP + 1):
                @pl.when(over == n)
                def _():
                    attend([list_ref[m] for m in range(n)], "given")

            rest(over)
            finish()

def after(values, earlier):
    return lax.optimization_barrier((list(values), list(earlier)))[0]


def move_pages(kv_new, kv_local, attend):
    inst_size = lax.axis_size("inst")
    tp_size = lax.axis_size("tp")
    inst = lax.axis_index("inst")
    tp = lax.axis_index("tp")
    slot_count, kv_heads = kv_new.shape[:2]
    sources = [list(range(inst_size))]
    hops = [(0, kv_new)]
    parts = []

    def along(x, pairs):
        return lax.ppermute(x, "inst", pairs)

    def exchange(hop, x):
        found = []
        for j in range(tp_size):
            head = ((tp ^ j) * kv_heads) // tp_size
            sent = lax.dynamic_slice_in_dim(x, head, kv_local, 1)
            if j:
                sent = lax.ppermute(sent, "tp", [(t, t ^ j) for t in range(tp_size)])
            found.append(((hop, j), sent))
        parts.extend(found)
        return [x for _, x in found]

    if inst_size != 4:
        exchange(0, kv_new)
        for s in range(1, inst_size):
            sources.append([(i - s) % inst_size for i in range(inst_size)])
            pairs = [(i, (i + s) % inst_size) for i in range(inst_size)]
            hops.append((s, along(kv_new, pairs)))
            exchange(s, hops[-1][1])
        return [], (list(range(inst_size)), parts, sources), hops

    sources += [[1, 0, 3, 2], [-1, 2, 1, -1], [-1, 3, 0, -1], [2, -1, -1, 1], [3, -1, -1, 0]]
    sources += [[2, 2, 1, 1], [3, 3, 0, 0]]
    middle = (inst == 1) | (inst == 2)
    outer = along(kv_new, [(0, 1), (1, 0), (2, 3), (3, 2)])
    inner = along(kv_new, [(1, 2), (2, 1)])
    waiting = exchange(0, kv_new)
    outer_on, inner_on = after([outer, inner], waiting)
    crossed = along(outer_on, [(1, 2), (2, 1)])
    inner_ends = along(inner_on, [(1, 0), (2, 3)])
    waiting = exchange(1, outer_on)
    crossed_ends = along(after([crossed], waiting)[0], [(1, 0), (2, 3)])
    first_parts = parts[:]
    second = exchange(6, jnp.where(middle, inner, inner_ends))
    second_parts = parts[len(first_parts):]
    state = attend([0, 1], first_parts, sources, later=[second[0], crossed])
    third = exchange(7, after([jnp.where(middle, crossed, crossed_ends)], second)[0])
    third_parts = parts[len(first_parts) + len(second_parts):]
    state = attend([6], second_parts, sources, state=state, later=third[:1])
    hops += enumerate((outer, inner, crossed, inner_ends, crossed_ends), 1)
    return state, ([7], third_parts, sources), hops


def body(queries, kv_new, prompt_spans, prompt_tail, span_plan, decode_owner):
    tp_size = lax.axis_size("tp")
    inst_size = lax.axis_size("inst")
    tp_index = lax.axis_index("tp")
    inst_index = lax.axis_index("inst")
    slot_count, span_len, row_width = queries.shape
    kv_heads, slice_len, width = kv_new.shape[1:]
    head_dim = width // 2
    local_heads = row_width // head_dim
    kv_local = max(1, kv_heads // tp_size)
    per_head = local_heads // kv_local
    span_total = slot_count * inst_size
    longest = span_total // 2
    anywhere = pl.BlockSpec(memory_space=pl.ANY)
    by_slot = pl.BlockSpec((1, span_len, row_width), lambda i, *_: (i, 0, 0))
    rows = per_head * span_len
    total_spec = pl.BlockSpec((1, span_len, head_dim), lambda i, *_: (i, 0, 0))
    state_specs = [by_slot, total_spec]
    work = slot_count * 4 * local_heads * span_len * span_len

    def numbers_of(sources):
        own_sources = lax.dynamic_index_in_dim(
            jnp.asarray(sources, jnp.int32), inst_index, 1, False
        )
        return jnp.concatenate([
            prompt_spans, prompt_tail, decode_owner, span_plan,
            jnp.stack([inst_index, tp_index]).astype(jnp.int32), own_sources,
        ])

    def attend(covers, parts, sources, state=(), later=(), last_call=False):
        first_call = not state
        numbers = numbers_of(sources)
        kernel = functools.partial(
            attend_kernel,
            covers=covers,
            parts=[name for name, _ in parts],
            later=len(later),
            first_call=first_call,
            last_call=last_call,
            inst_size=inst_size,
            tp_size=tp_size,
            kv_local=kv_local,
            per_head=per_head,
            head_dim=head_dim,
            span_len=span_len,
            slot_count=slot_count,
            longest=longest,
            prompt_count=prompt_spans.shape[0],
        )
        scratch = [
            pltpu.SMEM((span_total,), jnp.int32),
            pltpu.SMEM((span_total,), jnp.int32),
            pltpu.VMEM((span_total, kv_local, span_len, width), jnp.bfloat16),
            pltpu.VMEM((kv_local, rows, STEP * span_len), jnp.float32),
            pltpu.VMEM((kv_local, rows, STEP * span_len), jnp.bfloat16),
            pltpu.VMEM((local_heads, span_len, 2 * head_dim), jnp.float32),
            pltpu.VMEM((local_heads, span_len, head_dim), jnp.float32),
            pltpu.SemaphoreType.DMA((len(parts),)),
        ]
        out_specs = [by_slot] if last_call else state_specs
        out_shape = [
            jax.ShapeDtypeStruct(queries.shape, jnp.bfloat16),
            jax.ShapeDtypeStruct((slot_count, span_len, head_dim), jnp.float32),
        ][:len(out_specs)]
        return pl.pallas_call(
            kernel,
            grid_spec=pltpu.PrefetchScalarGridSpec(
                num_scalar_prefetch=1,
                grid=(slot_count,),
                in_specs=[by_slot] + (state_specs if state else [])
                + [anywhere] * (len(parts) + len(later)),
                out_specs=out_specs,
                scratch_shapes=scratch,
            ),
            out_shape=out_shape,
            cost_estimate=pl.CostEstimate(
                flops=4 * work * head_dim, bytes_accessed=8 << 20, transcendentals=work
            ),
            compiler_params=pltpu.CompilerParams(vmem_limit_bytes=VMEM_BYTES),
        )(
            numbers, queries, *state, *[x for _, x in parts], *later,
        )

    state, left, hops = move_pages(kv_new, kv_local, attend)
    page_shape = (kv_heads, slice_len, width)
    owner_cache = pl.pallas_call(
        functools.partial(
            place_kernel,
            hops=[name for name, _ in hops],
            slot_count=slot_count,
            span_total=span_total,
            longest=longest,
            prompt_count=prompt_spans.shape[0],
        ),
        grid_spec=pltpu.PrefetchScalarGridSpec(
            num_scalar_prefetch=1,
            grid=(1,),
            in_specs=[anywhere] * len(hops),
            out_specs=anywhere,
            scratch_shapes=[
                pltpu.SMEM((span_total,), jnp.int32),
                pltpu.VMEM((longest,) + page_shape, jnp.bfloat16),
                pltpu.SemaphoreType.DMA((longest,)),
                pltpu.SemaphoreType.DMA,
            ],
        ),
        out_shape=jax.ShapeDtypeStruct((longest,) + page_shape, jnp.bfloat16),
        cost_estimate=pl.CostEstimate(flops=0, bytes_accessed=8 << 20, transcendentals=0),
    )(numbers_of(left[2]), *[x for _, x in hops])
    (attended,) = attend(*left, state, last_call=True)
    return attended, owner_cache


def solution(mesh):
    placed = (
        P(("groups", "inst"), None, "tp"),
        P(("groups", "inst"), None, "tp", None),
        P("groups"),
        P("groups"),
        P("groups"),
        P("groups"),
    )
    return jax.shard_map(
        body,
        mesh=mesh,
        in_specs=placed,
        out_specs=(P(("groups", "inst"), None, "tp"), P(("groups", "inst"), None, "tp", None)),
        check_vma=False,
    )
```

```python
import functools
import math

import jax
import jax.numpy as jnp
from jax import lax
from jax.experimental import pallas as pl
from jax.experimental.pallas import tpu as pltpu
from jax.sharding import PartitionSpec as P

HEADS = 64
KVH = 8
LOG2E = 1.4426950408889634
STEP = 4
VMEM_BYTES = 18 << 20


class Part:
    def __init__(self, ref, start):
        self.ref, self.start = ref, start

    def __getitem__(self, at):
        return self.ref[self.start + at]


def place_kernel(numbers_ref, *refs, hops, slot_count, span_total, longest, prompt_count):
    hop_refs = refs[:len(hops)]
    cache_ref, place_ref, stage_ref, sems, out_sem = refs[len(hops):]
    spans_ref = Part(numbers_ref, 0)
    owner_ref = Part(numbers_ref, 2 * prompt_count)
    plan_ref = Part(numbers_ref, 3 * prompt_count)
    place_at_ref = Part(numbers_ref, 3 * prompt_count + span_total)
    inst = place_at_ref[0]
    first, count, start = jnp.int32(0), jnp.int32(0), jnp.int32(0)
    for p in range(prompt_count):
        hit = owner_ref[p] == inst
        first = jnp.where(hit, start, first)
        count = jnp.where(hit, spans_ref[p], count)
        start = start + spans_ref[p]

    def put(g, unused):
        place_ref[plan_ref[g]] = g
        return unused

    lax.fori_loop(0, span_total, put, 0)

    def copies(act, fill):
        def row(r, unused):
            page = place_ref[jnp.minimum(first + r, span_total - 1)]
            for n, hop in enumerate(hops):
                source = place_at_ref[2 + hop]
                slot = page - source * slot_count

                @pl.when((r < count) & (source >= 0) & (slot >= 0) & (slot < slot_count))
                def _():
                    act(pltpu.make_async_copy(hop_refs[n].at[slot], stage_ref.at[r], sems.at[r]))

            if fill:
                @pl.when(r >= count)
                def _():
                    stage_ref[r] = jnp.zeros(stage_ref.shape[1:], stage_ref.dtype)

            return unused

        lax.fori_loop(0, longest, row, 0)

    copies(lambda copy: copy.start(), True)
    copies(lambda copy: copy.wait(), False)
    out = pltpu.make_async_copy(stage_ref, cache_ref, out_sem)
    out.start()
    out.wait()


def attend_kernel(
    numbers_ref, *refs,
    covers, parts, later, first_call, last_call,
    inst_size, tp_size, kv_local, per_head, head_dim, span_len, slot_count, longest, prompt_count,
):
    refs = list(refs)

    def take(count):
        taken = refs[:count]
        del refs[:count]
        return taken

    (q_ref,) = take(1)
    mixed_ref, total_ref = (None, None) if first_call else take(2)
    part_refs = take(len(parts))
    take(later)
    (out_ref,) = take(1)
    if not last_call:
        (next_total_ref,) = take(1)
    place_ref, list_ref, kv_ref, s_ref, p_ref, acc_ref, max_ref, part_sems = take(8)
    step = pl.program_id(0)
    span_total = slot_count * inst_size
    spans_ref = Part(numbers_ref, 0)
    tail_ref = Part(numbers_ref, prompt_count)
    owner_ref = Part(numbers_ref, 2 * prompt_count)
    plan_ref = Part(numbers_ref, 3 * prompt_count)
    place_at_ref = Part(numbers_ref, 3 * prompt_count + span_total)
    inst = place_at_ref[0]
    tp = place_at_ref[1]
    slice_len = span_len // tp_size
    most = min(longest, len(covers) * slot_count)
    scale = LOG2E / math.sqrt(head_dim)

    def part_copies(act):
        for n, (hop, j) in enumerate(parts):
            slots = pl.ds(place_at_ref[2 + hop] * slot_count, slot_count)
            at = pl.ds(pl.multiple_of((tp ^ j) * slice_len, slice_len), slice_len)
            act(pltpu.make_async_copy(part_refs[n], kv_ref.at[slots, :, at], part_sems.at[n]))

    @pl.when(step == 0)
    def _():
        part_copies(lambda copy: copy.start())

        def put(g, unused):
            place_ref[plan_ref[g]] = g
            return unused

        lax.fori_loop(0, span_total, put, 0)
        part_copies(lambda copy: copy.wait())

    own = inst * slot_count + step
    span = plan_ref[own]
    first = jnp.int32(0)
    end = jnp.int32(0)
    length = jnp.int32(0)
    for p in range(prompt_count):
        start = end
        end = end + spans_ref[p]
        inside = (span >= start) & (span < end)
        first = jnp.where(inside, start, first)
        length = jnp.where(inside, (spans_ref[p] - 1) * span_len + tail_ref[p], length)
    live_rows = length - (span - first) * span_len

    def look(k, count):
        page = place_ref[k]
        source = page // slot_count
        covered = jnp.bool_(False)
        for hop in covers:
            covered = covered | (place_at_ref[2 + hop] == source)
        list_ref[count] = page
        return count + covered.astype(jnp.int32)

    count = lax.fori_loop(first, span, look, jnp.int32(0))

    ones = jnp.ones((span_len, head_dim), jnp.bfloat16)
    row_ids = lax.broadcasted_iota(jnp.int32, (span_len, span_len), 0)
    col_ids = lax.broadcasted_iota(jnp.int32, (span_len, span_len), 1)
    causal = row_ids >= col_ids
    lane_ids = lax.broadcasted_iota(jnp.int32, (span_len, head_dim), 1)
    def lanes_of(head):
        return slice(head * head_dim, (head + 1) * head_dim)

    def rows_of(h):
        return slice(h * span_len, (h + 1) * span_len)

    single = most <= STEP
    live = lax.broadcasted_iota(jnp.int32, (span_len, head_dim), 0) < live_rows

    def put_out(head, total):
        inverse = pl.reciprocal(total[:, head_dim:], approx=True)
        inverse = inverse * (2.0 - total[:, head_dim:] * inverse)
        mixed = (total[:, :head_dim] * inverse).astype(jnp.bfloat16)
        if last_call:
            mixed = jnp.where(live, mixed, jnp.zeros_like(mixed))
        out_ref[0, :, lanes_of(head)] = mixed

    def put_totals(tops, totals):
        if last_call:
            return
        top, total = tops[0], totals[0]
        for head in range(1, kv_local * per_head):
            top = jnp.where(lane_ids == head, tops[head], top)
            total = jnp.where(lane_ids == head, totals[head], total)
        next_total_ref[0] = top + jnp.log(total) * LOG2E

    def attend(pages, since):
        wide = len(pages) * span_len

        def cols_of(n):
            return slice(n * span_len, (n + 1) * span_len)

        for g in range(kv_local):
            q = jnp.concatenate(
                [q_ref[0, :, lanes_of(g * per_head + h)] for h in range(per_head)], axis=0
            )
            for n in range(0, len(pages), 2):
                some = pages[n:n + 2]
                keys = jnp.concatenate([kv_ref[p, g, :, :head_dim] for p in some], axis=0)
                s = lax.dot_general(
                    q, keys, (((1,), (1,)), ((), ())), preferred_element_type=jnp.float32
                )
                for m in range(len(some)):
                    if since == "start" and n + m == len(pages) - 1:
                        for h in range(per_head):
                            s_ref[g, rows_of(h), cols_of(n + m)] = jnp.where(
                                causal, s[rows_of(h), cols_of(m)], -1e30
                            )
                    else:
                        s_ref[g, :, cols_of(n + m)] = s[:, cols_of(m)]
        tops, totals = [], []
        for g in range(kv_local):
            rescales = []
            for h in range(per_head):
                head = g * per_head + h
                top = s_ref[g, rows_of(h), cols_of(0)]
                for n in range(1, len(pages)):
                    top = jnp.maximum(top, s_ref[g, rows_of(h), cols_of(n)])
                top = jnp.broadcast_to(
                    jnp.max(top, axis=1, keepdims=True) * scale, (span_len, head_dim)
                )
                if since != "start":
                    if since == "given":
                        old = jnp.broadcast_to(
                            total_ref[0, :, head:head + 1], (span_len, head_dim)
                        )
                    else:
                        old = max_ref[head]
                    top = jnp.maximum(old, top)
                    rescales.append(jnp.exp2(old - top))
                if single:
                    tops.append(top)
                else:
                    max_ref[head] = top
                for n in range(len(pages)):
                    p_ref[g, rows_of(h), cols_of(n)] = jnp.exp2(
                        s_ref[g, rows_of(h), cols_of(n)] * scale - top
                    ).astype(jnp.bfloat16)
            values = jnp.concatenate(
                [
                    jnp.concatenate([kv_ref[page, g, :, head_dim:], ones], axis=1)
                    for page in pages
                ],
                axis=0,
            )
            mixed = jnp.dot(p_ref[g, :, :wide], values, preferred_element_type=jnp.float32)
            for h in range(per_head):
                head = g * per_head + h
                new = mixed[rows_of(h)]
                if since == "given":
                    given = mixed_ref[0, :, lanes_of(head)].astype(jnp.float32)
                    new = new + jnp.concatenate([given * rescales[h], rescales[h]], axis=1)
                elif since == "here":
                    new = new + acc_ref[head] * jnp.concatenate([rescales[h]] * 2, axis=1)
                if single:
                    put_out(head, new)
                    totals.append(new[:, head_dim:])
                else:
                    acc_ref[head] = new
        if single:
            put_totals(tops, totals)

    def rest(begin):
        if single:
            return

        def block(j, unused):
            at = begin + STEP * j
            attend([list_ref[at + n] for n in range(STEP)], "here")
            return unused

        lax.fori_loop(0, (count - begin) // STEP, block, 0)

    def finish():
        if single:
            return
        heads = range(kv_local * per_head)
        for head in heads:
            put_out(head, acc_ref[head])
        put_totals([max_ref[head] for head in heads], [acc_ref[head, :, head_dim:] for head in heads])

    if first_call:
        over = lax.rem(count, STEP)
        for n in range(STEP):
            @pl.when(over == n)
            def _():
                attend([list_ref[m] for m in range(n)] + [own], "start")

        rest(over)
        finish()
    else:
        over = lax.rem(count + STEP - 1, STEP) + 1

        @pl.when(count == 0)
        def _():
            if last_call:
                for head in range(kv_local * per_head):
                    given = mixed_ref[0, :, lanes_of(head)]
                    out_ref[0, :, lanes_of(head)] = jnp.where(live, given, jnp.zeros_like(given))
            else:
                out_ref[...] = mixed_ref[...]
                next_total_ref[...] = total_ref[...]

        @pl.when(count > 0)
        def _():
            for n in range(1, STEP + 1):
                @pl.when(over == n)
                def _():
                    attend([list_ref[m] for m in range(n)], "given")

            rest(over)
            finish()

def after(values, earlier):
    return lax.optimization_barrier((list(values), list(earlier)))[0]


def move_pages(kv_new, kv_local, attend):
    inst_size = lax.axis_size("inst")
    tp_size = lax.axis_size("tp")
    inst = lax.axis_index("inst")
    tp = lax.axis_index("tp")
    slot_count, kv_heads = kv_new.shape[:2]
    sources = [list(range(inst_size))]
    hops = [(0, kv_new)]
    parts = []

    def along(x, pairs):
        return lax.ppermute(x, "inst", pairs)

    def exchange(hop, x):
        found = []
        for j in range(tp_size):
            head = ((tp ^ j) * kv_heads) // tp_size
            sent = lax.dynamic_slice_in_dim(x, head, kv_local, 1)
            if j:
                sent = lax.ppermute(sent, "tp", [(t, t ^ j) for t in range(tp_size)])
            found.append(((hop, j), sent))
        parts.extend(found)
        return [x for _, x in found]

    if inst_size != 4:
        exchange(0, kv_new)
        for s in range(1, inst_size):
            sources.append([(i - s) % inst_size for i in range(inst_size)])
            pairs = [(i, (i + s) % inst_size) for i in range(inst_size)]
            hops.append((s, along(kv_new, pairs)))
            exchange(s, hops[-1][1])
        return [], (list(range(inst_size)), parts, sources), hops

    sources += [[1, 0, 3, 2], [-1, 2, 1, -1], [-1, 3, 0, -1], [2, -1, -1, 1], [3, -1, -1, 0]]
    sources += [[2, 2, 1, 1], [3, 3, 0, 0]]
    middle = (inst == 1) | (inst == 2)
    outer = along(kv_new, [(0, 1), (1, 0), (2, 3), (3, 2)])
    inner = along(kv_new, [(1, 2), (2, 1)])
    waiting = exchange(0, kv_new)
    outer_on, inner_on = after([outer, inner], waiting)
    crossed = along(outer_on, [(1, 2), (2, 1)])
    inner_ends = along(inner_on, [(1, 0), (2, 3)])
    own_parts = parts[:]
    waiting = exchange(1, outer_on)
    first_parts = parts[len(own_parts):]
    state = attend([0], own_parts, sources, later=waiting[:1])
    crossed_ends = along(after([crossed], waiting)[0], [(1, 0), (2, 3)])
    second = exchange(6, jnp.where(middle, inner, inner_ends))
    second_parts = parts[2 * tp_size:]
    state = attend([1], first_parts, sources, state=state, later=[second[0], crossed])
    third = exchange(7, after([jnp.where(middle, crossed, crossed_ends)], second)[0])
    third_parts = parts[3 * tp_size:]
    state = attend([6], second_parts, sources, state=state)
    hops += enumerate((outer, inner, crossed, inner_ends, crossed_ends), 1)
    return state, ([7], third_parts, sources), hops


def body(queries, kv_new, prompt_spans, prompt_tail, span_plan, decode_owner):
    tp_size = lax.axis_size("tp")
    inst_size = lax.axis_size("inst")
    tp_index = lax.axis_index("tp")
    inst_index = lax.axis_index("inst")
    slot_count, span_len, row_width = queries.shape
    kv_heads, slice_len, width = kv_new.shape[1:]
    head_dim = width // 2
    local_heads = row_width // head_dim
    kv_local = max(1, kv_heads // tp_size)
    per_head = local_heads // kv_local
    span_total = slot_count * inst_size
    longest = span_total // 2
    anywhere = pl.BlockSpec(memory_space=pl.ANY)
    by_slot = pl.BlockSpec((1, span_len, row_width), lambda i, *_: (i, 0, 0))
    rows = per_head * span_len
    total_spec = pl.BlockSpec((1, span_len, head_dim), lambda i, *_: (i, 0, 0))
    state_specs = [by_slot, total_spec]
    work = slot_count * 4 * local_heads * span_len * span_len

    def numbers_of(sources):
        own_sources = lax.dynamic_index_in_dim(
            jnp.asarray(sources, jnp.int32), inst_index, 1, False
        )
        return jnp.concatenate([
            prompt_spans, prompt_tail, decode_owner, span_plan,
            jnp.stack([inst_index, tp_index]).astype(jnp.int32), own_sources,
        ])

    def attend(covers, parts, sources, state=(), later=(), last_call=False):
        first_call = not state
        numbers = numbers_of(sources)
        kernel = functools.partial(
            attend_kernel,
            covers=covers,
            parts=[name for name, _ in parts],
            later=len(later),
            first_call=first_call,
            last_call=last_call,
            inst_size=inst_size,
            tp_size=tp_size,
            kv_local=kv_local,
            per_head=per_head,
            head_dim=head_dim,
            span_len=span_len,
            slot_count=slot_count,
            longest=longest,
            prompt_count=prompt_spans.shape[0],
        )
        single = min(longest, len(covers) * slot_count) <= STEP
        kept = (1, 8) if single else (local_heads, span_len)
        scratch = [
            pltpu.SMEM((span_total,), jnp.int32),
            pltpu.SMEM((span_total,), jnp.int32),
            pltpu.VMEM((span_total, kv_local, span_len, width), jnp.bfloat16),
            pltpu.VMEM((kv_local, rows, STEP * span_len), jnp.float32),
            pltpu.VMEM((kv_local, rows, STEP * span_len), jnp.bfloat16),
            pltpu.VMEM(kept + (2 * head_dim,), jnp.float32),
            pltpu.VMEM(kept + (head_dim,), jnp.float32),
            pltpu.SemaphoreType.DMA((len(parts),)),
        ]
        out_specs = [by_slot] if last_call else state_specs
        out_shape = [
            jax.ShapeDtypeStruct(queries.shape, jnp.bfloat16),
            jax.ShapeDtypeStruct((slot_count, span_len, head_dim), jnp.float32),
        ][:len(out_specs)]
        return pl.pallas_call(
            kernel,
            grid_spec=pltpu.PrefetchScalarGridSpec(
                num_scalar_prefetch=1,
                grid=(slot_count,),
                in_specs=[by_slot] + (state_specs if state else [])
                + [anywhere] * (len(parts) + len(later)),
                out_specs=out_specs,
                scratch_shapes=scratch,
            ),
            out_shape=out_shape,
            cost_estimate=pl.CostEstimate(
                flops=4 * work * head_dim, bytes_accessed=8 << 20, transcendentals=work
            ),
            compiler_params=pltpu.CompilerParams(vmem_limit_bytes=VMEM_BYTES),
        )(
            numbers, queries, *state, *[x for _, x in parts], *later,
        )

    state, left, hops = move_pages(kv_new, kv_local, attend)
    page_shape = (kv_heads, slice_len, width)
    owner_cache = pl.pallas_call(
        functools.partial(
            place_kernel,
            hops=[name for name, _ in hops],
            slot_count=slot_count,
            span_total=span_total,
            longest=longest,
            prompt_count=prompt_spans.shape[0],
        ),
        grid_spec=pltpu.PrefetchScalarGridSpec(
            num_scalar_prefetch=1,
            grid=(1,),
            in_specs=[anywhere] * len(hops),
            out_specs=anywhere,
            scratch_shapes=[
                pltpu.SMEM((span_total,), jnp.int32),
                pltpu.VMEM((longest,) + page_shape, jnp.bfloat16),
                pltpu.SemaphoreType.DMA((longest,)),
                pltpu.SemaphoreType.DMA,
            ],
        ),
        out_shape=jax.ShapeDtypeStruct((longest,) + page_shape, jnp.bfloat16),
        cost_estimate=pl.CostEstimate(flops=0, bytes_accessed=8 << 20, transcendentals=0),
    )(numbers_of(left[2]), *[x for _, x in hops])
    (attended,) = attend(*left, state, last_call=True)
    return attended, owner_cache


def solution(mesh):
    placed = (
        P(("groups", "inst"), None, "tp"),
        P(("groups", "inst"), None, "tp", None),
        P("groups"),
        P("groups"),
        P("groups"),
        P("groups"),
    )
    return jax.shard_map(
        body,
        mesh=mesh,
        in_specs=placed,
        out_specs=(P(("groups", "inst"), None, "tp"), P(("groups", "inst"), None, "tp", None)),
        check_vma=False,
    )
```

```python
import functools
import math

import jax
import jax.numpy as jnp
from jax import lax
from jax.experimental import pallas as pl
from jax.experimental.pallas import tpu as pltpu
from jax.sharding import PartitionSpec as P

HEADS = 64
KVH = 8
LOG2E = 1.4426950408889634
STEP = 4
VMEM_BYTES = 18 << 20


def source_of(sources, hop, inst):
    found = jnp.int32(sources[hop][0])
    for i in range(1, len(sources[hop])):
        found = jnp.where(inst == i, sources[hop][i], found)
    return found


def place_kernel(
    spans_ref, owner_ref, plan_ref, *refs, hops, sources, slot_count, span_total, longest,
):
    hop_refs = refs[:len(hops)]
    cache_ref, place_ref, stage_ref, sems, out_sem = refs[len(hops):]
    inst = lax.axis_index("inst")
    first, count, start = jnp.int32(0), jnp.int32(0), jnp.int32(0)
    for p in range(spans_ref.shape[0]):
        hit = owner_ref[p] == inst
        first = jnp.where(hit, start, first)
        count = jnp.where(hit, spans_ref[p], count)
        start = start + spans_ref[p]

    def put(g, unused):
        place_ref[plan_ref[g]] = g
        return unused

    lax.fori_loop(0, span_total, put, 0)

    def copies(act, fill):
        def row(r, unused):
            page = place_ref[jnp.minimum(first + r, span_total - 1)]
            for n, hop in enumerate(hops):
                source = source_of(sources, hop, inst)
                slot = page - source * slot_count

                @pl.when((r < count) & (source >= 0) & (slot >= 0) & (slot < slot_count))
                def _():
                    act(pltpu.make_async_copy(hop_refs[n].at[slot], stage_ref.at[r], sems.at[r]))

            if fill:
                @pl.when(r >= count)
                def _():
                    stage_ref[r] = jnp.zeros(stage_ref.shape[1:], stage_ref.dtype)

            return unused

        lax.fori_loop(0, longest, row, 0)

    copies(lambda copy: copy.start(), True)
    copies(lambda copy: copy.wait(), False)
    out = pltpu.make_async_copy(stage_ref, cache_ref, out_sem)
    out.start()
    out.wait()


def attend_kernel(
    spans_ref, tail_ref, plan_ref, *refs,
    covers, sources, parts, later, first_call, last_call,
    inst_size, tp_size, kv_local, per_head, head_dim, span_len, slot_count, longest,
):
    refs = list(refs)

    def take(count):
        taken = refs[:count]
        del refs[:count]
        return taken

    (q_ref,) = take(1)
    mixed_ref, total_ref = (None, None) if first_call else take(2)
    part_refs = take(len(parts))
    take(later)
    (out_ref,) = take(1)
    if not last_call:
        (next_total_ref,) = take(1)
    place_ref, list_ref, kv_ref, s_ref, p_ref, acc_ref, max_ref, part_sems = take(8)
    step = pl.program_id(0)
    span_total = slot_count * inst_size
    prompt_count = spans_ref.shape[0]
    inst = lax.axis_index("inst")
    tp = lax.axis_index("tp")
    slice_len = span_len // tp_size
    most = min(longest, len(covers) * slot_count)
    scale = LOG2E / math.sqrt(head_dim)

    def part_copies(act):
        for n, (hop, j) in enumerate(parts):
            slots = pl.ds(source_of(sources, hop, inst) * slot_count, slot_count)
            at = pl.ds(pl.multiple_of((tp ^ j) * slice_len, slice_len), slice_len)
            act(pltpu.make_async_copy(part_refs[n], kv_ref.at[slots, :, at], part_sems.at[n]))

    @pl.when(step == 0)
    def _():
        part_copies(lambda copy: copy.start())

        def put(g, unused):
            place_ref[plan_ref[g]] = g
            return unused

        lax.fori_loop(0, span_total, put, 0)
        part_copies(lambda copy: copy.wait())

    own = inst * slot_count + step
    span = plan_ref[own]
    first = jnp.int32(0)
    end = jnp.int32(0)
    length = jnp.int32(0)
    for p in range(prompt_count):
        start = end
        end = end + spans_ref[p]
        inside = (span >= start) & (span < end)
        first = jnp.where(inside, start, first)
        length = jnp.where(inside, (spans_ref[p] - 1) * span_len + tail_ref[p], length)
    live_rows = length - (span - first) * span_len

    def look(k, count):
        page = place_ref[k]
        source = page // slot_count
        covered = jnp.bool_(False)
        for hop in covers:
            covered = covered | (source_of(sources, hop, inst) == source)
        list_ref[count] = page
        return count + covered.astype(jnp.int32)

    count = lax.fori_loop(first, span, look, jnp.int32(0))

    ones = jnp.ones((span_len, head_dim), jnp.bfloat16)
    row_ids = lax.broadcasted_iota(jnp.int32, (span_len, span_len), 0)
    col_ids = lax.broadcasted_iota(jnp.int32, (span_len, span_len), 1)
    causal = row_ids >= col_ids
    lane_ids = lax.broadcasted_iota(jnp.int32, (span_len, head_dim), 1)
    def lanes_of(head):
        return slice(head * head_dim, (head + 1) * head_dim)

    def rows_of(h):
        return slice(h * span_len, (h + 1) * span_len)

    single = most <= STEP
    live = lax.broadcasted_iota(jnp.int32, (span_len, head_dim), 0) < live_rows

    def put_out(head, total):
        inverse = pl.reciprocal(total[:, head_dim:], approx=True)
        inverse = inverse * (2.0 - total[:, head_dim:] * inverse)
        mixed = (total[:, :head_dim] * inverse).astype(jnp.bfloat16)
        if last_call:
            mixed = jnp.where(live, mixed, jnp.zeros_like(mixed))
        out_ref[0, :, lanes_of(head)] = mixed

    def put_totals(tops, totals):
        if last_call:
            return
        top, total = tops[0], totals[0]
        for head in range(1, kv_local * per_head):
            top = jnp.where(lane_ids == head, tops[head], top)
            total = jnp.where(lane_ids == head, totals[head], total)
        next_total_ref[0] = top + jnp.log(total) * LOG2E

    def attend(pages, since):
        wide = len(pages) * span_len

        def cols_of(n):
            return slice(n * span_len, (n + 1) * span_len)

        for g in range(kv_local):
            q = jnp.concatenate(
                [q_ref[0, :, lanes_of(g * per_head + h)] for h in range(per_head)], axis=0
            )
            for n in range(0, len(pages), 2):
                some = pages[n:n + 2]
                keys = jnp.concatenate([kv_ref[p, g, :, :head_dim] for p in some], axis=0)
                s = lax.dot_general(
                    q, keys, (((1,), (1,)), ((), ())), preferred_element_type=jnp.float32
                )
                for m in range(len(some)):
                    if since == "start" and n + m == len(pages) - 1:
                        for h in range(per_head):
                            s_ref[g, rows_of(h), cols_of(n + m)] = jnp.where(
                                causal, s[rows_of(h), cols_of(m)], -1e30
                            )
                    else:
                        s_ref[g, :, cols_of(n + m)] = s[:, cols_of(m)]
        tops, totals = [], []
        for g in range(kv_local):
            rescales = []
            for h in range(per_head):
                head = g * per_head + h
                top = s_ref[g, rows_of(h), cols_of(0)]
                for n in range(1, len(pages)):
                    top = jnp.maximum(top, s_ref[g, rows_of(h), cols_of(n)])
                top = jnp.broadcast_to(
                    jnp.max(top, axis=1, keepdims=True) * scale, (span_len, head_dim)
                )
                if since != "start":
                    if since == "given":
                        old = jnp.broadcast_to(
                            total_ref[0, :, head:head + 1], (span_len, head_dim)
                        )
                    else:
                        old = max_ref[head]
                    top = jnp.maximum(old, top)
                    rescales.append(jnp.exp2(old - top))
                if single:
                    tops.append(top)
                else:
                    max_ref[head] = top
                for n in range(len(pages)):
                    p_ref[g, rows_of(h), cols_of(n)] = jnp.exp2(
                        s_ref[g, rows_of(h), cols_of(n)] * scale - top
                    ).astype(jnp.bfloat16)
            values = jnp.concatenate(
                [
                    jnp.concatenate([kv_ref[page, g, :, head_dim:], ones], axis=1)
                    for page in pages
                ],
                axis=0,
            )
            mixed = jnp.dot(p_ref[g, :, :wide], values, preferred_element_type=jnp.float32)
            for h in range(per_head):
                head = g * per_head + h
                new = mixed[rows_of(h)]
                if since == "given":
                    given = mixed_ref[0, :, lanes_of(head)].astype(jnp.float32)
                    new = new + jnp.concatenate([given * rescales[h], rescales[h]], axis=1)
                elif since == "here":
                    new = new + acc_ref[head] * jnp.concatenate([rescales[h]] * 2, axis=1)
                if single:
                    put_out(head, new)
                    totals.append(new[:, head_dim:])
                else:
                    acc_ref[head] = new
        if single:
            put_totals(tops, totals)

    def rest(begin):
        if single:
            return

        def block(j, unused):
            at = begin + STEP * j
            attend([list_ref[at + n] for n in range(STEP)], "here")
            return unused

        lax.fori_loop(0, (count - begin) // STEP, block, 0)

    def finish():
        if single:
            return
        heads = range(kv_local * per_head)
        for head in heads:
            put_out(head, acc_ref[head])
        put_totals([max_ref[head] for head in heads], [acc_ref[head, :, head_dim:] for head in heads])

    if first_call:
        over = lax.rem(count, STEP)
        for n in range(STEP):
            @pl.when(over == n)
            def _():
                attend([list_ref[m] for m in range(n)] + [own], "start")

        rest(over)
        finish()
    else:
        over = lax.rem(count + STEP - 1, STEP) + 1

        @pl.when(count == 0)
        def _():
            if last_call:
                for head in range(kv_local * per_head):
                    given = mixed_ref[0, :, lanes_of(head)]
                    out_ref[0, :, lanes_of(head)] = jnp.where(live, given, jnp.zeros_like(given))
            else:
                out_ref[...] = mixed_ref[...]
                next_total_ref[...] = total_ref[...]

        @pl.when(count > 0)
        def _():
            for n in range(1, STEP + 1):
                @pl.when(over == n)
                def _():
                    attend([list_ref[m] for m in range(n)], "given")

            rest(over)
            finish()

def after(values, earlier):
    return lax.optimization_barrier((list(values), list(earlier)))[0]


def move_pages(kv_new, kv_local, attend):
    inst_size = lax.axis_size("inst")
    tp_size = lax.axis_size("tp")
    inst = lax.axis_index("inst")
    tp = lax.axis_index("tp")
    slot_count, kv_heads = kv_new.shape[:2]
    sources = [list(range(inst_size))]
    hops = [(0, kv_new)]
    parts = []

    def along(x, pairs):
        return lax.ppermute(x, "inst", pairs)

    def exchange(hop, x):
        found = []
        for j in range(tp_size):
            head = ((tp ^ j) * kv_heads) // tp_size
            sent = lax.dynamic_slice_in_dim(x, head, kv_local, 1)
            if j:
                sent = lax.ppermute(sent, "tp", [(t, t ^ j) for t in range(tp_size)])
            found.append(((hop, j), sent))
        parts.extend(found)
        return [x for _, x in found]

    if inst_size != 4:
        exchange(0, kv_new)
        for s in range(1, inst_size):
            sources.append([(i - s) % inst_size for i in range(inst_size)])
            pairs = [(i, (i + s) % inst_size) for i in range(inst_size)]
            hops.append((s, along(kv_new, pairs)))
            exchange(s, hops[-1][1])
        return [], (list(range(inst_size)), parts, sources), hops

    sources += [[1, 0, 3, 2], [-1, 2, 1, -1], [-1, 3, 0, -1], [2, -1, -1, 1], [3, -1, -1, 0]]
    sources += [[2, 2, 1, 1], [3, 3, 0, 0]]
    middle = (inst == 1) | (inst == 2)
    outer = along(kv_new, [(0, 1), (1, 0), (2, 3), (3, 2)])
    inner = along(kv_new, [(1, 2), (2, 1)])
    waiting = exchange(0, kv_new)
    outer_on, inner_on = after([outer, inner], waiting)
    crossed = along(outer_on, [(1, 2), (2, 1)])
    inner_ends = along(inner_on, [(1, 0), (2, 3)])
    own_parts = parts[:]
    waiting = exchange(1, outer_on)
    first_parts = parts[len(own_parts):]
    state = attend([0], own_parts, sources, later=waiting[:1])
    crossed_ends = along(crossed, [(1, 0), (2, 3)])
    second = exchange(6, jnp.where(middle, inner, inner_ends))
    second_parts = parts[2 * tp_size:]
    state = attend([1], first_parts, sources, state=state, later=[second[0], crossed])
    third = exchange(7, after([jnp.where(middle, crossed, crossed_ends)], second)[0])
    third_parts = parts[3 * tp_size:]
    state = attend([6], second_parts, sources, state=state)
    hops += enumerate((outer, inner, crossed, inner_ends, crossed_ends), 1)
    return state, ([7], third_parts, sources), hops


def body(queries, kv_new, prompt_spans, prompt_tail, span_plan, decode_owner):
    tp_size = lax.axis_size("tp")
    inst_size = lax.axis_size("inst")
    slot_count, span_len, row_width = queries.shape
    kv_heads, slice_len, width = kv_new.shape[1:]
    head_dim = width // 2
    local_heads = row_width // head_dim
    kv_local = max(1, kv_heads // tp_size)
    per_head = local_heads // kv_local
    span_total = slot_count * inst_size
    longest = span_total // 2
    anywhere = pl.BlockSpec(memory_space=pl.ANY)
    by_slot = pl.BlockSpec((1, span_len, row_width), lambda i, *_: (i, 0, 0))
    rows = per_head * span_len
    total_spec = pl.BlockSpec((1, span_len, head_dim), lambda i, *_: (i, 0, 0))
    state_specs = [by_slot, total_spec]
    work = slot_count * 4 * local_heads * span_len * span_len

    def attend(covers, parts, sources, state=(), later=(), last_call=False):
        first_call = not state
        kernel = functools.partial(
            attend_kernel,
            covers=covers,
            sources=sources,
            parts=[name for name, _ in parts],
            later=len(later),
            first_call=first_call,
            last_call=last_call,
            inst_size=inst_size,
            tp_size=tp_size,
            kv_local=kv_local,
            per_head=per_head,
            head_dim=head_dim,
            span_len=span_len,
            slot_count=slot_count,
            longest=longest,
        )
        single = min(longest, len(covers) * slot_count) <= STEP
        kept = (1, 8) if single else (local_heads, span_len)
        scratch = [
            pltpu.SMEM((span_total,), jnp.int32),
            pltpu.SMEM((span_total,), jnp.int32),
            pltpu.VMEM((span_total, kv_local, span_len, width), jnp.bfloat16),
            pltpu.VMEM((kv_local, rows, STEP * span_len), jnp.float32),
            pltpu.VMEM((kv_local, rows, STEP * span_len), jnp.bfloat16),
            pltpu.VMEM(kept + (2 * head_dim,), jnp.float32),
            pltpu.VMEM(kept + (head_dim,), jnp.float32),
            pltpu.SemaphoreType.DMA((len(parts),)),
        ]
        out_specs = [by_slot] if last_call else state_specs
        out_shape = [
            jax.ShapeDtypeStruct(queries.shape, jnp.bfloat16),
            jax.ShapeDtypeStruct((slot_count, span_len, head_dim), jnp.float32),
        ][:len(out_specs)]
        return pl.pallas_call(
            kernel,
            grid_spec=pltpu.PrefetchScalarGridSpec(
                num_scalar_prefetch=3,
                grid=(slot_count,),
                in_specs=[by_slot] + (state_specs if state else [])
                + [anywhere] * (len(parts) + len(later)),
                out_specs=out_specs,
                scratch_shapes=scratch,
            ),
            out_shape=out_shape,
            cost_estimate=pl.CostEstimate(
                flops=4 * work * head_dim, bytes_accessed=8 << 20, transcendentals=work
            ),
            compiler_params=pltpu.CompilerParams(vmem_limit_bytes=VMEM_BYTES),
        )(
            prompt_spans, prompt_tail, span_plan, queries,
            *state, *[x for _, x in parts], *later,
        )

    state, left, hops = move_pages(kv_new, kv_local, attend)
    page_shape = (kv_heads, slice_len, width)
    owner_cache = pl.pallas_call(
        functools.partial(
            place_kernel,
            hops=[name for name, _ in hops],
            sources=left[2],
            slot_count=slot_count,
            span_total=span_total,
            longest=longest,
        ),
        grid_spec=pltpu.PrefetchScalarGridSpec(
            num_scalar_prefetch=3,
            grid=(1,),
            in_specs=[anywhere] * len(hops),
            out_specs=anywhere,
            scratch_shapes=[
                pltpu.SMEM((span_total,), jnp.int32),
                pltpu.VMEM((longest,) + page_shape, jnp.bfloat16),
                pltpu.SemaphoreType.DMA((longest,)),
                pltpu.SemaphoreType.DMA,
            ],
        ),
        out_shape=jax.ShapeDtypeStruct((longest,) + page_shape, jnp.bfloat16),
        cost_estimate=pl.CostEstimate(flops=0, bytes_accessed=8 << 20, transcendentals=0),
        compiler_params=pltpu.CompilerParams(vmem_limit_bytes=4 << 20),
    )(prompt_spans, decode_owner, span_plan, *[x for _, x in hops])
    (attended,) = attend(*left, state, last_call=True)
    return attended, owner_cache


def solution(mesh):
    placed = (
        P(("groups", "inst"), None, "tp"),
        P(("groups", "inst"), None, "tp", None),
        P("groups"),
        P("groups"),
        P("groups"),
        P("groups"),
    )
    return jax.shard_map(
        body,
        mesh=mesh,
        in_specs=placed,
        out_specs=(P(("groups", "inst"), None, "tp"), P(("groups", "inst"), None, "tp", None)),
        check_vma=False,
    )
```

```python
import functools
import math

import jax
import jax.numpy as jnp
from jax import lax
from jax.experimental import pallas as pl
from jax.experimental.pallas import tpu as pltpu
from jax.sharding import PartitionSpec as P

HEADS = 64
KVH = 8
LOG2E = 1.4426950408889634
STEP = 4
VMEM_BYTES = 18 << 20
SMALL = 2.0 ** -60


def source_of(sources, hop, inst):
    found = jnp.int32(sources[hop][0])
    for i in range(1, len(sources[hop])):
        found = jnp.where(inst == i, sources[hop][i], found)
    return found


def place_pages(
    act, fill, spans_ref, owner_ref, place_ref, hop_refs, stage_ref, sems,
    *, hops, sources, slot_count,
):
    inst = lax.axis_index("inst")
    first, count, start = jnp.int32(0), jnp.int32(0), jnp.int32(0)
    for p in range(spans_ref.shape[0]):
        hit = owner_ref[p] == inst
        first = jnp.where(hit, start, first)
        count = jnp.where(hit, spans_ref[p], count)
        start = start + spans_ref[p]
    span_total = place_ref.shape[0]

    def row(r, unused):
        page = place_ref[jnp.minimum(first + r, span_total - 1)]
        for n, hop in enumerate(hops):
            source = source_of(sources, hop, inst)
            slot = page - source * slot_count

            @pl.when((r < count) & (source >= 0) & (slot >= 0) & (slot < slot_count))
            def _():
                act(pltpu.make_async_copy(hop_refs[n].at[slot], stage_ref.at[r], sems.at[r]))

        if fill:
            @pl.when(r >= count)
            def _():
                stage_ref[r] = jnp.zeros(stage_ref.shape[1:], stage_ref.dtype)

        return unused

    lax.fori_loop(0, stage_ref.shape[0], row, 0)


def attend_kernel(
    spans_ref, tail_ref, plan_ref, owner_ref, *refs,
    covers, sources, hops, parts, later, first_call, last_call,
    inst_size, tp_size, kv_local, per_head, head_dim, span_len, slot_count, longest,
):
    refs = list(refs)

    def take(count):
        taken = refs[:count]
        del refs[:count]
        return taken

    (q_ref,) = take(1)
    mixed_ref, total_ref = (None, None) if first_call else take(2)
    part_refs = take(len(parts))
    take(later)
    hop_refs = take(len(hops))
    if last_call:
        out_ref, cache_ref = take(2)
    else:
        out_ref, next_total_ref = take(2)
    place_ref, list_ref, kv_ref, s_ref, p_ref, acc_ref, max_ref, part_sems = take(8)
    if last_call:
        stage_ref, page_sems, cache_sem = take(3)
    step = pl.program_id(0)
    span_total = slot_count * inst_size
    prompt_count = spans_ref.shape[0]
    inst = lax.axis_index("inst")
    tp = lax.axis_index("tp")
    slice_len = span_len // tp_size
    most = min(longest, len(covers) * slot_count)
    scale = LOG2E / math.sqrt(head_dim)

    def part_copies(act):
        for n, (hop, j) in enumerate(parts):
            slots = pl.ds(source_of(sources, hop, inst) * slot_count, slot_count)
            at = pl.ds(pl.multiple_of((tp ^ j) * slice_len, slice_len), slice_len)
            act(pltpu.make_async_copy(part_refs[n], kv_ref.at[slots, :, at], part_sems.at[n]))

    def pages(act, fill):
        place_pages(
            act, fill, spans_ref, owner_ref, place_ref, hop_refs, stage_ref, page_sems,
            hops=hops, sources=sources, slot_count=slot_count,
        )

    @pl.when(step == 0)
    def _():
        part_copies(lambda copy: copy.start())

        def put(g, unused):
            place_ref[plan_ref[g]] = g
            return unused

        lax.fori_loop(0, span_total, put, 0)
        if last_call:
            pages(lambda copy: copy.start(), True)
        part_copies(lambda copy: copy.wait())

    if last_call:
        @pl.when(step == slot_count // 2)
        def _():
            pages(lambda copy: copy.wait(), False)
            pltpu.make_async_copy(stage_ref, cache_ref, cache_sem).start()

    own = inst * slot_count + step
    span = plan_ref[own]
    first = jnp.int32(0)
    end = jnp.int32(0)
    length = jnp.int32(0)
    for p in range(prompt_count):
        start = end
        end = end + spans_ref[p]
        inside = (span >= start) & (span < end)
        first = jnp.where(inside, start, first)
        length = jnp.where(inside, (spans_ref[p] - 1) * span_len + tail_ref[p], length)
    live_rows = length - (span - first) * span_len

    def look(k, count):
        page = place_ref[k]
        source = page // slot_count
        covered = jnp.bool_(False)
        for hop in covers:
            covered = covered | (source_of(sources, hop, inst) == source)
        list_ref[count] = page
        return count + covered.astype(jnp.int32)

    count = lax.fori_loop(first, span, look, jnp.int32(0))

    ones = jnp.ones((span_len, head_dim), jnp.bfloat16)
    row_ids = lax.broadcasted_iota(jnp.int32, (span_len, span_len), 0)
    col_ids = lax.broadcasted_iota(jnp.int32, (span_len, span_len), 1)
    causal = row_ids >= col_ids
    lane_ids = lax.broadcasted_iota(jnp.int32, (span_len, head_dim), 1)
    def lanes_of(head):
        return slice(head * head_dim, (head + 1) * head_dim)

    def rows_of(h):
        return slice(h * span_len, (h + 1) * span_len)

    single = most <= STEP
    live = lax.broadcasted_iota(jnp.int32, (span_len, head_dim), 0) < live_rows

    def put_out(head, total):
        inverse = pl.reciprocal(total[:, head_dim:], approx=True)
        inverse = inverse * (2.0 - total[:, head_dim:] * inverse)
        mixed = (total[:, :head_dim] * inverse).astype(jnp.bfloat16)
        if last_call:
            mixed = jnp.where(live, mixed, jnp.zeros_like(mixed))
        out_ref[0, :, lanes_of(head)] = mixed

    def put_totals(tops, totals):
        if last_call:
            return
        top, total = tops[0], totals[0]
        for head in range(1, kv_local * per_head):
            top = jnp.where(lane_ids == head, tops[head], top)
            total = jnp.where(lane_ids == head, totals[head], total)
        next_total_ref[0] = top + jnp.log(total) * LOG2E

    def attend(pages, since):
        wide = len(pages) * span_len

        def cols_of(n):
            return slice(n * span_len, (n + 1) * span_len)

        for g in range(kv_local):
            q = jnp.concatenate(
                [q_ref[0, :, lanes_of(g * per_head + h)] for h in range(per_head)], axis=0
            )
            for n in range(0, len(pages), 2):
                some = pages[n:n + 2]
                keys = jnp.concatenate([kv_ref[p, g, :, :head_dim] for p in some], axis=0)
                s = lax.dot_general(
                    q, keys, (((1,), (1,)), ((), ())), preferred_element_type=jnp.float32
                )
                for m in range(len(some)):
                    if since == "start" and n + m == len(pages) - 1:
                        for h in range(per_head):
                            s_ref[g, rows_of(h), cols_of(n + m)] = jnp.where(
                                causal, s[rows_of(h), cols_of(m)], -1e30
                            )
                    else:
                        s_ref[g, :, cols_of(n + m)] = s[:, cols_of(m)]
        def weigh(exact):
            tops, totals = [], []
            for g in range(kv_local):
                rescales = []
                for h in range(per_head):
                    head = g * per_head + h
                    top = s_ref[g, rows_of(h), cols_of(0)]
                    for n in range(1, len(pages)):
                        top = jnp.maximum(top, s_ref[g, rows_of(h), cols_of(n)])
                    if not exact:
                        top = jnp.max(top, axis=0, keepdims=True)
                    top = jnp.broadcast_to(
                        jnp.max(top, axis=1, keepdims=True) * scale, (span_len, head_dim)
                    )
                    if since != "start":
                        if since == "given":
                            old = jnp.broadcast_to(
                                total_ref[0, :, head:head + 1], (span_len, head_dim)
                            )
                        else:
                            old = max_ref[head]
                        top = jnp.maximum(old, top)
                        rescales.append(jnp.exp2(old - top))
                    if single:
                        tops.append(top)
                    else:
                        max_ref[head] = top
                    for n in range(len(pages)):
                        p_ref[g, rows_of(h), cols_of(n)] = jnp.exp2(
                            s_ref[g, rows_of(h), cols_of(n)] * scale - top
                        ).astype(jnp.bfloat16)
                values = jnp.concatenate(
                    [
                        jnp.concatenate([kv_ref[page, g, :, head_dim:], ones], axis=1)
                        for page in pages
                    ],
                    axis=0,
                )
                mixed = jnp.dot(p_ref[g, :, :wide], values, preferred_element_type=jnp.float32)
                for h in range(per_head):
                    head = g * per_head + h
                    new = mixed[rows_of(h)]
                    if since == "given":
                        given = mixed_ref[0, :, lanes_of(head)].astype(jnp.float32)
                        new = new + jnp.concatenate([given * rescales[h], rescales[h]], axis=1)
                    elif since == "here":
                        new = new + acc_ref[head] * jnp.concatenate([rescales[h]] * 2, axis=1)
                    if single:
                        put_out(head, new)
                    else:
                        acc_ref[head] = new
                    totals.append(new[:, head_dim:])
            if single:
                put_totals(tops, totals)
            return functools.reduce(jnp.minimum, totals)

        if not single:
            weigh(True)
            return
        least = jnp.min(weigh(False))

        @pl.when(jnp.logical_not(least > SMALL))
        def _():
            weigh(True)

    def rest(begin):
        if single:
            return

        def block(j, unused):
            at = begin + STEP * j
            attend([list_ref[at + n] for n in range(STEP)], "here")
            return unused

        lax.fori_loop(0, (count - begin) // STEP, block, 0)

    def finish():
        if single:
            return
        heads = range(kv_local * per_head)
        for head in heads:
            put_out(head, acc_ref[head])
        put_totals([max_ref[head] for head in heads], [acc_ref[head, :, head_dim:] for head in heads])

    if first_call:
        over = lax.rem(count, STEP)
        for n in range(STEP):
            @pl.when(over == n)
            def _():
                attend([list_ref[m] for m in range(n)] + [own], "start")

        rest(over)
        finish()
    else:
        over = lax.rem(count + STEP - 1, STEP) + 1

        @pl.when(count == 0)
        def _():
            if last_call:
                for head in range(kv_local * per_head):
                    given = mixed_ref[0, :, lanes_of(head)]
                    out_ref[0, :, lanes_of(head)] = jnp.where(live, given, jnp.zeros_like(given))
            else:
                out_ref[...] = mixed_ref[...]
                next_total_ref[...] = total_ref[...]

        @pl.when(count > 0)
        def _():
            for n in range(1, STEP + 1):
                @pl.when(over == n)
                def _():
                    attend([list_ref[m] for m in range(n)], "given")

            rest(over)
            finish()

    if last_call:
        @pl.when(step == slot_count - 1)
        def _():
            pltpu.make_async_copy(stage_ref, cache_ref, cache_sem).wait()


def after(values, earlier):
    return lax.optimization_barrier((list(values), list(earlier)))[0]


def move_pages(kv_new, kv_local, attend):
    inst_size = lax.axis_size("inst")
    tp_size = lax.axis_size("tp")
    inst = lax.axis_index("inst")
    tp = lax.axis_index("tp")
    slot_count, kv_heads = kv_new.shape[:2]
    sources = [list(range(inst_size))]
    hops = [(0, kv_new)]
    parts = []

    def along(x, pairs):
        return lax.ppermute(x, "inst", pairs)

    def exchange(hop, x):
        found = []
        for j in range(tp_size):
            head = ((tp ^ j) * kv_heads) // tp_size
            sent = lax.dynamic_slice_in_dim(x, head, kv_local, 1)
            if j:
                sent = lax.ppermute(sent, "tp", [(t, t ^ j) for t in range(tp_size)])
            found.append(((hop, j), sent))
        parts.extend(found)
        return [x for _, x in found]

    if inst_size != 4:
        exchange(0, kv_new)
        for s in range(1, inst_size):
            sources.append([(i - s) % inst_size for i in range(inst_size)])
            pairs = [(i, (i + s) % inst_size) for i in range(inst_size)]
            hops.append((s, along(kv_new, pairs)))
            exchange(s, hops[-1][1])
        return [], (list(range(inst_size)), parts, sources), hops

    sources += [[1, 0, 3, 2], [-1, 2, 1, -1], [-1, 3, 0, -1], [2, -1, -1, 1], [3, -1, -1, 0]]
    sources += [[2, 2, 1, 1], [3, 3, 0, 0]]
    middle = (inst == 1) | (inst == 2)
    outer = along(kv_new, [(0, 1), (1, 0), (2, 3), (3, 2)])
    inner = along(kv_new, [(1, 2), (2, 1)])
    waiting = exchange(0, kv_new)
    outer_on, inner_on = after([outer, inner], waiting)
    crossed = along(outer_on, [(1, 2), (2, 1)])
    inner_ends = along(inner_on, [(1, 0), (2, 3)])
    own_parts = parts[:]
    waiting = exchange(1, outer_on)
    first_parts = parts[len(own_parts):]
    state = attend([0], own_parts, sources, later=waiting[:1])
    crossed_ends = along(crossed, [(1, 0), (2, 3)])
    second = exchange(6, jnp.where(middle, inner, inner_ends))
    second_parts = parts[2 * tp_size:]
    state = attend([1], first_parts, sources, state=state, later=[second[0], crossed])
    third = exchange(7, after([jnp.where(middle, crossed, crossed_ends)], second)[0])
    third_parts = parts[3 * tp_size:]
    state = attend([6], second_parts, sources, state=state)
    hops += enumerate((outer, inner, crossed, inner_ends, crossed_ends), 1)
    return state, ([7], third_parts, sources), hops


def body(queries, kv_new, prompt_spans, prompt_tail, span_plan, decode_owner):
    tp_size = lax.axis_size("tp")
    inst_size = lax.axis_size("inst")
    slot_count, span_len, row_width = queries.shape
    kv_heads, slice_len, width = kv_new.shape[1:]
    head_dim = width // 2
    local_heads = row_width // head_dim
    kv_local = max(1, kv_heads // tp_size)
    per_head = local_heads // kv_local
    span_total = slot_count * inst_size
    longest = span_total // 2
    anywhere = pl.BlockSpec(memory_space=pl.ANY)
    by_slot = pl.BlockSpec((1, span_len, row_width), lambda i, *_: (i, 0, 0))
    rows = per_head * span_len
    total_spec = pl.BlockSpec((1, span_len, head_dim), lambda i, *_: (i, 0, 0))
    state_specs = [by_slot, total_spec]
    work = slot_count * 4 * local_heads * span_len * span_len

    page_shape = (kv_heads, slice_len, width)

    def attend(covers, parts, sources, state=(), later=(), hops=None):
        first_call, last_call = not state, hops is not None
        hops = hops or []
        kernel = functools.partial(
            attend_kernel,
            covers=covers,
            sources=sources,
            hops=[name for name, _ in hops],
            parts=[name for name, _ in parts],
            later=len(later),
            first_call=first_call,
            last_call=last_call,
            inst_size=inst_size,
            tp_size=tp_size,
            kv_local=kv_local,
            per_head=per_head,
            head_dim=head_dim,
            span_len=span_len,
            slot_count=slot_count,
            longest=longest,
        )
        single = min(longest, len(covers) * slot_count) <= STEP
        kept = (1, 8) if single else (local_heads, span_len)
        scratch = [
            pltpu.SMEM((span_total,), jnp.int32),
            pltpu.SMEM((span_total,), jnp.int32),
            pltpu.VMEM((span_total, kv_local, span_len, width), jnp.bfloat16),
            pltpu.VMEM((kv_local, rows, STEP * span_len), jnp.float32),
            pltpu.VMEM((kv_local, rows, STEP * span_len), jnp.bfloat16),
            pltpu.VMEM(kept + (2 * head_dim,), jnp.float32),
            pltpu.VMEM(kept + (head_dim,), jnp.float32),
            pltpu.SemaphoreType.DMA((len(parts),)),
        ]
        if last_call:
            scratch += [
                pltpu.VMEM((longest,) + page_shape, jnp.bfloat16),
                pltpu.SemaphoreType.DMA((longest,)),
                pltpu.SemaphoreType.DMA,
            ]
            out_specs = [by_slot, anywhere]
            second = jax.ShapeDtypeStruct((longest,) + page_shape, jnp.bfloat16)
        else:
            out_specs = state_specs
            second = jax.ShapeDtypeStruct((slot_count, span_len, head_dim), jnp.float32)
        out_shape = [jax.ShapeDtypeStruct(queries.shape, jnp.bfloat16), second]
        return pl.pallas_call(
            kernel,
            grid_spec=pltpu.PrefetchScalarGridSpec(
                num_scalar_prefetch=4,
                grid=(slot_count,),
                in_specs=[by_slot] + (state_specs if state else [])
                + [anywhere] * (len(parts) + len(later) + len(hops)),
                out_specs=out_specs,
                scratch_shapes=scratch,
            ),
            out_shape=out_shape,
            cost_estimate=pl.CostEstimate(
                flops=4 * work * head_dim, bytes_accessed=8 << 20, transcendentals=work
            ),
            compiler_params=pltpu.CompilerParams(vmem_limit_bytes=VMEM_BYTES),
        )(
            prompt_spans, prompt_tail, span_plan, decode_owner, queries,
            *state, *[x for _, x in parts], *later, *[x for _, x in hops],
        )

    state, left, hops = move_pages(kv_new, kv_local, attend)
    return tuple(attend(*left, state, hops=hops))


def solution(mesh):
    placed = (
        P(("groups", "inst"), None, "tp"),
        P(("groups", "inst"), None, "tp", None),
        P("groups"),
        P("groups"),
        P("groups"),
        P("groups"),
    )
    return jax.shard_map(
        body,
        mesh=mesh,
        in_specs=placed,
        out_specs=(P(("groups", "inst"), None, "tp"), P(("groups", "inst"), None, "tp", None)),
        check_vma=False,
    )
```

```python
import functools
import math

import jax
import jax.numpy as jnp
from jax import lax
from jax.experimental import pallas as pl
from jax.experimental.pallas import tpu as pltpu
from jax.sharding import PartitionSpec as P

HEADS = 64
KVH = 8
LOG2E = 1.4426950408889634
STEP = 4
VMEM_BYTES = 18 << 20


def source_of(sources, hop, inst):
    found = jnp.int32(sources[hop][0])
    for i in range(1, len(sources[hop])):
        found = jnp.where(inst == i, sources[hop][i], found)
    return found


def place_kernel(
    spans_ref, owner_ref, plan_ref, *refs, hops, sources, slot_count, longest,
):
    hop_refs = refs[:len(hops)]
    cache_ref, stage_ref, sems, out_sem = refs[len(hops):]
    inst = lax.axis_index("inst")
    first, count, start = jnp.int32(0), jnp.int32(0), jnp.int32(0)
    for p in range(spans_ref.shape[0]):
        hit = owner_ref[p] == inst
        first = jnp.where(hit, start, first)
        count = jnp.where(hit, spans_ref[p], count)
        start = start + spans_ref[p]

    for n, hop in enumerate(hops):
        source = source_of(sources, hop, inst)

        @pl.when(source >= 0)
        def _():
            for slot in range(slot_count):
                row = plan_ref[source * slot_count + slot] - first

                @pl.when((row >= 0) & (row < count))
                def _():
                    pltpu.make_async_copy(
                        hop_refs[n].at[slot], stage_ref.at[row], sems.at[row]
                    ).start()

    def clear(row, unused):
        stage_ref[row] = jnp.zeros(stage_ref.shape[1:], stage_ref.dtype)
        return unused

    def arrive(row, unused):
        pltpu.make_async_copy(hop_refs[0].at[0], stage_ref.at[row], sems.at[row]).wait()
        return unused

    lax.fori_loop(count, longest, clear, 0)
    lax.fori_loop(0, count, arrive, 0)
    out = pltpu.make_async_copy(stage_ref, cache_ref, out_sem)
    out.start()
    out.wait()


def attend_kernel(
    spans_ref, tail_ref, plan_ref, *refs,
    covers, sources, parts, later, first_call, last_call,
    inst_size, tp_size, kv_local, per_head, head_dim, span_len, slot_count, longest,
):
    refs = list(refs)

    def take(count):
        taken = refs[:count]
        del refs[:count]
        return taken

    (q_ref,) = take(1)
    mixed_ref, total_ref = (None, None) if first_call else take(2)
    part_refs = take(len(parts))
    take(later)
    (out_ref,) = take(1)
    if not last_call:
        (next_total_ref,) = take(1)
    place_ref, list_ref, kv_ref, s_ref, p_ref, acc_ref, max_ref, part_sems = take(8)
    step = pl.program_id(0)
    span_total = slot_count * inst_size
    prompt_count = spans_ref.shape[0]
    inst = lax.axis_index("inst")
    tp = lax.axis_index("tp")
    slice_len = span_len // tp_size
    most = min(longest, len(covers) * slot_count)
    scale = LOG2E / math.sqrt(head_dim)

    def part_copies(act):
        for n, (hop, j) in enumerate(parts):
            slots = pl.ds(source_of(sources, hop, inst) * slot_count, slot_count)
            at = pl.ds(pl.multiple_of((tp ^ j) * slice_len, slice_len), slice_len)
            act(pltpu.make_async_copy(part_refs[n], kv_ref.at[slots, :, at], part_sems.at[n]))

    @pl.when(step == 0)
    def _():
        part_copies(lambda copy: copy.start())

        def put(g, unused):
            place_ref[plan_ref[g]] = g
            return unused

        lax.fori_loop(0, span_total, put, 0)
        part_copies(lambda copy: copy.wait())

    own = inst * slot_count + step
    span = plan_ref[own]
    first = jnp.int32(0)
    end = jnp.int32(0)
    length = jnp.int32(0)
    for p in range(prompt_count):
        start = end
        end = end + spans_ref[p]
        inside = (span >= start) & (span < end)
        first = jnp.where(inside, start, first)
        length = jnp.where(inside, (spans_ref[p] - 1) * span_len + tail_ref[p], length)
    live_rows = length - (span - first) * span_len

    def look(k, count):
        page = place_ref[k]
        source = page // slot_count
        covered = jnp.bool_(False)
        for hop in covers:
            covered = covered | (source_of(sources, hop, inst) == source)
        list_ref[count] = page
        return count + covered.astype(jnp.int32)

    count = lax.fori_loop(first, span, look, jnp.int32(0))

    ones = jnp.ones((span_len, head_dim), jnp.bfloat16)
    row_ids = lax.broadcasted_iota(jnp.int32, (span_len, span_len), 0)
    col_ids = lax.broadcasted_iota(jnp.int32, (span_len, span_len), 1)
    causal = row_ids >= col_ids
    lane_ids = lax.broadcasted_iota(jnp.int32, (span_len, head_dim), 1)
    def lanes_of(head):
        return slice(head * head_dim, (head + 1) * head_dim)

    def rows_of(h):
        return slice(h * span_len, (h + 1) * span_len)

    single = most <= STEP
    live = lax.broadcasted_iota(jnp.int32, (span_len, head_dim), 0) < live_rows

    def put_out(head, total):
        inverse = pl.reciprocal(total[:, head_dim:], approx=True)
        inverse = inverse * (2.0 - total[:, head_dim:] * inverse)
        mixed = (total[:, :head_dim] * inverse).astype(jnp.bfloat16)
        if last_call:
            mixed = jnp.where(live, mixed, jnp.zeros_like(mixed))
        out_ref[0, :, lanes_of(head)] = mixed

    def put_totals(tops, totals):
        if last_call:
            return
        top, total = tops[0], totals[0]
        for head in range(1, kv_local * per_head):
            top = jnp.where(lane_ids == head, tops[head], top)
            total = jnp.where(lane_ids == head, totals[head], total)
        next_total_ref[0] = top + jnp.log(total) * LOG2E

    def attend(pages, since):
        wide = len(pages) * span_len

        def cols_of(n):
            return slice(n * span_len, (n + 1) * span_len)

        for g in range(kv_local):
            q = jnp.concatenate(
                [q_ref[0, :, lanes_of(g * per_head + h)] for h in range(per_head)], axis=0
            )
            for n in range(0, len(pages), 2):
                some = pages[n:n + 2]
                keys = jnp.concatenate([kv_ref[p, g, :, :head_dim] for p in some], axis=0)
                s = lax.dot_general(
                    q, keys, (((1,), (1,)), ((), ())), preferred_element_type=jnp.float32
                )
                for m in range(len(some)):
                    if since == "start" and n + m == len(pages) - 1:
                        for h in range(per_head):
                            s_ref[g, rows_of(h), cols_of(n + m)] = jnp.where(
                                causal, s[rows_of(h), cols_of(m)], -1e30
                            )
                    else:
                        s_ref[g, :, cols_of(n + m)] = s[:, cols_of(m)]
        tops, totals, rescales, sums = [], [], [], []
        for g in range(kv_local):
            for h in range(per_head):
                head = g * per_head + h
                top = s_ref[g, rows_of(h), cols_of(0)]
                for n in range(1, len(pages)):
                    top = jnp.maximum(top, s_ref[g, rows_of(h), cols_of(n)])
                top = jnp.broadcast_to(
                    jnp.max(top, axis=1, keepdims=True) * scale, (span_len, head_dim)
                )
                if since != "start":
                    if since == "given":
                        old = jnp.broadcast_to(
                            total_ref[0, :, head:head + 1], (span_len, head_dim)
                        )
                    else:
                        old = max_ref[head]
                    top = jnp.maximum(old, top)
                    rescales.append(jnp.exp2(old - top))
                if single:
                    tops.append(top)
                else:
                    max_ref[head] = top
                for n in range(len(pages)):
                    p_ref[g, rows_of(h), cols_of(n)] = jnp.exp2(
                        s_ref[g, rows_of(h), cols_of(n)] * scale - top
                    ).astype(jnp.bfloat16)
            values = jnp.concatenate(
                [
                    jnp.concatenate([kv_ref[page, g, :, head_dim:], ones], axis=1)
                    for page in pages
                ],
                axis=0,
            )
            sums.append(
                jnp.dot(p_ref[g, :, :wide], values, preferred_element_type=jnp.float32)
            )
        for g in range(kv_local):
            for h in range(per_head):
                head = g * per_head + h
                new = sums[g][rows_of(h)]
                if since == "given":
                    given = mixed_ref[0, :, lanes_of(head)].astype(jnp.float32)
                    new = new + jnp.concatenate([given * rescales[head], rescales[head]], axis=1)
                elif since == "here":
                    new = new + acc_ref[head] * jnp.concatenate([rescales[head]] * 2, axis=1)
                if single:
                    put_out(head, new)
                    totals.append(new[:, head_dim:])
                else:
                    acc_ref[head] = new
        if single:
            put_totals(tops, totals)

    def rest(begin):
        if single:
            return

        def block(j, unused):
            at = begin + STEP * j
            attend([list_ref[at + n] for n in range(STEP)], "here")
            return unused

        lax.fori_loop(0, (count - begin) // STEP, block, 0)

    def finish():
        if single:
            return
        heads = range(kv_local * per_head)
        for head in heads:
            put_out(head, acc_ref[head])
        put_totals([max_ref[head] for head in heads], [acc_ref[head, :, head_dim:] for head in heads])

    if first_call:
        over = lax.rem(count, STEP)
        for n in range(STEP):
            @pl.when(over == n)
            def _():
                attend([list_ref[m] for m in range(n)] + [own], "start")

        rest(over)
        finish()
    else:
        over = lax.rem(count + STEP - 1, STEP) + 1

        @pl.when(count == 0)
        def _():
            if last_call:
                for head in range(kv_local * per_head):
                    given = mixed_ref[0, :, lanes_of(head)]
                    out_ref[0, :, lanes_of(head)] = jnp.where(live, given, jnp.zeros_like(given))
            else:
                out_ref[...] = mixed_ref[...]
                next_total_ref[...] = total_ref[...]

        @pl.when(count > 0)
        def _():
            for n in range(1, STEP + 1):
                @pl.when(over == n)
                def _():
                    attend([list_ref[m] for m in range(n)], "given")

            rest(over)
            finish()

def after(values, earlier):
    return lax.optimization_barrier((list(values), list(earlier)))[0]


def move_pages(kv_new, kv_local, attend):
    inst_size = lax.axis_size("inst")
    tp_size = lax.axis_size("tp")
    inst = lax.axis_index("inst")
    tp = lax.axis_index("tp")
    slot_count, kv_heads = kv_new.shape[:2]
    sources = [list(range(inst_size))]
    hops = [(0, kv_new)]
    parts = []

    def along(x, pairs):
        return lax.ppermute(x, "inst", pairs)

    def exchange(hop, x):
        found = []
        for j in range(tp_size):
            head = ((tp ^ j) * kv_heads) // tp_size
            sent = lax.dynamic_slice_in_dim(x, head, kv_local, 1)
            if j:
                sent = lax.ppermute(sent, "tp", [(t, t ^ j) for t in range(tp_size)])
            found.append(((hop, j), sent))
        parts.extend(found)
        return [x for _, x in found]

    if inst_size != 4:
        exchange(0, kv_new)
        for s in range(1, inst_size):
            sources.append([(i - s) % inst_size for i in range(inst_size)])
            pairs = [(i, (i + s) % inst_size) for i in range(inst_size)]
            hops.append((s, along(kv_new, pairs)))
            exchange(s, hops[-1][1])
        return [], (list(range(inst_size)), parts, sources), hops

    sources += [[1, 0, 3, 2], [-1, 2, 1, -1], [-1, 3, 0, -1], [2, -1, -1, 1], [3, -1, -1, 0]]
    sources += [[2, 2, 1, 1], [3, 3, 0, 0]]
    middle = (inst == 1) | (inst == 2)
    outer = along(kv_new, [(0, 1), (1, 0), (2, 3), (3, 2)])
    inner = along(kv_new, [(1, 2), (2, 1)])
    waiting = exchange(0, kv_new)
    outer_on, inner_on = after([outer, inner], waiting)
    crossed = along(outer_on, [(1, 2), (2, 1)])
    inner_ends = along(inner_on, [(1, 0), (2, 3)])
    own_parts = parts[:]
    waiting = exchange(1, outer_on)
    first_parts = parts[len(own_parts):]
    state = attend([0], own_parts, sources, later=waiting[:1])
    crossed_ends = along(crossed, [(1, 0), (2, 3)])
    second = exchange(6, jnp.where(middle, inner, inner_ends))
    second_parts = parts[2 * tp_size:]
    state = attend([1], first_parts, sources, state=state, later=[second[0], crossed])
    third = exchange(7, after([jnp.where(middle, crossed, crossed_ends)], second)[0])
    third_parts = parts[3 * tp_size:]
    state = attend([6], second_parts, sources, state=state)
    hops += enumerate((outer, inner, crossed, inner_ends, crossed_ends), 1)
    return state, ([7], third_parts, sources), hops


def body(queries, kv_new, prompt_spans, prompt_tail, span_plan, decode_owner):
    tp_size = lax.axis_size("tp")
    inst_size = lax.axis_size("inst")
    slot_count, span_len, row_width = queries.shape
    kv_heads, slice_len, width = kv_new.shape[1:]
    head_dim = width // 2
    local_heads = row_width // head_dim
    kv_local = max(1, kv_heads // tp_size)
    per_head = local_heads // kv_local
    span_total = slot_count * inst_size
    longest = span_total // 2
    anywhere = pl.BlockSpec(memory_space=pl.ANY)
    by_slot = pl.BlockSpec((1, span_len, row_width), lambda i, *_: (i, 0, 0))
    rows = per_head * span_len
    total_spec = pl.BlockSpec((1, span_len, head_dim), lambda i, *_: (i, 0, 0))
    state_specs = [by_slot, total_spec]
    work = slot_count * 4 * local_heads * span_len * span_len

    def attend(covers, parts, sources, state=(), later=(), last_call=False):
        first_call = not state
        kernel = functools.partial(
            attend_kernel,
            covers=covers,
            sources=sources,
            parts=[name for name, _ in parts],
            later=len(later),
            first_call=first_call,
            last_call=last_call,
            inst_size=inst_size,
            tp_size=tp_size,
            kv_local=kv_local,
            per_head=per_head,
            head_dim=head_dim,
            span_len=span_len,
            slot_count=slot_count,
            longest=longest,
        )
        single = min(longest, len(covers) * slot_count) <= STEP
        kept = (1, 8) if single else (local_heads, span_len)
        scratch = [
            pltpu.SMEM((span_total,), jnp.int32),
            pltpu.SMEM((span_total,), jnp.int32),
            pltpu.VMEM((span_total, kv_local, span_len, width), jnp.bfloat16),
            pltpu.VMEM((kv_local, rows, STEP * span_len), jnp.float32),
            pltpu.VMEM((kv_local, rows, STEP * span_len), jnp.bfloat16),
            pltpu.VMEM(kept + (2 * head_dim,), jnp.float32),
            pltpu.VMEM(kept + (head_dim,), jnp.float32),
            pltpu.SemaphoreType.DMA((len(parts),)),
        ]
        out_specs = [by_slot] if last_call else state_specs
        out_shape = [
            jax.ShapeDtypeStruct(queries.shape, jnp.bfloat16),
            jax.ShapeDtypeStruct((slot_count, span_len, head_dim), jnp.float32),
        ][:len(out_specs)]
        return pl.pallas_call(
            kernel,
            grid_spec=pltpu.PrefetchScalarGridSpec(
                num_scalar_prefetch=3,
                grid=(slot_count,),
                in_specs=[by_slot] + (state_specs if state else [])
                + [anywhere] * (len(parts) + len(later)),
                out_specs=out_specs,
                scratch_shapes=scratch,
            ),
            out_shape=out_shape,
            cost_estimate=pl.CostEstimate(
                flops=4 * work * head_dim, bytes_accessed=8 << 20, transcendentals=work
            ),
            compiler_params=pltpu.CompilerParams(vmem_limit_bytes=VMEM_BYTES),
        )(
            prompt_spans, prompt_tail, span_plan, queries,
            *state, *[x for _, x in parts], *later,
        )

    state, left, hops = move_pages(kv_new, kv_local, attend)
    page_shape = (kv_heads, slice_len, width)
    owner_cache = pl.pallas_call(
        functools.partial(
            place_kernel,
            hops=[name for name, _ in hops],
            sources=left[2],
            slot_count=slot_count,
            longest=longest,
        ),
        grid_spec=pltpu.PrefetchScalarGridSpec(
            num_scalar_prefetch=3,
            grid=(1,),
            in_specs=[anywhere] * len(hops),
            out_specs=anywhere,
            scratch_shapes=[
                pltpu.VMEM((longest,) + page_shape, jnp.bfloat16),
                pltpu.SemaphoreType.DMA((longest,)),
                pltpu.SemaphoreType.DMA,
            ],
        ),
        out_shape=jax.ShapeDtypeStruct((longest,) + page_shape, jnp.bfloat16),
        cost_estimate=pl.CostEstimate(flops=0, bytes_accessed=8 << 20, transcendentals=0),
        compiler_params=pltpu.CompilerParams(vmem_limit_bytes=4 << 20),
    )(prompt_spans, decode_owner, span_plan, *[x for _, x in hops])
    (attended,) = attend(*left, state, last_call=True)
    return attended, owner_cache


def solution(mesh):
    placed = (
        P(("groups", "inst"), None, "tp"),
        P(("groups", "inst"), None, "tp", None),
        P("groups"),
        P("groups"),
        P("groups"),
        P("groups"),
    )
    return jax.shard_map(
        body,
        mesh=mesh,
        in_specs=placed,
        out_specs=(P(("groups", "inst"), None, "tp"), P(("groups", "inst"), None, "tp", None)),
        check_vma=False,
    )
```

```python
import functools
import math

import jax
import jax.numpy as jnp
from jax import lax
from jax.experimental import pallas as pl
from jax.experimental.pallas import tpu as pltpu
from jax.sharding import PartitionSpec as P

HEADS = 64
KVH = 8
LOG2E = 1.4426950408889634
STEP = 8
VMEM_BYTES = 20 << 20


def source_of(sources, hop, inst):
    found = jnp.int32(sources[hop][0])
    for i in range(1, len(sources[hop])):
        found = jnp.where(inst == i, sources[hop][i], found)
    return found


def place_kernel(
    spans_ref, owner_ref, plan_ref, *refs, hops, sources, slot_count, longest,
):
    hop_refs = refs[:len(hops)]
    cache_ref, stage_ref, sems, out_sem = refs[len(hops):]
    inst = lax.axis_index("inst")
    first, count, start = jnp.int32(0), jnp.int32(0), jnp.int32(0)
    for p in range(spans_ref.shape[0]):
        hit = owner_ref[p] == inst
        first = jnp.where(hit, start, first)
        count = jnp.where(hit, spans_ref[p], count)
        start = start + spans_ref[p]

    for n, (hop, first_slot) in enumerate(hops):
        source = source_of(sources, hop, inst)

        @pl.when(source >= 0)
        def _():
            for slot in range(hop_refs[n].shape[0]):
                row = plan_ref[source * slot_count + first_slot + slot] - first

                @pl.when((row >= 0) & (row < count))
                def _():
                    pltpu.make_async_copy(
                        hop_refs[n].at[slot], stage_ref.at[row], sems.at[row]
                    ).start()

    def clear(row, unused):
        stage_ref[row] = jnp.zeros(stage_ref.shape[1:], stage_ref.dtype)
        return unused

    def arrive(row, unused):
        pltpu.make_async_copy(hop_refs[0].at[0], stage_ref.at[row], sems.at[row]).wait()
        return unused

    lax.fori_loop(count, longest, clear, 0)
    lax.fori_loop(0, count, arrive, 0)
    out = pltpu.make_async_copy(stage_ref, cache_ref, out_sem)
    out.start()
    out.wait()


def attend_kernel(
    spans_ref, tail_ref, plan_ref, *refs,
    covers, sources, parts, later, first_call, last_call,
    inst_size, tp_size, kv_local, per_head, head_dim, span_len, slot_count, longest,
):
    refs = list(refs)

    def take(count):
        taken = refs[:count]
        del refs[:count]
        return taken

    (q_ref,) = take(1)
    mixed_ref, total_ref = (None, None) if first_call else take(2)
    part_refs = take(len(parts))
    take(later)
    (out_ref,) = take(1)
    if not last_call:
        (next_total_ref,) = take(1)
    place_ref, list_ref, kv_ref, s_ref, p_ref, acc_ref, max_ref, part_sems = take(8)
    step = pl.program_id(0)
    span_total = slot_count * inst_size
    prompt_count = spans_ref.shape[0]
    inst = lax.axis_index("inst")
    tp = lax.axis_index("tp")
    slice_len = span_len // tp_size
    most = min(longest, sum(size for _, _, size in covers))
    scale = LOG2E / math.sqrt(head_dim)

    def part_copies(act):
        for n, (hop, j, first_slot) in enumerate(parts):
            slots = pl.ds(
                source_of(sources, hop, inst) * slot_count + first_slot, part_refs[n].shape[0]
            )
            at = pl.ds(pl.multiple_of((tp ^ j) * slice_len, slice_len), slice_len)
            act(pltpu.make_async_copy(part_refs[n], kv_ref.at[slots, :, at], part_sems.at[n]))

    @pl.when(step == 0)
    def _():
        part_copies(lambda copy: copy.start())

        def put(g, unused):
            place_ref[plan_ref[g]] = g
            return unused

        lax.fori_loop(0, span_total, put, 0)
        part_copies(lambda copy: copy.wait())

    own = inst * slot_count + step
    span = plan_ref[own]
    first = jnp.int32(0)
    end = jnp.int32(0)
    length = jnp.int32(0)
    for p in range(prompt_count):
        start = end
        end = end + spans_ref[p]
        inside = (span >= start) & (span < end)
        first = jnp.where(inside, start, first)
        length = jnp.where(inside, (spans_ref[p] - 1) * span_len + tail_ref[p], length)
    live_rows = length - (span - first) * span_len

    def look(k, count):
        page = place_ref[k]
        covered = jnp.bool_(False)
        for hop, first_slot, size in covers:
            slot = page - source_of(sources, hop, inst) * slot_count
            covered = covered | ((slot >= first_slot) & (slot < first_slot + size))
        list_ref[count] = page
        return count + covered.astype(jnp.int32)

    count = lax.fori_loop(first, span, look, jnp.int32(0))

    ones = jnp.ones((span_len, head_dim), jnp.bfloat16)
    row_ids = lax.broadcasted_iota(jnp.int32, (span_len, span_len), 0)
    col_ids = lax.broadcasted_iota(jnp.int32, (span_len, span_len), 1)
    causal = row_ids >= col_ids
    lane_ids = lax.broadcasted_iota(jnp.int32, (span_len, head_dim), 1)
    def lanes_of(head):
        return slice(head * head_dim, (head + 1) * head_dim)

    def rows_of(h):
        return slice(h * span_len, (h + 1) * span_len)

    single = most <= STEP
    live = lax.broadcasted_iota(jnp.int32, (span_len, head_dim), 0) < live_rows

    def put_out(head, total):
        inverse = pl.reciprocal(total[:, head_dim:], approx=True)
        inverse = inverse * (2.0 - total[:, head_dim:] * inverse)
        mixed = (total[:, :head_dim] * inverse).astype(jnp.bfloat16)
        if last_call:
            mixed = jnp.where(live, mixed, jnp.zeros_like(mixed))
        out_ref[0, :, lanes_of(head)] = mixed

    def put_totals(tops, totals):
        if last_call:
            return
        top, total = tops[0], totals[0]
        for head in range(1, kv_local * per_head):
            top = jnp.where(lane_ids == head, tops[head], top)
            total = jnp.where(lane_ids == head, totals[head], total)
        next_total_ref[0] = top + jnp.log(total) * LOG2E

    def attend(pages, since):
        wide = len(pages) * span_len

        def cols_of(n):
            return slice(n * span_len, (n + 1) * span_len)

        for g in range(kv_local):
            q = jnp.concatenate(
                [q_ref[0, :, lanes_of(g * per_head + h)] for h in range(per_head)], axis=0
            )
            for n in range(0, len(pages), 2):
                some = pages[n:n + 2]
                keys = jnp.concatenate([kv_ref[p, g, :, :head_dim] for p in some], axis=0)
                s = lax.dot_general(
                    q, keys, (((1,), (1,)), ((), ())), preferred_element_type=jnp.float32
                )
                for m in range(len(some)):
                    if since == "start" and n + m == len(pages) - 1:
                        for h in range(per_head):
                            s_ref[g, rows_of(h), cols_of(n + m)] = jnp.where(
                                causal, s[rows_of(h), cols_of(m)], -1e30
                            )
                    else:
                        s_ref[g, :, cols_of(n + m)] = s[:, cols_of(m)]
        tops, totals, rescales, sums = [], [], [], []
        for g in range(kv_local):
            for h in range(per_head):
                head = g * per_head + h
                top = s_ref[g, rows_of(h), cols_of(0)]
                for n in range(1, len(pages)):
                    top = jnp.maximum(top, s_ref[g, rows_of(h), cols_of(n)])
                top = jnp.broadcast_to(
                    jnp.max(top, axis=1, keepdims=True) * scale, (span_len, head_dim)
                )
                if since != "start":
                    if since == "given":
                        old = jnp.broadcast_to(
                            total_ref[0, :, head:head + 1], (span_len, head_dim)
                        )
                    else:
                        old = max_ref[head]
                    top = jnp.maximum(old, top)
                    rescales.append(jnp.exp2(old - top))
                if single:
                    tops.append(top)
                else:
                    max_ref[head] = top
                for n in range(len(pages)):
                    p_ref[g, rows_of(h), cols_of(n)] = jnp.exp2(
                        s_ref[g, rows_of(h), cols_of(n)] * scale - top
                    ).astype(jnp.bfloat16)
            values = jnp.concatenate(
                [
                    jnp.concatenate([kv_ref[page, g, :, head_dim:], ones], axis=1)
                    for page in pages
                ],
                axis=0,
            )
            sums.append(
                jnp.dot(p_ref[g, :, :wide], values, preferred_element_type=jnp.float32)
            )
        for g in range(kv_local):
            for h in range(per_head):
                head = g * per_head + h
                new = sums[g][rows_of(h)]
                if since == "given":
                    given = mixed_ref[0, :, lanes_of(head)].astype(jnp.float32)
                    new = new + jnp.concatenate([given * rescales[head], rescales[head]], axis=1)
                elif since == "here":
                    new = new + acc_ref[head] * jnp.concatenate([rescales[head]] * 2, axis=1)
                if single:
                    put_out(head, new)
                    totals.append(new[:, head_dim:])
                else:
                    acc_ref[head] = new
        if single:
            put_totals(tops, totals)

    def rest(begin):
        if single:
            return

        def block(j, unused):
            at = begin + STEP * j
            attend([list_ref[at + n] for n in range(STEP)], "here")
            return unused

        lax.fori_loop(0, (count - begin) // STEP, block, 0)

    def finish():
        if single:
            return
        heads = range(kv_local * per_head)
        for head in heads:
            put_out(head, acc_ref[head])
        put_totals([max_ref[head] for head in heads], [acc_ref[head, :, head_dim:] for head in heads])

    if first_call:
        over = lax.rem(count, STEP)
        for n in range(min(STEP, most)):
            @pl.when(over == n)
            def _():
                attend([list_ref[m] for m in range(n)] + [own], "start")

        rest(over)
        finish()
    else:
        over = lax.rem(count + STEP - 1, STEP) + 1

        @pl.when(count == 0)
        def _():
            if last_call:
                for head in range(kv_local * per_head):
                    given = mixed_ref[0, :, lanes_of(head)]
                    out_ref[0, :, lanes_of(head)] = jnp.where(live, given, jnp.zeros_like(given))
            else:
                out_ref[...] = mixed_ref[...]
                next_total_ref[...] = total_ref[...]

        @pl.when(count > 0)
        def _():
            for n in range(1, min(STEP, most) + 1):
                @pl.when(over == n)
                def _():
                    attend([list_ref[m] for m in range(n)], "given")

            rest(over)
            finish()

def after(values, earlier):
    return lax.optimization_barrier((list(values), list(earlier)))[0]


def move_pages(kv_new, kv_local, attend):
    inst_size = lax.axis_size("inst")
    tp_size = lax.axis_size("tp")
    inst = lax.axis_index("inst")
    tp = lax.axis_index("tp")
    slot_count, kv_heads = kv_new.shape[:2]
    sources = [list(range(inst_size))]
    hops = [((0, 0), kv_new)]
    parts = []

    def along(x, pairs):
        return lax.ppermute(x, "inst", pairs)

    def exchange(hop, x, first_slot=0):
        found = []
        for j in range(tp_size):
            head = ((tp ^ j) * kv_heads) // tp_size
            sent = lax.dynamic_slice_in_dim(x, head, kv_local, 1)
            if j:
                sent = lax.ppermute(sent, "tp", [(t, t ^ j) for t in range(tp_size)])
            found.append(((hop, j, first_slot), sent))
        parts.extend(found)
        return [x for _, x in found]

    if inst_size != 4 or slot_count % 2:
        exchange(0, kv_new)
        for s in range(1, inst_size):
            sources.append([(i - s) % inst_size for i in range(inst_size)])
            pairs = [(i, (i + s) % inst_size) for i in range(inst_size)]
            hops.append(((s, 0), along(kv_new, pairs)))
            exchange(s, hops[-1][1])
        return [], ([(n, 0, slot_count) for n in range(inst_size)], parts, sources), hops

    sources += [[1, 0, 3, 2], [-1, 2, 1, -1], [-1, 3, 0, -1], [2, -1, -1, 1], [3, -1, -1, 0]]
    sources += [[2, 2, 1, 1], [3, 3, 0, 0]]
    middle = (inst == 1) | (inst == 2)
    outer = along(kv_new, [(0, 1), (1, 0), (2, 3), (3, 2)])
    inner = along(kv_new, [(1, 2), (2, 1)])
    waiting = exchange(0, kv_new)
    outer_on, inner_on = after([outer, inner], waiting)
    crossed = along(outer_on, [(1, 2), (2, 1)])
    inner_ends = along(inner_on, [(1, 0), (2, 3)])
    own_parts = parts[:]
    waiting = exchange(1, outer_on)
    first_parts = parts[len(own_parts):]
    state = attend([(0, 0, slot_count)], own_parts, sources, later=waiting[:1])
    half = slot_count // 2
    crossed_half = lax.optimization_barrier([crossed[:half], crossed[half:]])
    crossed_ends = [along(x, [(1, 0), (2, 3)]) for x in crossed_half]
    threes = [jnp.where(middle, x, y) for x, y in zip(crossed_half, crossed_ends)]
    second = exchange(6, jnp.where(middle, inner, inner_ends))
    state = attend(
        [(1, 0, slot_count)], first_parts, sources, state=state, later=[second[0], crossed]
    )
    third = exchange(7, after(threes[:1], second)[0])
    state = attend(
        [(6, 0, slot_count), (7, 0, half)], parts[2 * tp_size:], sources, state=state
    )
    before = len(parts)
    exchange(7, after(threes[1:], third)[0], half)
    hops += [((n, 0), x) for n, x in enumerate((outer, inner, crossed, inner_ends), 1)]
    hops += [((5, 0), crossed_ends[0]), ((5, half), crossed_ends[1])]
    return state, ([(7, half, slot_count - half)], parts[before:], sources), hops


def body(queries, kv_new, prompt_spans, prompt_tail, span_plan, decode_owner):
    tp_size = lax.axis_size("tp")
    inst_size = lax.axis_size("inst")
    slot_count, span_len, row_width = queries.shape
    kv_heads, slice_len, width = kv_new.shape[1:]
    head_dim = width // 2
    local_heads = row_width // head_dim
    kv_local = max(1, kv_heads // tp_size)
    per_head = local_heads // kv_local
    span_total = slot_count * inst_size
    longest = span_total // 2
    anywhere = pl.BlockSpec(memory_space=pl.ANY)
    by_slot = pl.BlockSpec((1, span_len, row_width), lambda i, *_: (i, 0, 0))
    rows = per_head * span_len
    total_spec = pl.BlockSpec((1, span_len, head_dim), lambda i, *_: (i, 0, 0))
    state_specs = [by_slot, total_spec]
    work = slot_count * 4 * local_heads * span_len * span_len

    def attend(covers, parts, sources, state=(), later=(), last_call=False):
        first_call = not state
        kernel = functools.partial(
            attend_kernel,
            covers=covers,
            sources=sources,
            parts=[name for name, _ in parts],
            later=len(later),
            first_call=first_call,
            last_call=last_call,
            inst_size=inst_size,
            tp_size=tp_size,
            kv_local=kv_local,
            per_head=per_head,
            head_dim=head_dim,
            span_len=span_len,
            slot_count=slot_count,
            longest=longest,
        )
        most = min(longest, sum(size for _, _, size in covers))
        single = most <= STEP
        wide = min(most, STEP) * span_len
        kept = (1, 8) if single else (local_heads, span_len)
        scratch = [
            pltpu.SMEM((span_total,), jnp.int32),
            pltpu.SMEM((span_total,), jnp.int32),
            pltpu.VMEM((span_total, kv_local, span_len, width), jnp.bfloat16),
            pltpu.VMEM((kv_local, rows, wide), jnp.float32),
            pltpu.VMEM((kv_local, rows, wide), jnp.bfloat16),
            pltpu.VMEM(kept + (2 * head_dim,), jnp.float32),
            pltpu.VMEM(kept + (head_dim,), jnp.float32),
            pltpu.SemaphoreType.DMA((len(parts),)),
        ]
        out_specs = [by_slot] if last_call else state_specs
        out_shape = [
            jax.ShapeDtypeStruct(queries.shape, jnp.bfloat16),
            jax.ShapeDtypeStruct((slot_count, span_len, head_dim), jnp.float32),
        ][:len(out_specs)]
        return pl.pallas_call(
            kernel,
            grid_spec=pltpu.PrefetchScalarGridSpec(
                num_scalar_prefetch=3,
                grid=(slot_count,),
                in_specs=[by_slot] + (state_specs if state else [])
                + [anywhere] * (len(parts) + len(later)),
                out_specs=out_specs,
                scratch_shapes=scratch,
            ),
            out_shape=out_shape,
            cost_estimate=pl.CostEstimate(
                flops=4 * work * head_dim, bytes_accessed=8 << 20, transcendentals=work
            ),
            compiler_params=pltpu.CompilerParams(vmem_limit_bytes=VMEM_BYTES),
        )(
            prompt_spans, prompt_tail, span_plan, queries,
            *state, *[x for _, x in parts], *later,
        )

    state, left, hops = move_pages(kv_new, kv_local, attend)
    page_shape = (kv_heads, slice_len, width)
    owner_cache = pl.pallas_call(
        functools.partial(
            place_kernel,
            hops=[name for name, _ in hops],
            sources=left[2],
            slot_count=slot_count,
            longest=longest,
        ),
        grid_spec=pltpu.PrefetchScalarGridSpec(
            num_scalar_prefetch=3,
            grid=(1,),
            in_specs=[anywhere] * len(hops),
            out_specs=anywhere,
            scratch_shapes=[
                pltpu.VMEM((longest,) + page_shape, jnp.bfloat16),
                pltpu.SemaphoreType.DMA((longest,)),
                pltpu.SemaphoreType.DMA,
            ],
        ),
        out_shape=jax.ShapeDtypeStruct((longest,) + page_shape, jnp.bfloat16),
        cost_estimate=pl.CostEstimate(flops=0, bytes_accessed=8 << 20, transcendentals=0),
        compiler_params=pltpu.CompilerParams(vmem_limit_bytes=4 << 20),
    )(prompt_spans, decode_owner, span_plan, *[x for _, x in hops])
    (attended,) = attend(*left, state, last_call=True)
    return attended, owner_cache


def solution(mesh):
    placed = (
        P(("groups", "inst"), None, "tp"),
        P(("groups", "inst"), None, "tp", None),
        P("groups"),
        P("groups"),
        P("groups"),
        P("groups"),
    )
    return jax.shard_map(
        body,
        mesh=mesh,
        in_specs=placed,
        out_specs=(P(("groups", "inst"), None, "tp"), P(("groups", "inst"), None, "tp", None)),
        check_vma=False,
    )
```
